32 devices in a mesh: wide: 16 (over z, x, core), narrow: 2 (over y).
Axes of the slice: x: 2, y: 2, z: 4, core: 2. Of those that a mesh axis runs over, the one named last changes fastest.
Arguments:
- resid_in: bfloat16 [16384, 767], P(('wide', 'narrow')), may hold values from -6 to 6
- w_qkv: bfloat16 [768, 2304], P(('wide', 'narrow')), may hold values from -0.21875 to 0.21875
- w_out: bfloat16 [768, 768], P(('wide', 'narrow')), may hold values from -1.75 to 1.75
- w_up: bfloat16 [768, 3072], P(('wide', 'narrow')), may hold values from -0.21875 to 0.21875
- b_up: bfloat16 [3072], P(('wide', 'narrow')), may hold values from -3 to 3
- w_down: bfloat16 [3072, 768], P(('wide', 'narrow')), may hold values from -0.109375 to 0.109375
- gain_attn: bfloat16 [768], P(('wide', 'narrow')), may hold values from 0.25 to 1.75
- gain_mlp: bfloat16 [768], P(('wide', 'narrow')), may hold values from 0.25 to 1.75
- cotangent: bfloat16 [16384, 767], P(('wide', 'narrow')), may hold values from -6 to 6
Outputs:
- resid_out: bfloat16 [16384, 767], P(('wide', 'narrow'))
- d_resid: float32 [16384, 767], P(('wide', 'narrow'))
- grad_w_qkv: float32 [768, 2304], P(('wide', 'narrow'))
- grad_w_out: float32 [768, 768], P(('wide', 'narrow'))
- grad_w_up: float32 [768, 3072], P(('wide', 'narrow'))
- grad_b_up: float32 [3072], P(('wide', 'narrow'))
- grad_w_down: float32 [3072, 768], P(('wide', 'narrow'))
- grad_gain_attn: float32 [768], P(('wide', 'narrow'))
- grad_gain_mlp: float32 [768], P(('wide', 'narrow'))
The draws below stay inside these ranges and needn't reach their ends.
All inputs are finite; a program needn't handle non-finite values.
Results may differ from the reference program's by a relative error of at most 0.011.
Values may be sent and summed in bfloat16 or wider, within the bound.
No kernel may reach another device: no remote copies, remote signals or barrier semaphores. Data moves between devices by JAX's collectives and lax.ppermute only.
A program may use at most 192 MiB of HBM per device.

```python
import jax
import jax.numpy as jnp
from jax import lax

D = 768
H = 12
HD = 64
FF = 3072
RES = 767
TOK_MB = 256
TOKENS = 16384


def steps_of(rng, extent, cuts, least, top_value):
    level = 1.0
    for axis_at, parts in cuts:
        steps = jax.random.uniform(jax.random.fold_in(jax.random.fold_in(rng, 6), axis_at), (parts,), jnp.float32, least / len(cuts), top_value / len(cuts))
        level = level * jnp.repeat(jnp.exp(steps), extent[axis_at] // parts).reshape((-1,) + (1,) * (len(extent) - 1 - axis_at))
    return level


def bell_draw(stream_key, extent, width, reach, pieces=(), held_as=jnp.bfloat16):
    entries = jax.random.normal(stream_key, extent, jnp.float32) * width
    if len(pieces) > 0:
        entries = steps_of(stream_key, extent, pieces, -0.22, 0.18) * entries
    return jnp.clip(entries, min=-reach, max=reach).astype(held_as)


def setup_inputs(seed: int = 0) -> dict:
    arg_keys = jax.random.split(jax.random.key(seed), 10)
    return {
        "resid_in": bell_draw(arg_keys[0], (TOKENS, RES), 1.0, 6.0, ((0, 32),)),
        "w_qkv": bell_draw(arg_keys[1], (D, 3 * D), D ** -0.5, 0.21875, ((0, 32),)),
        "w_out": bell_draw(arg_keys[2], (D, D), (D // 64) ** -0.5, 1.75, ((0, 32),)),
        "w_up": bell_draw(arg_keys[3], (D, FF), D ** -0.5, 0.21875, ((0, 32),)),
        "b_up": bell_draw(arg_keys[4], (FF,), 0.5, 3.0, ((0, 32),)),
        "w_down": bell_draw(arg_keys[5], (FF, D), FF ** -0.5, 0.109375, ((0, 32),)),
        "gain_attn": jnp.clip(1.0 + 0.15 * jax.random.normal(arg_keys[6], (D,), jnp.float32), 0.25, 1.75).astype(jnp.bfloat16),
        "gain_mlp": jnp.clip(1.0 + 0.15 * jax.random.normal(arg_keys[7], (D,), jnp.float32), 0.25, 1.75).astype(jnp.bfloat16),
        "cotangent": bell_draw(arg_keys[8], (TOKENS, RES), 1.0, 6.0, ((0, 32),)),
    }


@jax.custom_vjp
def low(v):
    return lax.optimization_barrier(v.astype(jnp.bfloat16)).astype(jnp.float32)

@jax.custom_vjp
def low_back(v):
    return v

def low_keep(v):
    return (low(v), None)

def low_pass(kept, grad):
    return (grad,)

def back_keep(v):
    return (v, None)

def back_low(kept, grad):
    return (low(grad),)
low.defvjp(low_keep, low_pass)
low_back.defvjp(back_keep, back_low)
highest = lax.Precision.HIGHEST

def decompress(compact):
    return jnp.concatenate([compact, -lax.optimization_barrier(jnp.sum(compact, axis=-1, keepdims=True))], axis=-1)

def compress(branch):
    centred = branch - lax.optimization_barrier(jnp.mean(branch, axis=-1, keepdims=True))
    return centred[:, :-1]

def crms_norm(values, gain):
    return values * lax.rsqrt(lax.optimization_barrier(jnp.mean(values * values, axis=-1, keepdims=True)) + 1e-05) * gain

def layer(resid_block, w_qkv, w_out, w_up, b_up, w_down, gain_attn, gain_mlp):
    length = resid_block.shape[0]
    normed = low(crms_norm(decompress(resid_block), gain_attn))
    project = low_back(low(jnp.dot(normed, w_qkv, precision=highest)))
    queries = project[:, :D].reshape(length, H, HD)
    key_heads = project[:, D:2 * D].reshape(length, H, HD)
    val_heads = project[:, 2 * D:].reshape(length, H, HD)
    scores = jnp.einsum('qhd,khd->hqk', queries, key_heads, precision=highest) * HD ** (-0.5)
    scores = low_back(scores)
    positions = jnp.arange(length)
    allowed = positions[:, None] >= positions[None, :]
    attn_probs = low(jax.nn.softmax(jnp.where(allowed[None], scores, -1e+30), axis=-1))
    mixed = jnp.einsum('hqk,khd->qhd', attn_probs, val_heads, precision=highest).reshape(length, D)
    mixed = low_back(low(mixed))
    attn_out = low_back(jnp.dot(mixed, w_out, precision=highest))
    middle = resid_block + compress(attn_out)
    normed_two = low(crms_norm(decompress(middle), gain_mlp))
    hidden = low_back(jnp.dot(normed_two, w_up, precision=highest) + b_up)
    active = low(jax.nn.gelu(hidden))
    mlp_out = low_back(jnp.dot(active, w_down, precision=highest))
    return middle + compress(mlp_out)

def reference(resid_in, w_qkv, w_out, w_up, b_up, w_down, gain_attn, gain_mlp, cotangent):
    weights = tuple((weight.astype(jnp.float32) for weight in (w_qkv, w_out, w_up, b_up, w_down, gain_attn, gain_mlp)))
    buffers = resid_in.shape[0] // TOK_MB
    resid_blocks = resid_in.astype(jnp.float32).reshape(buffers, TOK_MB, RES)
    cot_blocks = cotangent.astype(jnp.float32).reshape(buffers, TOK_MB, RES)

    def buffer_step(totals, inputs):
        resid_block, cot_block = inputs
        result, pullback = jax.vjp(layer, resid_block, *weights)
        gradients = pullback(cot_block)
        new_totals = tuple((total + grad_value for total, grad_value in zip(totals, gradients[1:])))
        return (new_totals, (result.astype(jnp.bfloat16), gradients[0]))
    zeros_init = tuple((jnp.zeros(weight.shape, jnp.float32) for weight in weights))
    totals, (out_blocks, grad_blocks) = lax.scan(buffer_step, zeros_init, (resid_blocks, cot_blocks))
    return (out_blocks.reshape(-1, RES), grad_blocks.reshape(-1, RES), totals[0], totals[1], totals[2], totals[3], totals[4], totals[5], totals[6])
```

```python
import jax
import jax.numpy as jnp
from jax import lax
from jax.sharding import PartitionSpec as P

D = 768
H = 12
HD = 64
TOK_MB = 256


def decompress(compact):
    return jnp.concatenate([compact, -jnp.sum(compact, axis=-1, keepdims=True)], axis=-1)


def compress(branch):
    centred = branch - jnp.mean(branch, axis=-1, keepdims=True)
    return centred[:, :-1]


def compress_back(grad_rows):
    padded = jnp.concatenate([grad_rows, jnp.zeros_like(grad_rows[:, :1])], axis=-1)
    return padded - jnp.mean(padded, axis=-1, keepdims=True)


def crms_input(resid_rows, gain):
    values = decompress(resid_rows)
    return values * lax.rsqrt(jnp.mean(values * values, axis=-1, keepdims=True) + 1e-05) * gain


def head_group(project, offset, group):
    width = 4 * HD
    length = project.shape[0]
    start = offset + group * width
    return project[:, start : start + width].reshape(length, 4, HD)


def masked_scores(queries, key_heads, allowed):
    raw_scores = jnp.einsum(
        "qhd,khd->hqk", queries, key_heads, preferred_element_type=jnp.float32
    ) * HD ** (-0.5)
    return jnp.where(allowed[None], raw_scores, -1e30)


def attention_group(queries, key_heads, val_heads, allowed):
    masked = masked_scores(queries, key_heads, allowed)
    row_max = jnp.max(masked, axis=-1, keepdims=True)
    powers = jnp.exp(masked - row_max)
    row_total = jnp.sum(powers, axis=-1, keepdims=True)
    attn_probs = (powers / row_total).astype(jnp.bfloat16)
    mixed = jnp.einsum("hqk,khd->qhd", attn_probs, val_heads, preferred_element_type=jnp.float32)
    return (mixed, row_max + jnp.log(row_total))


def attention_back(queries, key_heads, val_heads, allowed, log_total, d_mixed):
    masked = masked_scores(queries, key_heads, allowed)
    attn_probs = jnp.exp(masked - log_total)
    probs_low = attn_probs.astype(jnp.bfloat16)
    d_probs = jnp.einsum("qhd,khd->hqk", d_mixed, val_heads, preferred_element_type=jnp.float32)
    row_dot = jnp.sum(attn_probs * d_probs, axis=-1, keepdims=True)
    d_scores = (attn_probs * (d_probs - row_dot)).astype(jnp.bfloat16)
    score_scale = HD ** (-0.5)
    d_query = (
        jnp.einsum("hqk,khd->qhd", d_scores, key_heads, preferred_element_type=jnp.float32)
        * score_scale
    )
    d_key = (
        jnp.einsum("hqk,qhd->khd", d_scores, queries, preferred_element_type=jnp.float32)
        * score_scale
    )
    d_value = jnp.einsum("hqk,qhd->khd", probs_low, d_mixed, preferred_element_type=jnp.float32)
    return (d_query, d_key, d_value)


def forward(resid_rows, weights):
    w_qkv, w_out, w_up, b_up, w_down, gain_attn, gain_mlp = weights
    length = resid_rows.shape[0]
    normed_f, norm_pull = jax.vjp(crms_input, resid_rows, gain_attn.astype(jnp.float32))
    normed = normed_f.astype(jnp.bfloat16)
    project = jnp.dot(normed, w_qkv, preferred_element_type=jnp.float32).astype(jnp.bfloat16)
    positions = lax.iota(jnp.int32, length)
    allowed = positions[:, None] >= positions[None, :]
    mixed_parts = []
    log_parts = []
    for group in range(H // 4):
        mixed_group, log_group = attention_group(
            head_group(project, 0, group),
            head_group(project, D, group),
            head_group(project, 2 * D, group),
            allowed,
        )
        mixed_parts.append(mixed_group.reshape(length, 4 * HD))
        log_parts.append(log_group)
    mixed = jnp.concatenate(mixed_parts, axis=1).astype(jnp.bfloat16)
    attn_out = jnp.dot(mixed, w_out, preferred_element_type=jnp.float32)
    middle = resid_rows + compress(attn_out)
    normed_two_f, norm_two_pull = jax.vjp(crms_input, middle, gain_mlp.astype(jnp.float32))
    normed_two = normed_two_f.astype(jnp.bfloat16)
    hidden = jnp.dot(normed_two, w_up, preferred_element_type=jnp.float32) + b_up.astype(
        jnp.float32
    )
    active_f, gelu_pull = jax.vjp(jax.nn.gelu, hidden)
    active = active_f.astype(jnp.bfloat16)
    mlp_out = jnp.dot(active, w_down, preferred_element_type=jnp.float32)
    result = middle + compress(mlp_out)
    saved = (
        norm_pull,
        normed,
        project,
        allowed,
        log_parts,
        mixed,
        norm_two_pull,
        normed_two,
        gelu_pull,
        active,
    )
    return (result, saved)


def backward(saved, weights, cot_rows):
    w_qkv, w_out, w_up, b_up, w_down, gain_attn, gain_mlp = weights
    (
        norm_pull,
        normed,
        project,
        allowed,
        log_parts,
        mixed,
        norm_two_pull,
        normed_two,
        gelu_pull,
        active,
    ) = saved
    length = cot_rows.shape[0]
    d_mlp = compress_back(cot_rows).astype(jnp.bfloat16)
    grad_down = jnp.einsum("sf,sd->fd", active, d_mlp, preferred_element_type=jnp.float32)
    d_active = jnp.einsum("sd,fd->sf", d_mlp, w_down, preferred_element_type=jnp.float32)
    d_hidden = gelu_pull(d_active)[0].astype(jnp.bfloat16)
    grad_bias = jnp.sum(d_hidden, axis=0, dtype=jnp.float32)
    grad_up = jnp.einsum("sd,sf->df", normed_two, d_hidden, preferred_element_type=jnp.float32)
    d_normed_two = jnp.einsum("sf,df->sd", d_hidden, w_up, preferred_element_type=jnp.float32)
    d_middle, grad_gain_mlp = norm_two_pull(d_normed_two)
    d_middle = d_middle + cot_rows
    d_attn = compress_back(d_middle).astype(jnp.bfloat16)
    grad_out = jnp.einsum("se,sd->ed", mixed, d_attn, preferred_element_type=jnp.float32)
    d_mixed = jnp.einsum("sd,ed->se", d_attn, w_out, preferred_element_type=jnp.float32).astype(
        jnp.bfloat16
    )
    query_parts = []
    key_parts = []
    value_parts = []
    for group in range(H // 4):
        d_mixed_group = d_mixed[:, group * 4 * HD : (group + 1) * 4 * HD].reshape(length, 4, HD)
        d_query, d_key, d_value = attention_back(
            head_group(project, 0, group),
            head_group(project, D, group),
            head_group(project, 2 * D, group),
            allowed,
            log_parts[group],
            d_mixed_group,
        )
        query_parts.append(d_query.reshape(length, 4 * HD))
        key_parts.append(d_key.reshape(length, 4 * HD))
        value_parts.append(d_value.reshape(length, 4 * HD))
    d_project = jnp.concatenate(query_parts + key_parts + value_parts, axis=1).astype(jnp.bfloat16)
    grad_qkv = jnp.einsum("sd,se->de", normed, d_project, preferred_element_type=jnp.float32)
    d_normed = jnp.einsum("se,de->sd", d_project, w_qkv, preferred_element_type=jnp.float32)
    d_resid_rows, grad_gain_attn = norm_pull(d_normed)
    d_resid_rows = d_resid_rows + d_middle
    return (
        d_resid_rows,
        (grad_qkv, grad_out, grad_up, grad_bias, grad_down, grad_gain_attn, grad_gain_mlp),
    )


AXES = ("wide", "narrow")


def bits_of(count):
    return count.bit_length() - 1


class Plan:
    def __init__(self, mesh):
        self.wide, self.narrow = mesh.shape["wide"], mesh.shape["narrow"]
        self.count = self.wide * self.narrow
        low = bits_of(self.narrow)
        self.bits = bits_of(self.count)
        self.core = low
        outer = list(range(low + 1, self.bits))
        self.y_stages = [(b,) for b in range(low)]
        self.x_stages = [(b,) for b in outer[:1]]
        rest = outer[1:]
        self.z_stages = [tuple(rest[i : i + 2]) for i in range(0, len(rest), 2)]

    def index(self):
        return lax.axis_index("wide") * self.narrow + lax.axis_index("narrow")

    def send(self, value, mask):
        return lax.ppermute(value, AXES, [(i, i ^ mask) for i in range(self.count)])

    def masks(self, stage):
        return [sum(((m >> k) & 1) << b for k, b in enumerate(stage)) for m in range(1 << len(stage))]

    def gather(self, shard, stages):
        me = self.index()
        held = []
        value = shard
        for stage in stages:
            arrived = [value] + [self.send(value, m) for m in self.masks(stage)[1:]]
            mine = [(me >> b) & 1 for b in stage]
            for k, b in enumerate(stage):
                axis = sum(1 for h in held if h > b)
                pairs = []
                for j in range(0, len(arrived), 2):
                    first, second = arrived[j], arrived[j + 1]
                    pairs.append(
                        jnp.where(mine[k] == 1, jnp.stack([second, first], axis), jnp.stack([first, second], axis))
                    )
                arrived = pairs
                held = sorted(held + [b], reverse=True)
            value = arrived[0]
        return value.reshape((self.count,) + shard.shape)

    def scatter_sum(self, blocks, stages, add):
        me = self.index()
        value = blocks.reshape((2,) * self.bits + blocks.shape[1:])
        held = list(range(self.bits - 1, -1, -1))
        for number, stage in enumerate(stages):
            last = number == len(stages) - 1
            parts = {0: value}
            for b in stage:
                axis = held.index(b)
                bit = (me >> b) & 1
                fresh = {}
                for m, part in parts.items():
                    fresh[m] = lax.dynamic_index_in_dim(part, bit, axis, keepdims=False)
                    fresh[m | (1 << b)] = lax.dynamic_index_in_dim(part, 1 - bit, axis, keepdims=False)
                parts = fresh
                held.remove(b)
            arrived = [parts[0]] + [self.send(parts[m], m) for m in parts if m]
            value = add(arrived, last)
        return value


def add_plain(arrived, last):
    total = arrived[0].astype(jnp.float32)
    for part in arrived[1:]:
        total = total + part.astype(jnp.float32)
    return total if last else total.astype(jnp.bfloat16)


def split_two(value):
    high = lax.reduce_precision(value, 8, 7)
    return jnp.concatenate([high, value - high], axis=-1).astype(jnp.bfloat16)


def add_tail(width):
    def add(arrived, last):
        main = add_plain([a[..., :width] for a in arrived], last)
        tail = 0.0
        for part in arrived:
            whole = part[..., width:].astype(jnp.float32)
            tail = tail + (whole[..., :64] + whole[..., 64:])
        if last:
            return (main, tail)
        return jnp.concatenate([main, split_two(tail)], axis=-1)

    return add


def device_step(plan, resid_in, w_qkv, w_out, w_up, b_up, w_down, gain_attn, gain_mlp, cotangent):
    rows = w_qkv.shape[0]
    tokens = resid_in.shape[0]
    x, y, z, core = plan.x_stages, plan.y_stages, plan.z_stages, [(plan.core,)]
    small = jnp.concatenate(
        [gain_attn[:, None], gain_mlp[:, None], b_up.reshape(4, rows).T, jnp.zeros((rows, 122), jnp.bfloat16)], axis=1
    )
    first = plan.gather(w_qkv[:, : 2 * D], z + x + y + core).reshape(D, 2 * D)
    second = plan.gather(jnp.concatenate([w_qkv[:, 2 * D :], w_out, small], axis=1), z + y + x + core).reshape(D, 2 * D + 128)
    full_up = plan.gather(w_up, z + x + y + core).reshape(D, 4 * D)
    full_down = plan.gather(w_down, z + y + x + core).reshape(4 * D, D)
    full_qkv = jnp.concatenate([first, second[:, :D]], axis=1)
    full_out = second[:, D : 2 * D]
    tail = second[:, 2 * D :]
    full_ga, full_gm = tail[:, 0], tail[:, 1]
    full_b = tail[:, 2:6].reshape(plan.count, rows, 4).transpose(0, 2, 1).reshape(4 * D)
    weights = (full_qkv, full_out, full_up, full_b, full_down, full_ga, full_gm)
    outs, dres, grads = [], [], None
    for start in range(0, tokens, TOK_MB):
        result, saved = forward(resid_in[start : start + TOK_MB].astype(jnp.float32), weights)
        outs.append(result.astype(jnp.bfloat16))
        d_rows, g = backward(saved, weights, cotangent[start : start + TOK_MB].astype(jnp.float32))
        dres.append(d_rows)
        grads = g if grads is None else jax.tree.map(jnp.add, grads, g)
    g_qkv, g_out, g_up, g_b, g_down, g_ga, g_gm = grads
    low = jnp.bfloat16
    s_down = plan.scatter_sum(g_down.astype(low).reshape(plan.count, 4 * rows, D), core + x + y + z, add_plain)
    s_up = plan.scatter_sum(g_up.astype(low).reshape(plan.count, rows, 4 * D), core + y + x + z, add_plain)
    small_grads = jnp.concatenate(
        [
            g_ga[:, None],
            g_gm[:, None],
            g_b.reshape(plan.count, 4, rows).transpose(0, 2, 1).reshape(D, 4),
            jnp.zeros((D, 58), jnp.float32),
        ],
        axis=1,
    )
    b_in = jnp.concatenate([g_qkv[:, 2 * D :].astype(low), g_out.astype(low), split_two(small_grads)], axis=1)
    s_second, s_tail = plan.scatter_sum(b_in.reshape(plan.count, rows, 2 * D + 128), core + x + y + z, add_tail(2 * D))
    s_first = plan.scatter_sum(g_qkv[:, : 2 * D].astype(low).reshape(plan.count, rows, 2 * D), core + y + x + z, add_plain)
    return (
        jnp.concatenate(outs, axis=0),
        jnp.concatenate(dres, axis=0),
        jnp.concatenate([s_first, s_second[:, :D]], axis=1),
        s_second[:, D:],
        s_up,
        s_tail[:, 2:6].T.reshape(4 * rows),
        s_down,
        s_tail[:, 0],
        s_tail[:, 1],
    )


def solution(mesh):
    rows2, rows1 = P(AXES, None), P(AXES)
    in_specs = (rows2, rows2, rows2, rows2, rows1, rows2, rows1, rows1, rows2)
    out_specs = (rows2, rows2, rows2, rows2, rows2, rows1, rows2, rows1, rows1)
    plan = Plan(mesh)

    def on_device(*arrays):
        return device_step(plan, *arrays)

    return jax.shard_map(on_device, mesh=mesh, in_specs=in_specs, out_specs=out_specs, check_vma=False)
```

```python
import functools
import math

import jax
import jax.numpy as jnp
from jax import lax
from jax.experimental import pallas as pl
from jax.experimental.pallas import tpu as pltpu
from jax.sharding import PartitionSpec as P

D = 768
H = 12
HD = 64
FF = 3072
SEQ = 256
HALF = 384
EPS = 1e-05
AXES = ("wide", "narrow")
F32 = jnp.float32
BF16 = jnp.bfloat16
MIB = 1 << 20

VMEM_SPEC = pl.BlockSpec(memory_space=pltpu.VMEM)
SMEM_SPEC = pl.BlockSpec(memory_space=pltpu.SMEM)


def dot_nn(a, b):
    return lax.dot_general(a, b, (((1,), (0,)), ((), ())), preferred_element_type=F32)


def dot_nt(a, b):
    return lax.dot_general(a, b, (((1,), (1,)), ((), ())), preferred_element_type=F32)


def dot_tn(a, b):
    return lax.dot_general(a, b, (((0,), (0,)), ((), ())), preferred_element_type=F32)


def last_lane(shape):
    return lax.broadcasted_iota(jnp.int32, shape, 1) == D - 1


def decomp(padded):
    total = jnp.sum(padded, axis=1, keepdims=True)
    return jnp.where(last_lane(padded.shape), -total, padded)


def inv_rms(values):
    return lax.rsqrt(jnp.mean(values * values, axis=1, keepdims=True) + EPS)


def norm_back(x, r, gain, dh):
    xdh = x * dh
    dx = r * (gain * dh) - x * (r * r * r) * jnp.mean(xdh * gain, axis=1, keepdims=True)
    return dx, xdh * r


def decomp_back(dx):
    return dx - dx[:, D - 1 :]


def call(body, outs, *args, scratch=(), limit=40, flops=0, smem=0):
    n_smem = smem
    specs = [SMEM_SPEC] * n_smem + [VMEM_SPEC] * (len(args) - n_smem)
    return pl.pallas_call(
        body,
        out_shape=[jax.ShapeDtypeStruct(s, d) for s, d in outs],
        in_specs=specs,
        out_specs=[VMEM_SPEC] * len(outs),
        scratch_shapes=list(scratch),
        compiler_params=pltpu.CompilerParams(vmem_limit_bytes=limit * MIB),
        cost_estimate=pl.CostEstimate(flops=int(flops), bytes_accessed=0, transcendentals=0),
    )(*args)


def assemble(tab, pieces, out_ref):
    at = 0
    for ref in pieces:
        count, rows = ref.shape[0], ref.shape[1]
        for m in range(count):
            out_ref[pl.ds(pl.multiple_of(tab[at], rows), rows), :] = ref[m]
            at += 1


def to_relative(tab, full, out_ref, rows):
    for s in range(full.shape[0] // rows):
        out_ref[rows * s : rows * (s + 1), :] = full[pl.ds(pl.multiple_of(tab[s], rows), rows), :]


def row_loop(total, step, body):
    def go(i, carry):
        body(pl.multiple_of(i * step, step))
        return carry

    lax.fori_loop(0, total // step, go, 0)


def attend(qkv_ref, attn_ref, tokens, out_at):
    i_at = lax.broadcasted_iota(jnp.int32, (SEQ, SEQ), 0)
    j_at = lax.broadcasted_iota(jnp.int32, (SEQ, SEQ), 1)
    allowed = j_at <= i_at
    low = lax.broadcasted_iota(jnp.int32, (SEQ, 128), 1) < HD

    def one(seq):
        rows = pl.ds(seq, SEQ)
        for pair in range(HALF // 128):
            cols = slice(128 * pair, 128 * (pair + 1))
            q2 = qkv_ref[rows, cols]
            k2 = qkv_ref[rows, HALF + 128 * pair : HALF + 128 * (pair + 1)]
            v2 = qkv_ref[rows, 2 * HALF + 128 * pair : 2 * HALF + 128 * (pair + 1)]
            mixed = None
            for side in range(2):
                mine = low if side == 0 else jnp.logical_not(low)
                k_one = jnp.where(mine, k2, jnp.zeros_like(k2))
                v_one = jnp.where(mine, v2, jnp.zeros_like(v2))
                scores = jnp.where(allowed, dot_nt(q2, k_one) * (HD ** -0.5), -1e30)
                top = jnp.max(scores, axis=1, keepdims=True)
                powers = jnp.exp(scores - top)
                total = jnp.sum(powers, axis=1, keepdims=True)
                probs = (powers * (1.0 / total)).astype(BF16)
                part = dot_nn(probs, v_one)
                mixed = part if mixed is None else mixed + part
            attn_ref[rows, out_at + 128 * pair : out_at + 128 * (pair + 1)] = mixed.astype(BF16)

    row_loop(tokens, SEQ, one)


def k_first(n_pieces, tab, rel, resid_ref, *refs):
    pieces, (qkv_ref, attn_ref, w_ref, h_ref, ht_ref, tail_ref), (w_all, ht_all) = (
        refs[:n_pieces],
        refs[n_pieces : n_pieces + 6],
        refs[n_pieces + 6 :],
    )
    tokens = resid_ref.shape[0]
    assemble(tab, pieces, w_all)
    w_ref[...] = w_all[:, : 3 * HALF]
    tail = w_all[:, 3 * HALF :].astype(F32).T
    tail_ref[...] = tail[:8, :]
    gain = tail[0:1, :]

    def norm(at):
        rows = pl.ds(at, 32)
        x1 = decomp(resid_ref[rows, :].astype(F32))
        h_ref[rows, :] = (x1 * inv_rms(x1) * gain).astype(BF16)

    row_loop(tokens, 32, norm)
    qkv_ref[...] = dot_nn(h_ref[...], w_ref[...]).astype(BF16)
    attend(qkv_ref, attn_ref, tokens, 0)
    ht_all[...] = h_ref[...].T
    to_relative(rel, ht_all, ht_ref, D // rel.shape[0])


def k_second(n_pieces, tab, rel, resid_ref, h_ref, attn0_ref, gains_ref, *refs):
    pieces, (qkv_ref, w_ref, wo_ref, attnt_ref, x2_ref, h2_ref, h2t_ref), (w_all, attn_ref, t_all) = (
        refs[:n_pieces],
        refs[n_pieces : n_pieces + 7],
        refs[n_pieces + 7 :],
    )
    tokens = resid_ref.shape[0]
    assemble(tab, pieces, w_all)
    w_ref[...] = w_all[:, : 3 * HALF]
    wo_ref[...] = w_all[:, 3 * HALF :]
    qkv_ref[...] = dot_nn(h_ref[...], w_ref[...]).astype(BF16)
    attn_ref[:, :HALF] = attn0_ref[...]
    attend(qkv_ref, attn_ref, tokens, HALF)
    gain = gains_ref[1:2, :]
    x2_ref[...] = dot_nn(attn_ref[...], wo_ref[...])

    def norm(at):
        rows = pl.ds(at, 32)
        y = x2_ref[rows, :]
        middle = resid_ref[rows, :].astype(F32) + (y - jnp.mean(y, axis=1, keepdims=True))
        x2 = decomp(jnp.where(last_lane(middle.shape), 0.0, middle))
        x2_ref[rows, :] = x2
        h2_ref[rows, :] = (x2 * inv_rms(x2) * gain).astype(BF16)

    row_loop(tokens, 32, norm)
    blocks = D // rel.shape[0]
    t_all[...] = attn_ref[...].T
    to_relative(rel, t_all, attnt_ref, blocks)
    t_all[...] = h2_ref[...].T
    to_relative(rel, t_all, h2t_ref, blocks)


GELU_A = math.sqrt(2.0 / math.pi)
GELU_B = 0.044715


def k_up(n_pieces, tab, slots, h2_ref, gains_ref, spread_ref, pick_ref, *refs):
    pieces, (w_ref, act_ref, actt_ref, slope_ref), (u_ref,) = (
        refs[:n_pieces],
        refs[n_pieces : n_pieces + 4],
        refs[n_pieces + 4 :],
    )
    tokens = h2_ref.shape[0]
    assemble(tab, pieces, w_ref)
    blocks = min(FF // slots.shape[0], D)
    wide = D
    for tile in range(FF // wide):
        cols = slice(tile * wide, (tile + 1) * wide)
        u_ref[...] = dot_nn(h2_ref[...], w_ref[:, cols])
        part = tile * wide // (FF // 2)
        inner = tile * wide - part * (FF // 2)
        small = gains_ref[:, part * (D // 2) : (part + 1) * (D // 2)].astype(BF16)
        spread = dot_nn(small, spread_ref[:, inner : inner + wide])
        bias = jnp.sum(spread * pick_ref[:, inner : inner + wide], axis=0, keepdims=True)

        def gelu(at):
            rows = pl.ds(at, 32)
            u = u_ref[rows, :] + bias
            square = u * u
            t = jnp.tanh(GELU_A * (u + GELU_B * (square * u)))
            half = 0.5 * (1.0 + t)
            act_ref[rows, cols] = (u * half).astype(BF16)
            slope_ref[rows, cols] = half + (0.5 * u) * (1.0 - t * t) * (GELU_A * (1.0 + (3.0 * GELU_B) * square))

        row_loop(tokens, 32, gelu)
        turned = act_ref[:, cols].T
        for b in range(wide // blocks):
            q = tile * wide // blocks + b
            to = q * blocks if slots.shape[0] == 1 else pl.multiple_of(slots[q], blocks)
            actt_ref[pl.ds(to, blocks), :] = turned[b * blocks : (b + 1) * blocks, :]


def k_grad_down(cot_ref, actt_ref, keep_ref, send_ref, dz_ref):
    tokens = cot_ref.shape[0]

    def rows32(at):
        rows = pl.ds(at, 32)
        c = cot_ref[rows, :].astype(F32)
        dz_ref[rows, :] = (c - jnp.mean(c, axis=1, keepdims=True)).astype(BF16)

    row_loop(tokens, 32, rows32)
    split_dot(actt_ref, dz_ref, keep_ref, send_ref)


def split_dot(left_ref, right_ref, keep_ref, send_ref):
    half = left_ref.shape[0] // 2
    for ref, start in ((send_ref, half), (keep_ref, 0)):
        for at in range(0, half, 384):
            rows = min(384, half - at)
            ref[at : at + rows, :] = dot_nn(left_ref[start + at : start + at + rows, :], right_ref[...]).astype(BF16)


def k_down(n_pieces, tab, x2_ref, act_ref, dz_ref, slope_ref, *refs):
    pieces, (out_ref, du_ref, gb_ref), (w_ref, z_ref) = (
        refs[:n_pieces],
        refs[n_pieces : n_pieces + 3],
        refs[n_pieces + 3 :],
    )
    tokens = act_ref.shape[0]
    assemble(tab, pieces, w_ref)
    wide = D
    for tile in range(FF // wide):
        cols = slice(tile * wide, (tile + 1) * wide)
        z_ref[...] = dot_nt(dz_ref[...], w_ref[cols, :])

        def slope(i, total):
            rows = pl.ds(pl.multiple_of(i * 32, 32), 32)
            du = (z_ref[rows, :] * slope_ref[rows, cols]).astype(BF16)
            du_ref[rows, cols] = du
            d32 = du.astype(F32)
            return total + (d32[0:8] + d32[8:16]) + (d32[16:24] + d32[24:32])

        total = lax.fori_loop(0, tokens // 32, slope, jnp.zeros((8, wide), F32))
        gb_ref[:, cols] = jnp.sum(total, axis=0, keepdims=True)
    z_ref[...] = dot_nn(act_ref[...], w_ref[...])

    def result(at):
        rows = pl.ds(at, 32)
        z = z_ref[rows, :]
        out_ref[rows, :] = (x2_ref[rows, :] + (z - jnp.mean(z, axis=1, keepdims=True))).astype(BF16)

    row_loop(tokens, 32, result)


def k_mid(cot_ref, x2_ref, gains_ref, du_ref, w_up_ref, attnt_ref, dmid_ref, dy_ref, gg_ref, keep_ref, send_ref, dh_ref):
    tokens = cot_ref.shape[0]
    dh_ref[...] = dot_nt(du_ref[...], w_up_ref[...])
    gain = gains_ref[1:2, :]

    def back(i, total):
        rows = pl.ds(pl.multiple_of(i * 32, 32), 32)
        x2 = x2_ref[rows, :]
        dx, summand = norm_back(x2, inv_rms(x2), gain, dh_ref[rows, :])
        dmid = cot_ref[rows, :].astype(F32) + decomp_back(dx)
        dmid_ref[rows, :] = dmid
        dy_ref[rows, :] = (dmid - jnp.mean(dmid, axis=1, keepdims=True)).astype(BF16)
        return total + (summand[0:8] + summand[8:16]) + (summand[16:24] + summand[24:32])

    total = lax.fori_loop(0, tokens // 32, back, jnp.zeros((8, D), F32))
    gg_ref[...] = jnp.sum(total, axis=0, keepdims=True)
    split_dot(attnt_ref, dy_ref, keep_ref, send_ref)


def k_grad_up(h2t_ref, du_ref, keep_ref, send_ref):
    split_dot(h2t_ref, du_ref, keep_ref, send_ref)


def k_attn_back(group, dy_ref, wo_ref, qkv_ref, ht_ref, dqkv_ref, keep_ref, send_ref, da_ref):
    tokens = dy_ref.shape[0]
    da_ref[...] = dot_nt(dy_ref[...], wo_ref[HALF * group : HALF * (group + 1), :]).astype(BF16)
    j_at = lax.broadcasted_iota(jnp.int32, (SEQ, SEQ), 0)
    i_at = lax.broadcasted_iota(jnp.int32, (SEQ, SEQ), 1)
    allowed = j_at <= i_at
    low = lax.broadcasted_iota(jnp.int32, (SEQ, 128), 1) < HD
    scale = HD ** -0.5

    def one(seq):
        rows = pl.ds(seq, SEQ)
        for pair in range(HALF // 128):
            cols = [slice(HALF * part + 128 * pair, HALF * part + 128 * (pair + 1)) for part in range(3)]
            q2, k2, v2 = (qkv_ref[rows, c] for c in cols)
            d2 = da_ref[rows, cols[0]]
            dq = dk = dv = None
            for side in range(2):
                mine = low if side == 0 else jnp.logical_not(low)
                q1, k1, v1, d1 = (jnp.where(mine, a, jnp.zeros_like(a)) for a in (q2, k2, v2, d2))
                scores = jnp.where(allowed, dot_nt(k1, q2) * scale, -1e30)
                top = jnp.max(scores, axis=0, keepdims=True)
                powers = jnp.exp(scores - top)
                probs = powers * (1.0 / jnp.sum(powers, axis=0, keepdims=True))
                dp = dot_nt(v1, d2)
                inner = jnp.sum(probs * dp, axis=0, keepdims=True)
                ds = (probs * (dp - inner)).astype(BF16)
                parts = (dot_tn(ds, k1), dot_nn(ds, q1), dot_nn(probs.astype(BF16), d1))
                dq, dk, dv = parts if dq is None else (dq + parts[0], dk + parts[1], dv + parts[2])
            dqkv_ref[rows, cols[0]] = (dq * scale).astype(BF16)
            dqkv_ref[rows, cols[1]] = (dk * scale).astype(BF16)
            dqkv_ref[rows, cols[2]] = dv.astype(BF16)

    row_loop(tokens, SEQ, one)
    split_dot(ht_ref, dqkv_ref, keep_ref, send_ref)


def round_low(value):
    return value.astype(BF16).astype(F32)


def k_last(resid_ref, dmid_ref, gains_ref, dq0_ref, w0_ref, dq1_ref, w1_ref, gg_ref, gb_ref, spread_ref, pick_ref, out_ref, tail_ref, dh_ref):
    tokens = resid_ref.shape[0]
    dh_ref[...] = dot_nt(dq0_ref[...], w0_ref[...]) + dot_nt(dq1_ref[...], w1_ref[...])
    gain = gains_ref[0:1, :]

    def back(i, total):
        rows = pl.ds(pl.multiple_of(i * 32, 32), 32)
        x1 = decomp(resid_ref[rows, :].astype(F32))
        dx, summand = norm_back(x1, inv_rms(x1), gain, dh_ref[rows, :])
        out_ref[rows, :] = dmid_ref[rows, :] + decomp_back(dx)
        return total + (summand[0:8] + summand[8:16]) + (summand[16:24] + summand[24:32])

    total = lax.fori_loop(0, tokens // 32, back, jnp.zeros((8, D), F32))
    ga = jnp.sum(total, axis=0, keepdims=True)
    parts = []
    for part in range(2):
        g = gb_ref[:, part * (FF // 2) : (part + 1) * (FF // 2)] * pick_ref[...]
        high = g.astype(BF16)
        lower = (g - high.astype(F32)).astype(BF16)
        parts.append(dot_nt(high, spread_ref[...]) + dot_nt(lower, spread_ref[...]))
    biases = jnp.concatenate(parts, axis=1)
    row = lax.broadcasted_iota(jnp.int32, (8, D), 0)
    rows8 = jnp.where(row == 0, ga, jnp.where(row == 1, gg_ref[...], biases))
    high = rows8.astype(BF16).astype(F32)
    both = jnp.concatenate([high, rows8 - high, jnp.zeros((112, D), F32)], axis=0)
    tail_ref[...] = both.T.astype(BF16)


def bits_of(count):
    return count.bit_length() - 1


class Plan:
    def __init__(self, mesh):
        self.wide, self.narrow = mesh.shape["wide"], mesh.shape["narrow"]
        self.count = self.wide * self.narrow
        low = bits_of(self.narrow)
        self.bits = bits_of(self.count)
        self.core = low
        outer = list(range(low + 1, self.bits))
        self.y = list(range(low))
        self.x = outer[0]
        self.z = outer[1:]
        self.fine = (D // self.count) * self.narrow % 16 == 0 and len(self.y) == 1 and len(self.z) == 2

    def index(self):
        return lax.axis_index("wide") * self.narrow + lax.axis_index("narrow")

    def send(self, value, mask):
        return lax.ppermute(value, AXES, [(i, i ^ mask) for i in range(self.count)])

    def z_masks(self):
        return [((m & 1) << self.z[0]) | ((m >> 1) << self.z[1]) for m in range(4)]

    def slot_masks(self):
        return [c | x | z for c in (0, 1 << self.core) for x in (0, 1 << self.x) for z in self.z_masks()]

    def block_starts(self, rows):
        me = self.index()
        if not self.fine:
            return jnp.zeros((1,), jnp.int32)
        masks = jnp.array(self.slot_masks(), jnp.int32)
        return ((me ^ masks) >> bits_of(self.narrow)) * (rows * self.narrow)

    def slot_starts(self, rows):
        if not self.fine:
            return jnp.zeros((1,), jnp.int32)
        me = self.index()
        low = bits_of(self.narrow)
        q = jnp.arange(self.count // self.narrow, dtype=jnp.int32)
        diff = q ^ (me >> low)
        bit = lambda b: (diff >> (b - low)) & 1
        slot = bit(self.core) * 8 + bit(self.x) * 4 + bit(self.z[1]) * 2 + bit(self.z[0])
        return slot * (rows * self.narrow)

    def pair_up(self, own, other, bit, axis):
        mine = (self.index() >> bit) & 1
        return jnp.where(mine == 1, jnp.stack([other, own], axis), jnp.stack([own, other], axis))

    def gather(self, shard, y_last):
        rows, columns = shard.shape
        if not self.fine:
            return [self.gather_plain(shard)]
        y = self.y[0]
        group = [shard] + [self.send(shard, m) for m in self.z_masks()[1:]]
        four = jnp.stack(group, 0)
        if y_last:
            moved = self.send(four, 1 << self.x)
            own = jnp.concatenate([four, moved], 0)
            value = [self.pair_up(own, self.send(own, 1 << y), y, 1).reshape(8, 2 * rows, columns)]
        else:
            own = self.pair_up(four, self.send(four, 1 << y), y, 1).reshape(4, 2 * rows, columns)
            value = [own, self.send(own, 1 << self.x)]
        return value + [self.send(v, 1 << self.core) for v in value]

    def gather_plain(self, shard):
        me = self.index()
        value, held = shard, []
        for b in self.z + [self.x] + self.y + [self.core]:
            axis = sum(1 for h in held if h > b)
            value = self.pair_up(value, self.send(value, 1 << b), b, axis)
            held.append(b)
        return value.reshape(1, -1, shard.shape[1])

    def scatter_sum(self, keep, send, y_first, add):
        if not self.fine:
            return self.scatter_plain(jnp.concatenate([keep, send], 0), add)
        columns = keep.shape[1]
        got = self.send(send, 1 << self.core)
        rows = keep.shape[0] // 16
        shape = (2, 4, 2, rows, columns)
        a, b = keep.reshape(shape), got.reshape(shape)
        y = self.y[0]
        bit = (self.index() >> y) & 1
        pick = lambda v, axis, which: lax.dynamic_index_in_dim(v, which, axis, keepdims=False)
        if y_first:
            mine = add([pick(a, 2, bit), pick(b, 2, bit)], False)
            yours = add([pick(a, 2, 1 - bit), pick(b, 2, 1 - bit)], False)
            got = self.send(yours, 1 << y)
            mine, yours = add([mine[0], got[0]], False), add([mine[1], got[1]], False)
            got = self.send(yours, 1 << self.x)
        else:
            mine, yours = add([a[0], b[0]], False), add([a[1], b[1]], False)
            got = self.send(yours, 1 << self.x)
            mine, yours = (
                add([pick(mine, 1, bit), pick(got, 1, bit)], False),
                add([pick(mine, 1, 1 - bit), pick(got, 1, 1 - bit)], False),
            )
            got = self.send(yours, 1 << y)
        outs = [add([mine[m], got[m]], False) for m in range(4)]
        return add([outs[0]] + [self.send(outs[m], self.z_masks()[m]) for m in range(1, 4)], True)

    def scatter_plain(self, blocks, add):
        me = self.index()
        value = blocks.reshape((2,) * self.bits + (-1, blocks.shape[1]))
        held = list(range(self.bits - 1, -1, -1))
        order = [self.core] + self.y + [self.x] + self.z
        for b in order:
            axis, bit = held.index(b), (me >> b) & 1
            mine = lax.dynamic_index_in_dim(value, bit, axis, keepdims=False)
            yours = lax.dynamic_index_in_dim(value, 1 - bit, axis, keepdims=False)
            held.remove(b)
            value = add([mine, self.send(yours, 1 << b)], not held)
        return value


def add_plain(arrived, last):
    total = arrived[0].astype(F32)
    for part in arrived[1:]:
        total = total + part.astype(F32)
    return total if last else total.astype(BF16)


def add_two(arrived, last):
    total = 0.0
    for part in arrived:
        whole = part.astype(F32)
        total = total + (whole[..., :8] + whole[..., 8:16])
    if last:
        return total
    high = lax.reduce_precision(total, 8, 7)
    rest = jnp.zeros(total.shape[:-1] + (112,), F32)
    return jnp.concatenate([high, total - high, rest], axis=-1).astype(BF16)


def after(value, *others):
    return lax.optimization_barrier((value,) + others)[0]


def device_step(plan, resid_in, w_qkv, w_out, w_up, b_up, w_down, gain_attn, gain_mlp, cotangent):
    rows = w_qkv.shape[0]
    tokens = resid_in.shape[0]
    resid = jnp.pad(resid_in, ((0, 0), (0, 1)))
    cot = jnp.pad(cotangent, ((0, 0), (0, 1)))
    small = jnp.concatenate(
        [gain_attn[:, None], gain_mlp[:, None], b_up.reshape(4, rows).T, jnp.zeros((rows, 122), BF16)], axis=1
    )
    group = lambda g: [w_qkv[:, part * D + g * HALF : part * D + (g + 1) * HALF] for part in range(3)]
    p_first = plan.gather(jnp.concatenate(group(0) + [small], axis=1), False)
    p_second = plan.gather(jnp.concatenate(group(1) + [w_out], axis=1), False)
    p_up = plan.gather(w_up, False)
    p_down = plan.gather(w_down, True)

    tab = plan.block_starts(rows)
    tab4 = plan.block_starts(4 * rows)
    slots4 = plan.slot_starts(4 * rows)
    half = D // 2
    i_at = lax.broadcasted_iota(jnp.int32, (half, 4 * half), 0)
    f_at = lax.broadcasted_iota(jnp.int32, (half, 4 * half), 1)
    spread = ((i_at // rows == f_at // (4 * rows)) & (i_at % rows == f_at % rows)).astype(BF16)
    f8 = lax.broadcasted_iota(jnp.int32, (8, 4 * half), 1)
    r8 = lax.broadcasted_iota(jnp.int32, (8, 4 * half), 0)
    pick = ((f8 // rows) % 4 + 2 == r8).astype(F32)

    wide3 = 3 * HALF
    t, d = tokens, D
    qkv0, attn0, w0, h1, h1t, gains = call(
        functools.partial(k_first, len(p_first)),
        [((t, wide3), BF16), ((t, HALF), BF16), ((d, wide3), BF16), ((t, d), BF16), ((d, t), BF16), ((8, d), F32)],
        tab, tab, resid, *p_first,
        scratch=[pltpu.VMEM((d, wide3 + 128), BF16), pltpu.VMEM((d, t), BF16)],
        flops=4e9, smem=2,
    )
    qkv1, w1, wo, attnt, x2, h2, h2t = call(
        functools.partial(k_second, len(p_second)),
        [((t, wide3), BF16), ((d, wide3), BF16), ((d, d), BF16), ((d, t), BF16), ((t, d), F32), ((t, d), BF16), ((d, t), BF16)],
        tab, tab, resid, h1, attn0, gains, *p_second,
        scratch=[pltpu.VMEM((d, wide3 + d), BF16), pltpu.VMEM((t, d), BF16), pltpu.VMEM((d, t), BF16)],
        flops=5e9, smem=2,
    )
    wu, act, actt, slope = call(
        functools.partial(k_up, len(p_up)),
        [((d, FF), BF16), ((t, FF), BF16), ((FF, t), BF16), ((t, FF), F32)],
        tab, slots4, h2, gains, spread, pick, *p_up,
        scratch=[pltpu.VMEM((t, d), F32)],
        flops=4e9, smem=2,
    )
    keep_d, send_d, dz = call(
        k_grad_down, [((FF // 2, d), BF16), ((FF // 2, d), BF16), ((t, d), BF16)], cot, actt, flops=3e9
    )
    out, du, gb = call(
        functools.partial(k_down, len(p_down)),
        [((t, d), BF16), ((t, FF), BF16), ((1, FF), F32)],
        tab4, x2, act, dz, slope, *p_down,
        scratch=[pltpu.VMEM((FF, d), BF16), pltpu.VMEM((t, d), F32)],
        flops=6e9, smem=1,
    )
    keep_u, send_u = call(k_grad_up, [((half, FF), BF16), ((half, FF), BF16)], h2t, du, flops=3e9)
    dmid, dy, gg, keep_o, send_o = call(
        k_mid,
        [((t, d), F32), ((t, d), BF16), ((1, d), F32), ((half, d), BF16), ((half, d), BF16)],
        cot, x2, gains, after(du, keep_u), wu, attnt,
        scratch=[pltpu.VMEM((t, d), F32)],
        flops=4e9,
    )
    back_outs = [((t, wide3), BF16), ((half, wide3), BF16), ((half, wide3), BF16)]
    back_scratch = [pltpu.VMEM((t, HALF), BF16)]
    dqkv1, keep_1, send_1 = call(
        functools.partial(k_attn_back, 1), back_outs, dy, wo, qkv1, h1t, scratch=back_scratch, flops=6e9
    )
    dqkv0, keep_0, send_0 = call(
        functools.partial(k_attn_back, 0), back_outs, after(dy, keep_1), wo, qkv0, h1t, scratch=back_scratch, flops=6e9
    )
    dres, tail = call(
        k_last,
        [((t, d), F32), ((d, 128), BF16)],
        resid, dmid, gains, dqkv0, w0, dqkv1, w1, gg, gb, spread, pick,
        scratch=[pltpu.VMEM((t, d), F32)],
        flops=3e9,
    )

    s_down = plan.scatter_sum(keep_d, send_d, True, add_plain)
    s_up = plan.scatter_sum(keep_u, send_u, False, add_plain)
    s_second = plan.scatter_sum(
        jnp.concatenate([keep_1, keep_o], 1), jnp.concatenate([send_1, send_o], 1), False, add_plain
    )
    s_first = plan.scatter_sum(keep_0, send_0, False, add_plain)
    if plan.fine:
        ordered = tail.reshape(-1, rows * plan.narrow, 128)[tab // (rows * plan.narrow)].reshape(d, 128)
    else:
        ordered = tail
    s_tail = plan.scatter_sum(ordered[:half], ordered[half:], True, add_two)
    s_qkv = jnp.concatenate(
        [piece for part in range(3) for piece in (s_first[:, part * HALF : (part + 1) * HALF], s_second[:, part * HALF : (part + 1) * HALF])],
        axis=1,
    )
    return (
        out[:, : d - 1],
        dres[:, : d - 1],
        s_qkv,
        s_second[:, wide3:],
        s_up,
        s_tail[:, 2:6].T.reshape(4 * rows),
        s_down,
        s_tail[:, 0],
        s_tail[:, 1],
    )


def solution(mesh):
    rows2, rows1 = P(AXES, None), P(AXES)
    in_specs = (rows2, rows2, rows2, rows2, rows1, rows2, rows1, rows1, rows2)
    out_specs = (rows2, rows2, rows2, rows2, rows2, rows1, rows2, rows1, rows1)
    plan = Plan(mesh)

    def on_device(*arrays):
        return device_step(plan, *arrays)

    return jax.shard_map(on_device, mesh=mesh, in_specs=in_specs, out_specs=out_specs, check_vma=False)
```

```python
import functools
import math

import jax
import jax.numpy as jnp
from jax import lax
from jax.experimental import pallas as pl
from jax.experimental.pallas import tpu as pltpu
from jax.sharding import PartitionSpec as P

D = 768
H = 12
HD = 64
FF = 3072
SEQ = 256
HALF = 384
EPS = 1e-05
AXES = ("wide", "narrow")
F32 = jnp.float32
BF16 = jnp.bfloat16
MIB = 1 << 20
LIMIT = 12

VMEM_SPEC = pl.BlockSpec(memory_space=pltpu.VMEM)
SMEM_SPEC = pl.BlockSpec(memory_space=pltpu.SMEM)
ANY_SPEC = pl.BlockSpec(memory_space=pl.ANY)


def dot_nn(a, b):
    return lax.dot_general(a, b, (((1,), (0,)), ((), ())), preferred_element_type=F32)


def dot_nt(a, b):
    return lax.dot_general(a, b, (((1,), (1,)), ((), ())), preferred_element_type=F32)


def dot_tn(a, b):
    return lax.dot_general(a, b, (((0,), (0,)), ((), ())), preferred_element_type=F32)


STEP = 128


def last_lane(shape):
    return lax.broadcasted_iota(jnp.int32, shape, 1) == D - 1


def decomp(padded):
    total = jnp.sum(padded, axis=1, keepdims=True)
    return jnp.where(last_lane(padded.shape), -total, padded)


def inv_rms(values):
    return lax.rsqrt(jnp.mean(values * values, axis=1, keepdims=True) + EPS)


def norm_back(x, r, gain, dh):
    xdh = x * dh
    dx = r * (gain * dh) - x * (r * r * r) * jnp.mean(xdh * gain, axis=1, keepdims=True)
    return dx, xdh * r


def decomp_back(dx):
    return dx - dx[:, D - 1 :]


CHAIN = []


def call(body, outs, *args, scratch=(), limit=LIMIT, smem=0, waits=(), free=False):
    wait = CHAIN[-1:] + list(waits)
    specs = [SMEM_SPEC] * smem + [ANY_SPEC if free else VMEM_SPEC] * (len(args) - smem) + [ANY_SPEC] * len(wait)

    def run(*refs):
        body(*refs[: len(args)], *refs[len(args) + len(wait) :])

    results = pl.pallas_call(
        run,
        out_shape=[jax.ShapeDtypeStruct(s, d) for s, d in outs],
        in_specs=specs,
        out_specs=[VMEM_SPEC] * len(outs),
        scratch_shapes=list(scratch),
        compiler_params=pltpu.CompilerParams(vmem_limit_bytes=limit * MIB),
        cost_estimate=pl.CostEstimate(flops=1000, bytes_accessed=1000, transcendentals=0),
    )(*args, *wait)
    CHAIN.append(min(results, key=lambda r: r.size * r.dtype.itemsize))
    return results


def assemble_plain(starts, pieces, out_ref):
    at = 0
    for ref in pieces:
        count, rows, _ = ref.shape
        for m in range(count):
            out_ref[pl.ds(pl.multiple_of(starts[at], rows), rows), :] = ref[m]
            at += 1


def assemble(starts, pieces, out_refs, wide_ref):
    column = 0
    for out_ref in out_refs:
        for begin in range(0, out_ref.shape[1], wide_ref.shape[1]):
            width = min(wide_ref.shape[1], out_ref.shape[1] - begin)
            at = 0
            for ref in pieces:
                count, rows, _ = ref.shape
                for m in range(count):
                    block = ref[m, :, column + begin : column + begin + width].astype(F32)
                    wide_ref[pl.ds(pl.multiple_of(starts[at], rows), rows), :width] = block
                    at += 1
            out_ref[:, begin : begin + width] = wide_ref[:, :width].astype(BF16)
        column += out_ref.shape[1]


def turn(starts, value, out_ref, t_ref, r_ref):
    turned = value.astype(F32).T
    if len(starts) == 1:
        out_ref[...] = turned.astype(BF16)
        return
    t_ref[...] = turned
    rows = turned.shape[0] // len(starts)
    for s, start in enumerate(starts):
        r_ref[rows * s : rows * (s + 1), :] = t_ref[pl.ds(pl.multiple_of(start, rows), rows), :]
    out_ref[...] = r_ref[...].astype(BF16)


def row_loop(total, step, body):
    def go(i, carry):
        body(pl.multiple_of(i * step, step))
        return carry

    lax.fori_loop(0, total // step, go, 0)


def fold8(rows):
    total = rows[0:8]
    for at in range(8, rows.shape[0], 8):
        total = total + rows[at : at + 8]
    return total


def column_of(row, first, count):
    r_at = lax.broadcasted_iota(jnp.int32, (count, row.shape[1]), 0)
    c_at = lax.broadcasted_iota(jnp.int32, (count, row.shape[1]), 1)
    return jnp.sum(jnp.where(c_at == r_at + first, row, 0.0), axis=1, keepdims=True)


def k_pack(w_any, wo_any, ga_any, gm_any, b_any, out_ref, w_ref, wo_ref, ga_ref, gm_ref, b_ref, sems):
    refs = ((w_any, w_ref), (wo_any, wo_ref), (ga_any, ga_ref), (gm_any, gm_ref), (b_any, b_ref))
    copies = [pltpu.make_async_copy(a, b, sems.at[i]) for i, (a, b) in enumerate(refs)]
    for copy in copies:
        copy.start()
    for copy in copies:
        copy.wait()
    rows = w_ref.shape[0]
    for group, start in ((0, 0), (1, 3 * HALF + 128)):
        for part in range(3):
            at = part * D + group * HALF
            out_ref[:, start + part * HALF : start + (part + 1) * HALF] = w_ref[:, at : at + HALF]
    out_ref[:, 6 * HALF + 128 :] = wo_ref[...]
    b = b_ref[...].astype(F32)
    columns = [column_of(ga_ref[...].astype(F32), 0, rows), column_of(gm_ref[...].astype(F32), 0, rows)]
    columns += [column_of(b, k * rows, rows) for k in range(4)]
    lane = lax.broadcasted_iota(jnp.int32, (rows, 128), 1)
    small = jnp.zeros((rows, 128), F32)
    for at, column in enumerate(columns):
        small = jnp.where(lane == at, column, small)
    out_ref[:, 3 * HALF : 3 * HALF + 128] = small.astype(BF16)


def k_stack(n, *refs):
    for at, ref in enumerate(refs[:n]):
        start = 0
        for out_ref in refs[n:]:
            out_ref[at] = ref[:, start : start + out_ref.shape[2]]
            start += out_ref.shape[2]


def k_join(first_ref, second_ref, out_ref):
    half = first_ref.shape[0]
    out_ref[:half] = first_ref[...]
    out_ref[half:] = second_ref[...]


def k_qkv(plan, me, resid_ref, spread_ref, pick_ref, *refs):
    n = plan.pieces
    pieces, (qkv_ref, w_ref, h_ref, gains_ref, bias_ref), (tail_ref, wide) = refs[:n], refs[n : n + 5], refs[n + 5 :]
    tokens = resid_ref.shape[0]
    assemble(plan.starts(me[0], plan.LATE, D), pieces, (w_ref, tail_ref), wide)
    tail = tail_ref[...].astype(F32).T
    gains_ref[...] = tail[:8, :]
    gain = tail[0:1, :]
    small = tail[:8, :].astype(BF16)
    both = dot_nn(jnp.concatenate([small[:, : D // 2], small[:, D // 2 :]], axis=0), spread_ref[...])
    for part in range(2):
        picked = both[8 * part : 8 * part + 8] * pick_ref[...]
        bias_ref[:, part * (FF // 2) : (part + 1) * (FF // 2)] = jnp.sum(picked, axis=0, keepdims=True)

    def norm(at):
        rows = pl.ds(at, STEP)
        x1 = decomp(resid_ref[rows, :].astype(F32))
        h_ref[rows, :] = (x1 * inv_rms(x1) * gain).astype(BF16)

    row_loop(tokens, STEP, norm)
    qkv_ref[...] = dot_nn(h_ref[...], w_ref[...]).astype(BF16)


def attend(qkv_ref, attn_ref, tokens, out_at):
    i_at = lax.broadcasted_iota(jnp.int32, (SEQ, SEQ), 0)
    j_at = lax.broadcasted_iota(jnp.int32, (SEQ, SEQ), 1)
    allowed = j_at <= i_at
    low = lax.broadcasted_iota(jnp.int32, (SEQ, 128), 1) < HD

    def one(seq):
        rows = pl.ds(seq, SEQ)
        for pair in range(HALF // 128):
            cols = slice(128 * pair, 128 * (pair + 1))
            q2 = qkv_ref[rows, cols]
            k2 = qkv_ref[rows, HALF + 128 * pair : HALF + 128 * (pair + 1)]
            v2 = qkv_ref[rows, 2 * HALF + 128 * pair : 2 * HALF + 128 * (pair + 1)]
            mixed = None
            for side in range(2):
                mine = low if side == 0 else jnp.logical_not(low)
                k_one = jnp.where(mine, k2, jnp.zeros_like(k2))
                v_one = jnp.where(mine, v2, jnp.zeros_like(v2))
                scores = jnp.where(allowed, dot_nt(q2, k_one) * (HD ** -0.5), -1e30)
                top = jnp.max(scores, axis=1, keepdims=True)
                powers = jnp.exp(scores - top)
                total = jnp.sum(powers, axis=1, keepdims=True)
                probs = (powers * (1.0 / total)).astype(BF16)
                part = dot_nn(probs, v_one)
                mixed = part if mixed is None else mixed + part
            attn_ref[rows, out_at + 128 * pair : out_at + 128 * (pair + 1)] = mixed.astype(BF16)

    row_loop(tokens, SEQ, one)


def k_attn(plan, me, qkv_ref, h_ref, attn_ref, ht_ref, t_ref, r_ref):
    attend(qkv_ref, attn_ref, qkv_ref.shape[0], 0)
    turn(plan.starts(me[0], plan.SUM, D), h_ref[...], ht_ref, t_ref, r_ref)


def k_second(plan, me, resid_ref, h_ref, attn0_ref, gains_ref, *refs):
    n = plan.pieces
    pieces, (qkv_ref, w_ref, wo_ref, attnt_ref, x2_ref, h2_ref, h2t_ref), (wide, attn_ref, t_ref, r_ref) = (
        refs[:n],
        refs[n : n + 7],
        refs[n + 7 :],
    )
    tokens = resid_ref.shape[0]
    assemble(plan.starts(me[0], plan.LATE, D), pieces, (w_ref, wo_ref), wide)
    qkv_ref[...] = dot_nn(h_ref[...], w_ref[...]).astype(BF16)
    attn_ref[:, :HALF] = attn0_ref[...]
    attend(qkv_ref, attn_ref, tokens, HALF)
    gain = gains_ref[1:2, :]
    x2_ref[...] = dot_nn(attn_ref[...], wo_ref[...])

    def norm(at):
        rows = pl.ds(at, STEP)
        y = x2_ref[rows, :]
        middle = resid_ref[rows, :].astype(F32) + (y - jnp.mean(y, axis=1, keepdims=True))
        x2 = decomp(jnp.where(last_lane(middle.shape), 0.0, middle))
        x2_ref[rows, :] = x2
        h2_ref[rows, :] = (x2 * inv_rms(x2) * gain).astype(BF16)

    row_loop(tokens, STEP, norm)
    turn(plan.starts(me[0], plan.SUM, D), attn_ref[...], attnt_ref, t_ref, r_ref)
    turn(plan.starts(me[0], plan.SUM, D), h2_ref[...], h2t_ref, t_ref, r_ref)


GELU_A = math.sqrt(2.0 / math.pi)
GELU_B = 0.044715


def k_up(plan, me, h2_ref, bias_ref, *refs):
    n = plan.pieces
    pieces, (w_ref, act_ref, actt_ref, slope_ref), (u_ref, wide_ref) = refs[:n], refs[n : n + 4], refs[n + 4 :]
    tokens = h2_ref.shape[0]
    assemble(plan.starts(me[0], plan.EARLY, D), pieces, (w_ref,), wide_ref)
    wide = D
    blocks = FF // plan.count if plan.fine else wide
    for tile in range(FF // wide):
        cols = slice(tile * wide, (tile + 1) * wide)
        u_ref[...] = dot_nn(h2_ref[...], w_ref[:, cols])
        bias = bias_ref[:, cols]

        def gelu(at):
            rows = pl.ds(at, 64)
            u = u_ref[rows, :] + bias
            square = u * u
            t = jnp.tanh(u * (GELU_A + (GELU_A * GELU_B) * square))
            half = 0.5 * t + 0.5
            act_ref[rows, cols] = (u * half).astype(BF16)
            slope = half + (u * (0.5 - 0.5 * (t * t))) * (GELU_A + (3.0 * GELU_A * GELU_B) * square)
            slope_ref[rows, cols] = slope

        row_loop(tokens, 64, gelu)
        turned = act_ref[:, cols].T
        for b in range(wide // blocks):
            q = tile * wide // blocks + b
            to = pl.multiple_of(plan.slot(me[0], plan.SUM_DOWN, q) * blocks, blocks) if plan.fine else q * blocks
            actt_ref[pl.ds(to, blocks), :] = turned[b * blocks : (b + 1) * blocks, :]


def place_of(refs, at):
    for ref in refs:
        if at < ref.shape[0]:
            return ref, at
        at -= ref.shape[0]


def split_dot(left_ref, right_ref, keep_ref, *send_refs):
    half = left_ref.shape[0] // 2
    width = right_ref.shape[1]
    _, rows, _ = keep_ref.shape
    for refs, start in ((send_refs, half), ((keep_ref,), 0)):
        for at in range(0, half, 384):
            part = dot_nn(left_ref[start + at : start + at + 384, :], right_ref[...]).astype(BF16)
            if rows > 384:
                refs[0][0, at : at + 384, :width] = part
                continue
            for j in range(384 // rows):
                ref, place = place_of(refs, at // rows + j)
                ref[place, :, :width] = part[j * rows : (j + 1) * rows]


def k_prep(rows, resid_in, cot_in, resid_ref, cot_ref, dz_ref, spread_ref, pick_ref):
    for ref, source in ((resid_ref, resid_in), (cot_ref, cot_in)):
        ref[:, D - 128 :] = jnp.zeros((ref.shape[0], 128), BF16)
        ref[:, : D - 1] = source[...]

    def go(at):
        at_rows = pl.ds(at, STEP)
        c = cot_ref[at_rows, :].astype(F32)
        dz_ref[at_rows, :] = (c - jnp.mean(c, axis=1, keepdims=True)).astype(BF16)

    row_loop(cot_ref.shape[0], STEP, go)
    half, full = spread_ref.shape
    column = lax.broadcasted_iota(jnp.int32, (half, 1), 0)
    device = jnp.zeros((half, 1), jnp.int32)
    for j in range(1, half // rows):
        device = device + jnp.where(column >= j * rows, 1, 0)
    first = column + 3 * rows * device
    width = 384
    for at in range(0, full, width):
        f = lax.broadcasted_iota(jnp.int32, (half, width), 1) + at
        hit = f == first
        for k in range(1, 4):
            hit = jnp.logical_or(hit, f == first + k * rows)
        spread_ref[:, at : at + width] = jnp.where(hit, 1.0, 0.0).astype(BF16)
    f = lax.broadcasted_iota(jnp.int32, (1, full), 1)
    group = jnp.zeros((1, full), jnp.int32)
    for j in range(1, full // rows):
        group = group + jnp.where(f >= j * rows, 1, 0)
    row = lax.broadcasted_iota(jnp.int32, (8, full), 0)
    pick_ref[...] = jnp.where((group & 3) + 2 == row, 1.0, 0.0)


def k_du(plan, me, dz_ref, slope_ref, *refs):
    n = plan.pieces
    pieces, (du_ref, gb_ref, w_ref), (z_ref,) = refs[:n], refs[n : n + 3], refs[n + 3 :]
    tokens = dz_ref.shape[0]
    assemble_plain(plan.starts(me[0], plan.EARLY, FF), pieces, w_ref)
    wide = D
    for tile in range(FF // wide):
        cols = slice(tile * wide, (tile + 1) * wide)
        z_ref[...] = dot_nt(dz_ref[...], w_ref[cols, :])

        def go(i, total):
            rows = pl.ds(pl.multiple_of(i * 64, 64), 64)
            du = (z_ref[rows, :] * slope_ref[rows, cols]).astype(BF16)
            du_ref[rows, cols] = du
            return total + fold8(du.astype(F32))

        total = lax.fori_loop(0, tokens // 64, go, jnp.zeros((8, wide), F32))
        gb_ref[:, cols] = jnp.sum(total, axis=0, keepdims=True)


def k_result(x2_ref, act_ref, w_ref, out_ref, z_ref):
    z_ref[...] = dot_nn(act_ref[...], w_ref[...])

    def result(at):
        rows = pl.ds(at, STEP)
        z = z_ref[rows, :]
        out = (x2_ref[rows, :] + (z - jnp.mean(z, axis=1, keepdims=True))).astype(BF16)
        out_ref[rows, :] = out[:, : D - 1]

    row_loop(act_ref.shape[0], STEP, result)


def k_mid(cot_ref, x2_ref, gains_ref, du_ref, w_up_ref, attnt_ref, dmid_ref, dy_ref, gg_ref, keep_ref, send_ref, dh_ref):
    tokens = cot_ref.shape[0]
    dh_ref[...] = dot_nt(du_ref[...], w_up_ref[...])
    gain = gains_ref[1:2, :]

    def back(i, total):
        rows = pl.ds(pl.multiple_of(i * STEP, STEP), STEP)
        x2 = x2_ref[rows, :]
        dx, summand = norm_back(x2, inv_rms(x2), gain, dh_ref[rows, :])
        dmid = cot_ref[rows, :].astype(F32) + decomp_back(dx)
        dmid_ref[rows, :] = dmid
        dy_ref[rows, :] = (dmid - jnp.mean(dmid, axis=1, keepdims=True)).astype(BF16)
        return total + fold8(summand)

    total = lax.fori_loop(0, tokens // STEP, back, jnp.zeros((8, D), F32))
    gg_ref[...] = jnp.sum(total, axis=0, keepdims=True)
    split_dot(attnt_ref, dy_ref, keep_ref, send_ref)


def k_attn_back(group, dy_ref, wo_ref, qkv_ref, ht_ref, *refs):
    *refs, da_ref = refs
    if group == 1:
        keep_o, send_o, *refs = refs
    dqkv_ref, keep_ref, *send_refs = refs
    if group == 1:
        keep_ref[:, :, 3 * HALF :] = keep_o[...]
        at = 0
        for ref in send_refs:
            ref[:, :, 3 * HALF :] = send_o[at : at + ref.shape[0]]
            at += ref.shape[0]
    tokens = dy_ref.shape[0]
    da_ref[...] = dot_nt(dy_ref[...], wo_ref[HALF * group : HALF * (group + 1), :]).astype(BF16)
    j_at = lax.broadcasted_iota(jnp.int32, (SEQ, SEQ), 0)
    i_at = lax.broadcasted_iota(jnp.int32, (SEQ, SEQ), 1)
    allowed = j_at <= i_at
    low = lax.broadcasted_iota(jnp.int32, (SEQ, 128), 1) < HD
    scale = HD ** -0.5

    def one(seq):
        rows = pl.ds(seq, SEQ)
        for pair in range(HALF // 128):
            cols = [slice(HALF * part + 128 * pair, HALF * part + 128 * (pair + 1)) for part in range(3)]
            q2, k2, v2 = (qkv_ref[rows, c] for c in cols)
            d2 = da_ref[rows, cols[0]]
            dq = dk = dv = None
            for side in range(2):
                mine = low if side == 0 else jnp.logical_not(low)
                q1, k1, v1, d1 = (jnp.where(mine, a, jnp.zeros_like(a)) for a in (q2, k2, v2, d2))
                scores = jnp.where(allowed, dot_nt(k1, q2) * scale, -1e30)
                top = jnp.max(scores, axis=0, keepdims=True)
                powers = jnp.exp(scores - top)
                probs = powers * (1.0 / jnp.sum(powers, axis=0, keepdims=True))
                dp = dot_nt(v1, d2)
                inner = jnp.sum(probs * dp, axis=0, keepdims=True)
                ds = (probs * (dp - inner)).astype(BF16)
                parts = (dot_tn(ds, k1), dot_nn(ds, q1), dot_nn(probs.astype(BF16), d1))
                dq, dk, dv = parts if dq is None else (dq + parts[0], dk + parts[1], dv + parts[2])
            dqkv_ref[rows, cols[0]] = (dq * scale).astype(BF16)
            dqkv_ref[rows, cols[1]] = (dk * scale).astype(BF16)
            dqkv_ref[rows, cols[2]] = dv.astype(BF16)

    row_loop(tokens, SEQ, one)
    split_dot(ht_ref, dqkv_ref, keep_ref, *send_refs)


def k_last(plan, me, resid_ref, dmid_ref, gains_ref, dq0_ref, w0_ref, dq1_ref, w1_ref, gg_ref, gb_ref, spread_ref, pick_ref, out_ref, keep_ref, send_ref, dh_ref, tail_ref):
    tokens = resid_ref.shape[0]
    dh_ref[...] = dot_nt(dq0_ref[...], w0_ref[...]) + dot_nt(dq1_ref[...], w1_ref[...])
    gain = gains_ref[0:1, :]

    def back(i, total):
        rows = pl.ds(pl.multiple_of(i * STEP, STEP), STEP)
        x1 = decomp(resid_ref[rows, :].astype(F32))
        dx, summand = norm_back(x1, inv_rms(x1), gain, dh_ref[rows, :])
        out_ref[rows, :] = (dmid_ref[rows, :] + decomp_back(dx))[:, : D - 1]
        return total + fold8(summand)

    total = lax.fori_loop(0, tokens // STEP, back, jnp.zeros((8, D), F32))
    ga = jnp.sum(total, axis=0, keepdims=True)
    g = jnp.concatenate([gb_ref[:, : FF // 2] * pick_ref[...], gb_ref[:, FF // 2 :] * pick_ref[...]], axis=0)
    high = g.astype(BF16)
    lower = (g - high.astype(F32)).astype(BF16)
    both = dot_nt(jnp.concatenate([high, lower], axis=0), spread_ref[...])
    biases = jnp.concatenate([both[:8] + both[16:24], both[8:16] + both[24:]], axis=1)
    row = lax.broadcasted_iota(jnp.int32, (8, D), 0)
    rows8 = jnp.where(row == 0, ga, jnp.where(row == 1, gg_ref[...], biases))
    high = rows8.astype(BF16).astype(F32)
    both = jnp.concatenate([high, rows8 - high, jnp.zeros((112, D), F32)], axis=0)
    tail_ref[...] = both.T
    starts = plan.starts(me[0], plan.SUM, D)
    if len(starts) == 1:
        keep_ref[0] = tail_ref[: D // 2, :].astype(BF16)
        send_ref[0] = tail_ref[D // 2 :, :].astype(BF16)
    else:
        half = len(starts) // 2
        rows = D // len(starts)
        for s, start in enumerate(starts):
            ref, at = (keep_ref, s) if s < half else (send_ref, s - half)
            ref[at] = tail_ref[pl.ds(pl.multiple_of(start, rows), rows), :].astype(BF16)


def renew(value):
    lane = lax.broadcasted_iota(jnp.int32, value.shape, 1)
    total = value + pltpu.roll(value, 120, 1)
    high = total.astype(BF16).astype(F32)
    lower = pltpu.roll(total - high, 8, 1)
    return jnp.where(lane < 8, high, jnp.where(lane < 16, lower, 0.0))


def add_blocks(tail, a, b):
    value = a.astype(F32) + b.astype(F32)
    if not tail:
        return value
    return jnp.concatenate([value[:, :-128], renew(value[:, -128:])], axis=1)


def k_sum_half(tail, keep_ref, *refs):
    *got, mine_ref, yours_ref = refs
    half = mine_ref.shape[0]
    for s in range(half):
        for ref, at in ((yours_ref, half + s), (mine_ref, s)):
            other, place = place_of(got, at)
            ref[s] = add_blocks(tail, keep_ref[at], other[place]).astype(BF16)


def k_sum_small(keep_ref, keep_t, got_t, *refs):
    *got, mine_ref, yours_ref = refs
    half = mine_ref.shape[0]
    width = keep_ref.shape[2]
    for s in range(2 * half):
        ref, at = (mine_ref, s) if s < half else (yours_ref, s - half)
        other, place = place_of(got, s)
        ref[at, :, :width] = add_blocks(False, keep_ref[s], other[place]).astype(BF16)
        ref[at, :, width:] = renew(add_blocks(False, keep_t[s], got_t[s])).astype(BF16)


def k_sum_four(keep_b, got_b, keep_a, got_a, own, one, two, three):
    width = keep_b.shape[2]
    for m, ref in enumerate((own, one, two, three)):
        ref[:, :width] = add_blocks(False, keep_b[m], got_b[m]).astype(ref.dtype)
        ref[:, width:] = add_blocks(True, keep_a[m], got_a[m]).astype(ref.dtype)


def bits_of(count):
    return count.bit_length() - 1


SWAP = {"m1": "m2", "m2": "m1", "z1": "z2", "z2": "z1", "zl": "zl", "zh": "zh"}


class Plan:
    LATE = ("zl", "zh", "m1", "m2")
    EARLY = ("m1", "z1", "z2", "m2")
    SUM = ("z1", "z2", "m2", "m1")
    SUM_DOWN = ("m2", "z1", "z2", "m1")

    def __init__(self, mesh):
        self.wide, self.narrow = mesh.shape["wide"], mesh.shape["narrow"]
        self.count = self.wide * self.narrow
        self.low = bits_of(self.narrow)
        self.bits = bits_of(self.count)
        self.core = self.low
        outer = list(range(self.low + 1, self.bits))
        self.ys = list(range(self.low))
        self.x_bit, self.z_bits = outer[0], outer[1:]
        self.cm, self.xm, self.ym = 1 << self.core, 1 << self.x_bit, 1
        self.zl, self.zh = (1 << b for b in self.z_bits[:2])
        self.fine = (D // self.count) % 8 == 0 and self.low == 1 and len(self.z_bits) == 2
        self.pieces = 4 if self.fine else 1

    def index(self):
        return lax.axis_index("wide") * self.narrow + lax.axis_index("narrow")

    def send(self, value, mask, other=None):
        masks = [mask, mask if other is None else other]
        return lax.ppermute(value, AXES, [(i, i ^ masks[(i >> self.core) & 1]) for i in range(self.count)])

    def both(self, name):
        low = {"m1": self.xm, "m2": self.ym, "z1": self.zl, "z2": self.zh, "zl": self.zl, "zh": self.zh}
        return low[name], low[SWAP[name]]

    def exchange(self, name):
        return lambda value: self.send(value, *self.both(name))

    def mask(self, me, name):
        first, second = self.both(name)
        return first if first == second else jnp.where(((me >> self.core) & 1) == 0, first, second)

    def starts(self, me, bits, total):
        if not self.fine:
            return [0]
        masks = []
        for names, extra in ((bits, 0), ([SWAP[b] for b in bits], self.cm)):
            ways = [self.mask(me, name) for name in names]
            for block in range(1 << len(bits)):
                whole = extra
                for k, way in enumerate(ways):
                    if (block >> k) & 1:
                        whole = whole | way
                masks.append(whole)
        return [(me ^ m) * (total // self.count) for m in masks]

    def slot(self, me, bits, device):
        diff = me ^ device
        other = (diff & self.cm) != 0
        at = jnp.where(other, 1 << len(bits), 0)
        for k, name in enumerate(bits):
            way = jnp.where(other, self.mask(me, SWAP[name]), self.mask(me, name))
            at = at + jnp.where((diff & way) != 0, 1 << k, 0)
        return at

    def pair_up(self, own, other, bit, axis):
        mine = (self.index() >> bit) & 1
        return jnp.where(mine == 1, jnp.stack([other, own], axis), jnp.stack([own, other], axis))

    def gather_plain(self, shard):
        value, held = shard, []
        for b in self.z_bits + [self.x_bit] + self.ys + [self.core]:
            axis = sum(1 for h in held if h > b)
            value = self.pair_up(value, self.send(value, 1 << b), b, axis)
            held.append(b)
        return value.reshape(1, -1, shard.shape[1])

    def scatter_plain(self, keep, send, add):
        me = self.index()
        blocks = jnp.concatenate([keep[0], send[0]], 0)
        value = blocks.reshape((2,) * self.bits + (-1, blocks.shape[1]))
        held = list(range(self.bits - 1, -1, -1))
        for b in [self.core] + self.ys + [self.x_bit] + self.z_bits:
            axis, bit = held.index(b), (me >> b) & 1
            mine = lax.dynamic_index_in_dim(value, bit, axis, keepdims=False)
            yours = lax.dynamic_index_in_dim(value, 1 - bit, axis, keepdims=False)
            held.remove(b)
            value = add([mine, self.send(yours, 1 << b)], not held)
        return value


class Gather:
    def __init__(self, plan):
        self.plan, self.fine = plan, plan.fine

    def begin(self, blocks, name):
        if self.fine:
            self.a = blocks if blocks.ndim == 3 else blocks.reshape((1,) + blocks.shape)
            self.got = self.plan.exchange(name)(self.a)
        else:
            self.got = self.plan.gather_plain(blocks) if blocks.ndim == 2 else blocks

    def grow(self, name, waits=()):
        if self.fine:
            count, rows, columns = self.a.shape
            (self.a,) = call(k_join, [((2 * count, rows, columns), BF16)], self.a, self.got, waits=waits)
            self.got = self.plan.exchange(name)(self.a)

    def to_core(self):
        self.near = [self.plan.send(fence(self.a, CHAIN[-1])[0], self.plan.cm)] if self.fine else []

    def finish(self):
        if self.fine:
            return [self.a, self.got, *self.near, self.plan.send(self.got, self.plan.cm)]
        return [self.got]


def stack(plan, shard, got, widths, waits):
    if not plan.fine:
        cuts = [sum(widths[:i]) for i in range(len(widths) + 1)]
        return [got[:, :, i:j] for i, j in zip(cuts, cuts[1:])]
    return call(functools.partial(k_stack, 4), [((4, shard.shape[0], w), BF16) for w in widths], shard, *got, waits=waits)


class Scatter:
    def __init__(self, plan, keep, *sends):
        self.plan, self.fine, self.keep = plan, plan.fine, keep
        self.small = False
        if plan.fine:
            self.got = [plan.send(part, plan.cm) for part in sends]
        else:
            self.got = [plan.scatter_plain(keep, sends[0], add_plain)]

    def add_small(self, keep, send):
        if self.fine:
            self.small_parts = [keep, self.plan.send(send, self.plan.cm)]
        else:
            self.got.append(self.plan.scatter_plain(keep, send, add_two))

    def halve(self, name, waits=()):
        if not self.fine:
            return
        count, rows, columns = self.keep.shape
        if not self.small and hasattr(self, "small_parts"):
            self.small = True
            body, columns = k_sum_small, columns + 128
            args = [self.keep, *self.small_parts, *self.got]
        else:
            body = functools.partial(k_sum_half, self.small)
            args = [self.keep, *self.got]
        self.keep, yours = call(body, [((count // 2, rows, columns), BF16)] * 2, *args, waits=waits)
        self.got = [self.plan.exchange(name)(yours)]

    def total(self):
        if not self.fine:
            return self.got[0]
        return self.keep[0].astype(F32) + self.got[0][0].astype(F32)


def finish_late(plan, sb, sa, rows):
    if not plan.fine:
        return sb.got[0], sa.got[0], sa.got[1]
    width = sb.keep.shape[2]
    whole = width + sa.keep.shape[2]
    own, *others = call(
        k_sum_four, [((rows, whole), F32)] + [((rows, whole), BF16)] * 3, sb.keep, sb.got[0], sa.keep, sa.got[0]
    )
    got = [plan.exchange("z1")(others[0]), plan.exchange("z2")(others[1]), plan.send(others[2], plan.zl | plan.zh)]
    total = own
    for part in got:
        total = total + part.astype(F32)
    return total[:, :width], total[:, width:-128], total[:, -128:-120] + total[:, -120:-112]


def add_plain(arrived, last):
    total = arrived[0].astype(F32)
    for part in arrived[1:]:
        total = total + part.astype(F32)
    return total if last else total.astype(BF16)


def add_two(arrived, last):
    total = 0.0
    for part in arrived:
        whole = part.astype(F32)
        total = total + (whole[..., :8] + whole[..., 8:16])
    if last:
        return total
    high = lax.reduce_precision(total, 8, 7)
    rest = jnp.zeros(total.shape[:-1] + (112,), F32)
    return jnp.concatenate([high, total - high, rest], axis=-1).astype(BF16)


def fence(*values):
    return lax.optimization_barrier(values)


def device_step(plan, resid_in, w_qkv, w_out, w_up, b_up, w_down, gain_attn, gain_mlp, cotangent):
    rows = w_qkv.shape[0]
    t, d, half = resid_in.shape[0], D, D // 2
    wide3 = 3 * HALF
    CHAIN.clear()
    first = wide3 + 128
    fine = plan.fine
    me = plan.index().reshape(1)
    bind = lambda body: functools.partial(body, plan)
    turned = [pltpu.VMEM((d, t), F32)] * 2

    def blocks(r, columns, *pieces):
        if not fine:
            return [((1, half * r // rows, columns), BF16)] * 2
        return [((count, r, columns), BF16) for count in (16, *(pieces or (16,)))]

    a, b, u, v = (Gather(plan) for _ in range(4))
    u.begin(w_up, "m1")
    v.begin(w_down, "m1")
    (shard,) = call(
        k_pack, [((rows, first + wide3 + d), BF16)],
        w_qkv, w_out, gain_attn.reshape(1, rows), gain_mlp.reshape(1, rows), b_up.reshape(1, 4 * rows), free=True,
        scratch=[pltpu.VMEM(shape, BF16) for shape in ((rows, 3 * d), (rows, d), (1, rows), (1, rows), (1, 4 * rows))]
        + [pltpu.SemaphoreType.DMA((5,))],
    )
    got = [plan.send(shard, m) for m in (plan.zl, plan.zh, plan.zl | plan.zh)] if fine else plan.gather_plain(shard)
    resid, cot, dz, spread, pick = call(
        functools.partial(k_prep, rows),
        [((t, d), BF16), ((t, d), BF16), ((t, d), BF16), ((half, 4 * half), BF16), ((8, 4 * half), F32)],
        resid_in, cotangent,
    )
    four_a, four_b = stack(plan, shard, got, (first, wide3 + d), [u.got, v.got])
    a.begin(four_a, "m1")
    b.begin(four_b, "m1")
    u.grow("z1")
    v.grow("z1")
    a.grow("m2", [b.got, u.got, v.got])
    b.grow("m2")
    u.grow("z2")
    a.to_core()
    b.to_core()
    u.grow("m2", [a.got, b.got, *a.near, *b.near])
    v.grow("z2")
    a_pieces, b_pieces = a.finish(), b.finish()
    qkv0, w0, h1, gains, bias = call(
        bind(k_qkv),
        [((t, wide3), BF16), ((d, wide3), BF16), ((t, d), BF16), ((8, d), F32), ((1, FF), F32)],
        me, resid, spread, pick, *a_pieces,
        scratch=[pltpu.VMEM((d, 128), BF16), pltpu.VMEM((d, half), F32)], smem=1, waits=b_pieces[-1:],
    )
    attn0, h1t = call(bind(k_attn), [((t, HALF), BF16), ((d, t), BF16)], me, qkv0, h1, scratch=turned, smem=1)
    qkv1, w1, wo, attnt, x2, h2, h2t = call(
        bind(k_second),
        [((t, wide3), BF16), ((d, wide3), BF16), ((d, d), BF16), ((d, t), BF16), ((t, d), F32), ((t, d), BF16), ((d, t), BF16)],
        me, resid, h1, attn0, gains, *b_pieces,
        scratch=[pltpu.VMEM((d, half), F32), pltpu.VMEM((t, d), BF16)] + turned, smem=1,
    )
    v.grow("m2", [u.got])
    u.to_core()
    v.to_core()
    wu, act, actt, slope = call(
        bind(k_up),
        [((d, FF), BF16), ((t, FF), BF16), ((FF, t), BF16), ((t, FF), F32)],
        me, h2, bias, *u.finish(),
        scratch=[pltpu.VMEM((t, d), F32), pltpu.VMEM((d, half), F32)], smem=1,
    )
    sv = Scatter(plan, *call(split_dot, blocks(4 * rows, d, 4, 4, 4, 4), actt, dz, waits=v.near))
    sv.halve("m1")
    du, gb, w_down_all = call(
        bind(k_du),
        [((t, FF), BF16), ((1, FF), F32), ((FF, d), BF16)],
        me, dz, slope, *v.finish(), scratch=[pltpu.VMEM((t, d), F32)], smem=1,
    )
    su = Scatter(plan, *call(split_dot, blocks(rows, FF, 4, 4, 4, 4), h2t, du))
    dmid, dy, gg, keep_o, send_o = call(
        k_mid,
        [((t, d), F32), ((t, d), BF16), ((1, d), F32)] + blocks(rows, d),
        cot, x2, gains, du, wu, attnt,
        scratch=[pltpu.VMEM((t, d), F32)],
    )
    sv.halve("z2")
    su.halve("m1")
    back_scratch = [pltpu.VMEM((t, HALF), BF16)]
    dqkv1, *parts = call(
        functools.partial(k_attn_back, 1), [((t, wide3), BF16)] + blocks(rows, wide3 + d, 6, 5, 5),
        dy, wo, qkv1, h1t, keep_o, send_o, scratch=back_scratch,
    )
    sb = Scatter(plan, *parts)
    dqkv0, *parts = call(
        functools.partial(k_attn_back, 0), [((t, wide3), BF16)] + blocks(rows, wide3, 8, 8),
        dy, wo, qkv0, h1t, scratch=back_scratch,
    )
    sa = Scatter(plan, *parts)
    sb.halve("m1")
    dres, *parts = call(
        bind(k_last),
        [((t, d - 1), F32)] + blocks(rows, 128),
        me, resid, dmid, gains, dqkv0, w0, dqkv1, w1, gg, gb, spread, pick,
        scratch=[pltpu.VMEM((t, d), F32), pltpu.VMEM((d, 128), F32)], smem=1,
    )
    sa.add_small(*parts)
    sv.halve("z1")
    su.halve("m2")
    sa.halve("m1")
    (out,) = call(k_result, [((t, d - 1), BF16)], x2, act, w_down_all, scratch=[pltpu.VMEM((t, d), F32)])
    sb.halve("m2")
    sv.halve("m2")
    su.halve("z2")
    sa.halve("m2")
    s_second, s_first, s_tail = finish_late(plan, sb, sa, rows)
    su.halve("z1")
    s_down, s_up = sv.total(), su.total()
    s_qkv = jnp.concatenate(
        [piece for part in range(3) for piece in (s_first[:, part * HALF : (part + 1) * HALF], s_second[:, part * HALF : (part + 1) * HALF])],
        axis=1,
    )
    return (out, dres, s_qkv, s_second[:, wide3:], s_up, s_tail[:, 2:6].T.reshape(4 * rows), s_down, s_tail[:, 0], s_tail[:, 1])


def solution(mesh):
    rows2, rows1 = P(AXES, None), P(AXES)
    in_specs = (rows2, rows2, rows2, rows2, rows1, rows2, rows1, rows1, rows2)
    out_specs = (rows2, rows2, rows2, rows2, rows2, rows1, rows2, rows1, rows1)
    plan = Plan(mesh)

    def on_device(*arrays):
        return device_step(plan, *arrays)

    return jax.shard_map(on_device, mesh=mesh, in_specs=in_specs, out_specs=out_specs, check_vma=False)
```

```python
import functools
import math

import jax
import jax.numpy as jnp
from jax import lax
from jax.experimental import pallas as pl
from jax.experimental.pallas import tpu as pltpu
from jax.sharding import PartitionSpec as P

D = 768
H = 12
HD = 64
FF = 3072
SEQ = 256
HALF = 384
EPS = 1e-05
AXES = ("wide", "narrow")
F32 = jnp.float32
BF16 = jnp.bfloat16
MIB = 1 << 20
LIMIT = 12

VMEM_SPEC = pl.BlockSpec(memory_space=pltpu.VMEM)
SMEM_SPEC = pl.BlockSpec(memory_space=pltpu.SMEM)
ANY_SPEC = pl.BlockSpec(memory_space=pl.ANY)


def dot_nn(a, b):
    return lax.dot_general(a, b, (((1,), (0,)), ((), ())), preferred_element_type=F32)


def dot_nt(a, b):
    return lax.dot_general(a, b, (((1,), (1,)), ((), ())), preferred_element_type=F32)


def dot_tn(a, b):
    return lax.dot_general(a, b, (((0,), (0,)), ((), ())), preferred_element_type=F32)


STEP = 128


def last_lane(shape):
    return lax.broadcasted_iota(jnp.int32, shape, 1) == D - 1


def decomp(padded):
    total = jnp.sum(padded, axis=1, keepdims=True)
    return jnp.where(last_lane(padded.shape), -total, padded)


def inv_rms(values):
    return lax.rsqrt(jnp.mean(values * values, axis=1, keepdims=True) + EPS)


def norm_back(x, r, gain, dh):
    xdh = x * dh
    dx = r * (gain * dh) - x * (r * r * r) * jnp.mean(xdh * gain, axis=1, keepdims=True)
    return dx, xdh * r


def decomp_back(dx):
    return dx - dx[:, D - 1 :]


KEEP = []
CHAIN = []


def call(body, outs, *args, scratch=(), limit=LIMIT, smem=0, waits=(), free=False):
    wait = CHAIN[-1:] + list(waits)
    wait += [k for k in KEEP if not any(k is x for x in (*args, *wait))]
    specs = [SMEM_SPEC] * smem + [ANY_SPEC if free else VMEM_SPEC] * (len(args) - smem) + [ANY_SPEC] * len(wait)

    def run(*refs):
        body(*refs[: len(args)], *refs[len(args) + len(wait) :])

    results = pl.pallas_call(
        run,
        out_shape=[jax.ShapeDtypeStruct(s, d) for s, d in outs],
        in_specs=specs,
        out_specs=[VMEM_SPEC] * len(outs),
        scratch_shapes=list(scratch),
        compiler_params=pltpu.CompilerParams(vmem_limit_bytes=limit * MIB),
        cost_estimate=pl.CostEstimate(flops=1000, bytes_accessed=1000, transcendentals=0),
    )(*args, *wait)
    CHAIN.append(min(results, key=lambda r: r.size * r.dtype.itemsize))
    return results


def assemble_plain(starts, pieces, out_ref):
    at = 0
    for ref in pieces:
        count, rows, _ = ref.shape
        for m in range(count):
            out_ref[pl.ds(pl.multiple_of(starts[at], rows), rows), :] = ref[m]
            at += 1


def assemble(starts, pieces, out_refs, wide_ref):
    column = 0
    for out_ref in out_refs:
        for begin in range(0, out_ref.shape[1], wide_ref.shape[1]):
            width = min(wide_ref.shape[1], out_ref.shape[1] - begin)
            at = 0
            for ref in pieces:
                count, rows, _ = ref.shape
                for m in range(count):
                    block = ref[m, :, column + begin : column + begin + width].astype(F32)
                    wide_ref[pl.ds(pl.multiple_of(starts[at], rows), rows), :width] = block
                    at += 1
            out_ref[:, begin : begin + width] = wide_ref[:, :width].astype(BF16)
        column += out_ref.shape[1]


def turn(starts, value, out_ref, t_ref, r_ref):
    turned = value.astype(F32).T
    if len(starts) == 1:
        out_ref[...] = turned.astype(BF16)
        return
    t_ref[...] = turned
    rows = turned.shape[0] // len(starts)
    for s, start in enumerate(starts):
        r_ref[rows * s : rows * (s + 1), :] = t_ref[pl.ds(pl.multiple_of(start, rows), rows), :]
    out_ref[...] = r_ref[...].astype(BF16)


def row_loop(total, step, body):
    def go(i, carry):
        body(pl.multiple_of(i * step, step))
        return carry

    lax.fori_loop(0, total // step, go, 0)


def fold8(rows):
    total = rows[0:8]
    for at in range(8, rows.shape[0], 8):
        total = total + rows[at : at + 8]
    return total


def column_of(row, first, count):
    r_at = lax.broadcasted_iota(jnp.int32, (count, row.shape[1]), 0)
    c_at = lax.broadcasted_iota(jnp.int32, (count, row.shape[1]), 1)
    return jnp.sum(jnp.where(c_at == r_at + first, row, 0.0), axis=1, keepdims=True)


def k_pack(w_any, wo_any, small_any, out_ref, w_ref, wo_ref, small_ref, sems):
    refs = ((w_any, w_ref), (wo_any, wo_ref), (small_any, small_ref))
    copies = [pltpu.make_async_copy(a, b, sems.at[i]) for i, (a, b) in enumerate(refs)]
    for copy in copies:
        copy.start()
    for copy in copies:
        copy.wait()
    rows = w_ref.shape[0]
    for group, start in ((0, 0), (1, 3 * HALF + 128)):
        for part in range(3):
            at = part * D + group * HALF
            out_ref[:, start + part * HALF : start + (part + 1) * HALF] = w_ref[:, at : at + HALF]
    out_ref[:, 6 * HALF + 128 :] = wo_ref[...]
    row = small_ref[...].astype(F32)
    columns = [column_of(row, k * rows, rows) for k in range(6)]
    lane = lax.broadcasted_iota(jnp.int32, (rows, 128), 1)
    small = jnp.zeros((rows, 128), F32)
    for at, column in enumerate(columns):
        small = jnp.where(lane == at, column, small)
    out_ref[:, 3 * HALF : 3 * HALF + 128] = small.astype(BF16)


def k_stack(n, *refs):
    for at, ref in enumerate(refs[:n]):
        start = 0
        for out_ref in refs[n:]:
            out_ref[at] = ref[:, start : start + out_ref.shape[2]]
            start += out_ref.shape[2]


def k_join(first_ref, second_ref, out_ref):
    half = first_ref.shape[0]
    out_ref[:half] = first_ref[...]
    out_ref[half:] = second_ref[...]


def k_qkv(plan, me, resid_ref, *refs):
    n = plan.pieces
    pieces, (qkv_ref, w_ref, h_ref, gains_ref), (tail_ref, wide) = refs[:n], refs[n : n + 4], refs[n + 4 :]
    tokens = resid_ref.shape[0]
    assemble(plan.starts(me[0], plan.LATE, D), pieces, (w_ref, tail_ref), wide)
    tail = tail_ref[...].astype(F32).T
    gains_ref[...] = tail[:8, :]
    gain = tail[0:1, :]

    def norm(at):
        rows = pl.ds(at, STEP)
        x1 = decomp(resid_ref[rows, :].astype(F32))
        h_ref[rows, :] = (x1 * inv_rms(x1) * gain).astype(BF16)

    row_loop(tokens, STEP, norm)
    qkv_ref[...] = dot_nn(h_ref[...], w_ref[...]).astype(BF16)


def attend(qkv_ref, attn_ref, tokens, out_at):
    i_at = lax.broadcasted_iota(jnp.int32, (SEQ, SEQ), 0)
    j_at = lax.broadcasted_iota(jnp.int32, (SEQ, SEQ), 1)
    allowed = j_at <= i_at
    low = lax.broadcasted_iota(jnp.int32, (SEQ, 128), 1) < HD

    def one(seq):
        rows = pl.ds(seq, SEQ)
        for pair in range(HALF // 128):
            cols = slice(128 * pair, 128 * (pair + 1))
            q2 = qkv_ref[rows, cols]
            k2 = qkv_ref[rows, HALF + 128 * pair : HALF + 128 * (pair + 1)]
            v2 = qkv_ref[rows, 2 * HALF + 128 * pair : 2 * HALF + 128 * (pair + 1)]
            mixed = None
            for side in range(2):
                mine = low if side == 0 else jnp.logical_not(low)
                k_one = jnp.where(mine, k2, jnp.zeros_like(k2))
                v_one = jnp.where(mine, v2, jnp.zeros_like(v2))
                scores = jnp.where(allowed, dot_nt(q2, k_one) * (HD ** -0.5), -1e30)
                top = jnp.max(scores, axis=1, keepdims=True)
                powers = jnp.exp(scores - top)
                total = jnp.sum(powers, axis=1, keepdims=True)
                probs = (powers * (1.0 / total)).astype(BF16)
                part = dot_nn(probs, v_one)
                mixed = part if mixed is None else mixed + part
            attn_ref[rows, out_at + 128 * pair : out_at + 128 * (pair + 1)] = mixed.astype(BF16)

    row_loop(tokens, SEQ, one)


def k_attn(qkv_ref, attn_ref):
    attend(qkv_ref, attn_ref, qkv_ref.shape[0], 0)


def k_turn(plan, me, h_ref, attn_ref, h2_ref, ht_ref, attnt_ref, h2t_ref, t_ref, r_ref):
    starts = plan.starts(me[0], plan.SUM, D)
    for ref, out_ref in ((h_ref, ht_ref), (attn_ref, attnt_ref), (h2_ref, h2t_ref)):
        turn(starts, ref[...], out_ref, t_ref, r_ref)


def k_second(plan, me, resid_ref, h_ref, attn0_ref, gains_ref, *refs):
    n = plan.pieces
    pieces, (qkv_ref, w_ref, wo_ref, attn_ref, x2_ref, h2_ref), (wide,) = refs[:n], refs[n : n + 6], refs[n + 6 :]
    tokens = resid_ref.shape[0]
    assemble(plan.starts(me[0], plan.LATE, D), pieces, (w_ref, wo_ref), wide)
    qkv_ref[...] = dot_nn(h_ref[...], w_ref[...]).astype(BF16)
    attn_ref[:, :HALF] = attn0_ref[...]
    attend(qkv_ref, attn_ref, tokens, HALF)
    gain = gains_ref[1:2, :]
    x2_ref[...] = dot_nn(attn_ref[...], wo_ref[...])

    def norm(at):
        rows = pl.ds(at, STEP)
        y = x2_ref[rows, :]
        middle = resid_ref[rows, :].astype(F32) + (y - jnp.mean(y, axis=1, keepdims=True))
        x2 = decomp(jnp.where(last_lane(middle.shape), 0.0, middle))
        x2_ref[rows, :] = x2
        h2_ref[rows, :] = (x2 * inv_rms(x2) * gain).astype(BF16)

    row_loop(tokens, STEP, norm)


GELU_A = math.sqrt(2.0 / math.pi)
GELU_B = 0.044715


def k_up(plan, me, h2_ref, bias_ref, *refs):
    n = plan.pieces
    pieces, (w_ref, act_ref, actt_ref, slope_ref), (u_ref, wide_ref) = refs[:n], refs[n : n + 4], refs[n + 4 :]
    tokens = h2_ref.shape[0]
    assemble(plan.starts(me[0], plan.EARLY, D), pieces, (w_ref,), wide_ref)
    wide = D
    blocks = FF // plan.count if plan.fine else wide
    for tile in range(FF // wide):
        cols = slice(tile * wide, (tile + 1) * wide)
        u_ref[...] = dot_nn(h2_ref[...], w_ref[:, cols])
        bias = bias_ref[:, cols]

        def gelu(at):
            rows = pl.ds(at, 64)
            u = u_ref[rows, :] + bias
            square = u * u
            t = jnp.tanh(u * (GELU_A + (GELU_A * GELU_B) * square))
            half = 0.5 * t + 0.5
            act_ref[rows, cols] = (u * half).astype(BF16)
            slope = half + (u * (0.5 - 0.5 * (t * t))) * (GELU_A + (3.0 * GELU_A * GELU_B) * square)
            slope_ref[rows, cols] = slope

        row_loop(tokens, 64, gelu)
        turned = act_ref[:, cols].T
        for b in range(wide // blocks):
            q = tile * wide // blocks + b
            to = pl.multiple_of(plan.slot(me[0], plan.SUM_DOWN, q) * blocks, blocks) if plan.fine else q * blocks
            actt_ref[pl.ds(to, blocks), :] = turned[b * blocks : (b + 1) * blocks, :]


def place_of(refs, at):
    for ref in refs:
        if at < ref.shape[0]:
            return ref, at
        at -= ref.shape[0]


def split_dot(left_ref, right_ref, keep_ref, *send_refs):
    half = left_ref.shape[0] // 2
    width = right_ref.shape[1]
    _, rows, _ = keep_ref.shape
    for refs, start in ((send_refs, half), ((keep_ref,), 0)):
        for at in range(0, half, 384):
            part = dot_nn(left_ref[start + at : start + at + 384, :], right_ref[...]).astype(BF16)
            if rows > 384:
                refs[0][0, at : at + 384, :width] = part
                continue
            for j in range(384 // rows):
                ref, place = place_of(refs, at // rows + j)
                ref[place, :, :width] = part[j * rows : (j + 1) * rows]


def k_prep(resid_in, cot_in, resid_ref, cot_ref, dz_ref):
    for ref, source in ((resid_ref, resid_in), (cot_ref, cot_in)):
        ref[:, D - 128 :] = jnp.zeros((ref.shape[0], 128), BF16)
        ref[:, : D - 1] = source[...]

    def go(at):
        at_rows = pl.ds(at, STEP)
        c = cot_ref[at_rows, :].astype(F32)
        dz_ref[at_rows, :] = (c - jnp.mean(c, axis=1, keepdims=True)).astype(BF16)

    row_loop(cot_ref.shape[0], STEP, go)


def k_bias(rows, gains_ref, bias_ref, spread_ref, pick_ref):
    half, full = spread_ref.shape
    column = lax.broadcasted_iota(jnp.int32, (half, 1), 0)
    device = jnp.zeros((half, 1), jnp.int32)
    for j in range(1, half // rows):
        device = device + jnp.where(column >= j * rows, 1, 0)
    first = column + 3 * rows * device
    width = 384
    for at in range(0, full, width):
        f = lax.broadcasted_iota(jnp.int32, (half, width), 1) + at
        hit = f == first
        for k in range(1, 4):
            hit = jnp.logical_or(hit, f == first + k * rows)
        spread_ref[:, at : at + width] = jnp.where(hit, 1.0, 0.0).astype(BF16)
    f = lax.broadcasted_iota(jnp.int32, (1, full), 1)
    group = jnp.zeros((1, full), jnp.int32)
    for j in range(1, full // rows):
        group = group + jnp.where(f >= j * rows, 1, 0)
    row = lax.broadcasted_iota(jnp.int32, (8, full), 0)
    pick_ref[...] = jnp.where((group & 3) + 2 == row, 1.0, 0.0)
    small = gains_ref[...].astype(BF16)
    both = dot_nn(jnp.concatenate([small[:, : D // 2], small[:, D // 2 :]], axis=0), spread_ref[...])
    for part in range(2):
        picked = both[8 * part : 8 * part + 8] * pick_ref[...]
        bias_ref[:, part * (FF // 2) : (part + 1) * (FF // 2)] = jnp.sum(picked, axis=0, keepdims=True)


def k_du(plan, me, dz_ref, slope_ref, *refs):
    n = plan.pieces
    pieces, (du_ref, gb_ref, w_ref), (z_ref,) = refs[:n], refs[n : n + 3], refs[n + 3 :]
    tokens = dz_ref.shape[0]
    assemble_plain(plan.starts(me[0], plan.EARLY, FF), pieces, w_ref)
    wide = D
    for tile in range(FF // wide):
        cols = slice(tile * wide, (tile + 1) * wide)
        z_ref[...] = dot_nt(dz_ref[...], w_ref[cols, :])

        def go(i, total):
            rows = pl.ds(pl.multiple_of(i * 64, 64), 64)
            du = (z_ref[rows, :] * slope_ref[rows, cols]).astype(BF16)
            du_ref[rows, cols] = du
            return total + fold8(du.astype(F32))

        total = lax.fori_loop(0, tokens // 64, go, jnp.zeros((8, wide), F32))
        gb_ref[:, cols] = jnp.sum(total, axis=0, keepdims=True)


def k_result(x2_ref, act_ref, w_ref, out_ref, z_ref):
    z_ref[...] = dot_nn(act_ref[...], w_ref[...])

    def result(at):
        rows = pl.ds(at, STEP)
        z = z_ref[rows, :]
        out = (x2_ref[rows, :] + (z - jnp.mean(z, axis=1, keepdims=True))).astype(BF16)
        out_ref[rows, :] = out[:, : D - 1]

    row_loop(act_ref.shape[0], STEP, result)


def k_mid(cot_ref, x2_ref, gains_ref, du_ref, w_up_ref, attnt_ref, dmid_ref, dy_ref, gg_ref, keep_ref, send_ref, dh_ref):
    tokens = cot_ref.shape[0]
    dh_ref[...] = dot_nt(du_ref[...], w_up_ref[...])
    gain = gains_ref[1:2, :]

    def back(i, total):
        rows = pl.ds(pl.multiple_of(i * STEP, STEP), STEP)
        x2 = x2_ref[rows, :]
        dx, summand = norm_back(x2, inv_rms(x2), gain, dh_ref[rows, :])
        dmid = cot_ref[rows, :].astype(F32) + decomp_back(dx)
        dmid_ref[rows, :] = dmid
        dy_ref[rows, :] = (dmid - jnp.mean(dmid, axis=1, keepdims=True)).astype(BF16)
        return total + fold8(summand)

    total = lax.fori_loop(0, tokens // STEP, back, jnp.zeros((8, D), F32))
    gg_ref[...] = jnp.sum(total, axis=0, keepdims=True)
    split_dot(attnt_ref, dy_ref, keep_ref, send_ref)


def k_attn_back(group, dy_ref, wo_ref, qkv_ref, ht_ref, *refs):
    *refs, da_ref = refs
    if group == 1:
        keep_o, send_o, *refs = refs
    dqkv_ref, keep_ref, *send_refs = refs
    if group == 1:
        keep_ref[:, :, 3 * HALF :] = keep_o[...]
        at = 0
        for ref in send_refs:
            ref[:, :, 3 * HALF :] = send_o[at : at + ref.shape[0]]
            at += ref.shape[0]
    tokens = dy_ref.shape[0]
    da_ref[...] = dot_nt(dy_ref[...], wo_ref[HALF * group : HALF * (group + 1), :]).astype(BF16)
    j_at = lax.broadcasted_iota(jnp.int32, (SEQ, SEQ), 0)
    i_at = lax.broadcasted_iota(jnp.int32, (SEQ, SEQ), 1)
    allowed = j_at <= i_at
    low = lax.broadcasted_iota(jnp.int32, (SEQ, 128), 1) < HD
    scale = HD ** -0.5

    def one(seq):
        rows = pl.ds(seq, SEQ)
        for pair in range(HALF // 128):
            cols = [slice(HALF * part + 128 * pair, HALF * part + 128 * (pair + 1)) for part in range(3)]
            q2, k2, v2 = (qkv_ref[rows, c] for c in cols)
            d2 = da_ref[rows, cols[0]]
            dq = dk = dv = None
            for side in range(2):
                mine = low if side == 0 else jnp.logical_not(low)
                q1, k1, v1, d1 = (jnp.where(mine, a, jnp.zeros_like(a)) for a in (q2, k2, v2, d2))
                scores = jnp.where(allowed, dot_nt(k1, q2) * scale, -1e30)
                top = jnp.max(scores, axis=0, keepdims=True)
                powers = jnp.exp(scores - top)
                probs = powers * (1.0 / jnp.sum(powers, axis=0, keepdims=True))
                dp = dot_nt(v1, d2)
                inner = jnp.sum(probs * dp, axis=0, keepdims=True)
                ds = (probs * (dp - inner)).astype(BF16)
                parts = (dot_tn(ds, k1), dot_nn(ds, q1), dot_nn(probs.astype(BF16), d1))
                dq, dk, dv = parts if dq is None else (dq + parts[0], dk + parts[1], dv + parts[2])
            dqkv_ref[rows, cols[0]] = (dq * scale).astype(BF16)
            dqkv_ref[rows, cols[1]] = (dk * scale).astype(BF16)
            dqkv_ref[rows, cols[2]] = dv.astype(BF16)

    row_loop(tokens, SEQ, one)
    split_dot(ht_ref, dqkv_ref, keep_ref, *send_refs)


def k_last(plan, me, resid_ref, dmid_ref, gains_ref, dq0_ref, w0_ref, dq1_ref, w1_ref, gg_ref, gb_ref, spread_ref, pick_ref, out_ref, keep_ref, send_ref, dh_ref, tail_ref):
    tokens = resid_ref.shape[0]
    dh_ref[...] = dot_nt(dq0_ref[...], w0_ref[...]) + dot_nt(dq1_ref[...], w1_ref[...])
    gain = gains_ref[0:1, :]

    def back(i, total):
        rows = pl.ds(pl.multiple_of(i * STEP, STEP), STEP)
        x1 = decomp(resid_ref[rows, :].astype(F32))
        dx, summand = norm_back(x1, inv_rms(x1), gain, dh_ref[rows, :])
        out_ref[rows, :] = (dmid_ref[rows, :] + decomp_back(dx))[:, : D - 1]
        return total + fold8(summand)

    total = lax.fori_loop(0, tokens // STEP, back, jnp.zeros((8, D), F32))
    ga = jnp.sum(total, axis=0, keepdims=True)
    g = jnp.concatenate([gb_ref[:, : FF // 2] * pick_ref[...], gb_ref[:, FF // 2 :] * pick_ref[...]], axis=0)
    high = g.astype(BF16)
    lower = (g - high.astype(F32)).astype(BF16)
    both = dot_nt(jnp.concatenate([high, lower], axis=0), spread_ref[...])
    biases = jnp.concatenate([both[:8] + both[16:24], both[8:16] + both[24:]], axis=1)
    row = lax.broadcasted_iota(jnp.int32, (8, D), 0)
    rows8 = jnp.where(row == 0, ga, jnp.where(row == 1, gg_ref[...], biases))
    high = rows8.astype(BF16).astype(F32)
    both = jnp.concatenate([high, rows8 - high, jnp.zeros((112, D), F32)], axis=0)
    tail_ref[...] = both.T
    starts = plan.starts(me[0], plan.SUM, D)
    if len(starts) == 1:
        keep_ref[0] = tail_ref[: D // 2, :].astype(BF16)
        send_ref[0] = tail_ref[D // 2 :, :].astype(BF16)
    else:
        half = len(starts) // 2
        rows = D // len(starts)
        for s, start in enumerate(starts):
            ref, at = (keep_ref, s) if s < half else (send_ref, s - half)
            ref[at] = tail_ref[pl.ds(pl.multiple_of(start, rows), rows), :].astype(BF16)


def renew(value):
    lane = lax.broadcasted_iota(jnp.int32, value.shape, 1)
    total = value + pltpu.roll(value, 120, 1)
    high = total.astype(BF16).astype(F32)
    lower = pltpu.roll(total - high, 8, 1)
    return jnp.where(lane < 8, high, jnp.where(lane < 16, lower, 0.0))


def add_blocks(tail, a, b):
    value = a.astype(F32) + b.astype(F32)
    if not tail:
        return value
    return jnp.concatenate([value[:, :-128], renew(value[:, -128:])], axis=1)


def k_sum_half(tail, keep_ref, *refs):
    *got, mine_ref, yours_ref = refs
    half = mine_ref.shape[0]
    for s in range(half):
        for ref, at in ((yours_ref, half + s), (mine_ref, s)):
            other, place = place_of(got, at)
            ref[s] = add_blocks(tail, keep_ref[at], other[place]).astype(BF16)


def k_sum_small(keep_ref, keep_t, got_t, *refs):
    *got, mine_ref, yours_ref = refs
    half = mine_ref.shape[0]
    width = keep_ref.shape[2]
    for s in range(2 * half):
        ref, at = (mine_ref, s) if s < half else (yours_ref, s - half)
        other, place = place_of(got, s)
        ref[at, :, :width] = add_blocks(False, keep_ref[s], other[place]).astype(BF16)
        ref[at, :, width:] = renew(add_blocks(False, keep_t[s], got_t[s])).astype(BF16)


def k_sum_four(keep_b, got_b, keep_a, got_a, own, one, two, three):
    width = keep_b.shape[2]
    for m, ref in enumerate((own, one, two, three)):
        ref[:, :width] = add_blocks(False, keep_b[m], got_b[m]).astype(ref.dtype)
        ref[:, width:] = add_blocks(True, keep_a[m], got_a[m]).astype(ref.dtype)


def k_final(n, *refs):
    parts, (qkv_ref, out_ref, b_ref, ga_ref, gm_ref) = refs[:n], refs[n:]
    rows = qkv_ref.shape[0]

    def total(start, width):
        value = parts[0][:, start : start + width]
        for part in parts[1:]:
            value = value + part[:, start : start + width].astype(F32)
        return value

    for part in range(3):
        for at, start in ((0, 3 * HALF + D), (HALF, 0)):
            qkv_ref[:, part * D + at : part * D + at + HALF] = total(start + part * HALF, HALF)
    out_ref[...] = total(3 * HALF, D)
    small = total(6 * HALF + D, 128)
    small = small + pltpu.roll(small, 120, 1)
    lane = lax.broadcasted_iota(jnp.int32, (rows, 128), 1)
    row = lax.broadcasted_iota(jnp.int32, (rows, 128), 0)

    def as_row(column, first):
        return jnp.sum(jnp.where(lane == row + first, small[:, column : column + 1], 0.0), axis=0, keepdims=True)

    ga_ref[...] = as_row(0, 0)[:, :rows]
    gm_ref[...] = as_row(1, 0)[:, :rows]
    b_ref[...] = sum(as_row(2 + k, k * rows) for k in range(4))[:, : 4 * rows]


def bits_of(count):
    return count.bit_length() - 1


SWAP = {"m1": "m2", "m2": "m1", "z1": "z2", "z2": "z1", "zl": "zl", "zh": "zh"}


class Plan:
    LATE = ("zl", "zh", "m1", "m2")
    EARLY = ("m1", "z1", "z2", "m2")
    SUM = ("z1", "z2", "m2", "m1")
    SUM_DOWN = ("m2", "z1", "z2", "m1")

    def __init__(self, mesh):
        self.wide, self.narrow = mesh.shape["wide"], mesh.shape["narrow"]
        self.count = self.wide * self.narrow
        self.low = bits_of(self.narrow)
        self.bits = bits_of(self.count)
        self.core = self.low
        outer = list(range(self.low + 1, self.bits))
        self.ys = list(range(self.low))
        self.x_bit, self.z_bits = outer[0], outer[1:]
        self.cm, self.xm, self.ym = 1 << self.core, 1 << self.x_bit, 1
        self.zl, self.zh = (1 << b for b in self.z_bits[:2])
        self.fine = (D // self.count) % 8 == 0 and self.low == 1 and len(self.z_bits) == 2
        self.pieces = 4 if self.fine else 1

    def index(self):
        return lax.axis_index("wide") * self.narrow + lax.axis_index("narrow")

    def send(self, value, mask, other=None):
        masks = [mask, mask if other is None else other]
        return lax.ppermute(value, AXES, [(i, i ^ masks[(i >> self.core) & 1]) for i in range(self.count)])

    def both(self, name):
        low = {"m1": self.xm, "m2": self.ym, "z1": self.zl, "z2": self.zh, "zl": self.zl, "zh": self.zh}
        return low[name], low[SWAP[name]]

    def exchange(self, name):
        return lambda value: self.send(value, *self.both(name))

    def mask(self, me, name):
        first, second = self.both(name)
        return first if first == second else jnp.where(((me >> self.core) & 1) == 0, first, second)

    def starts(self, me, bits, total):
        if not self.fine:
            return [0]
        masks = []
        for names, extra in ((bits, 0), ([SWAP[b] for b in bits], self.cm)):
            ways = [self.mask(me, name) for name in names]
            for block in range(1 << len(bits)):
                whole = extra
                for k, way in enumerate(ways):
                    if (block >> k) & 1:
                        whole = whole | way
                masks.append(whole)
        return [(me ^ m) * (total // self.count) for m in masks]

    def slot(self, me, bits, device):
        diff = me ^ device
        other = (diff & self.cm) != 0
        at = jnp.where(other, 1 << len(bits), 0)
        for k, name in enumerate(bits):
            way = jnp.where(other, self.mask(me, SWAP[name]), self.mask(me, name))
            at = at + jnp.where((diff & way) != 0, 1 << k, 0)
        return at

    def pair_up(self, own, other, bit, axis):
        mine = (self.index() >> bit) & 1
        return jnp.where(mine == 1, jnp.stack([other, own], axis), jnp.stack([own, other], axis))

    def gather_plain(self, shard):
        value, held = shard, []
        for b in self.z_bits + [self.x_bit] + self.ys + [self.core]:
            axis = sum(1 for h in held if h > b)
            value = self.pair_up(value, self.send(value, 1 << b), b, axis)
            held.append(b)
        return value.reshape(1, -1, shard.shape[1])

    def scatter_plain(self, keep, send, add):
        me = self.index()
        blocks = jnp.concatenate([keep[0], send[0]], 0)
        value = blocks.reshape((2,) * self.bits + (-1, blocks.shape[1]))
        held = list(range(self.bits - 1, -1, -1))
        for b in [self.core] + self.ys + [self.x_bit] + self.z_bits:
            axis, bit = held.index(b), (me >> b) & 1
            mine = lax.dynamic_index_in_dim(value, bit, axis, keepdims=False)
            yours = lax.dynamic_index_in_dim(value, 1 - bit, axis, keepdims=False)
            held.remove(b)
            value = add([mine, self.send(yours, 1 << b)], not held)
        return value


class Gather:
    def __init__(self, plan):
        self.plan, self.fine = plan, plan.fine

    def begin(self, blocks, name):
        if self.fine:
            self.a = blocks if blocks.ndim == 3 else blocks.reshape((1,) + blocks.shape)
            self.got = self.plan.exchange(name)(self.a)
        else:
            self.got = self.plan.gather_plain(blocks) if blocks.ndim == 2 else blocks

    def grow(self, name, waits=()):
        if self.fine:
            count, rows, columns = self.a.shape
            (self.a,) = call(k_join, [((2 * count, rows, columns), BF16)], self.a, self.got, waits=waits)
            self.got = self.plan.exchange(name)(self.a)

    def to_core(self, *after):
        self.near = [self.plan.send(fence(self.a, *after)[0] if after else self.a, self.plan.cm)] if self.fine else []

    def finish(self):
        if self.fine:
            return [self.a, self.got, *self.near, self.plan.send(self.got, self.plan.cm)]
        return [self.got]


def stack(plan, shard, got, widths, waits):
    if not plan.fine:
        cuts = [sum(widths[:i]) for i in range(len(widths) + 1)]
        return [got[:, :, i:j] for i, j in zip(cuts, cuts[1:])]
    return call(functools.partial(k_stack, 4), [((4, shard.shape[0], w), BF16) for w in widths], shard, *got, waits=waits)


class Scatter:
    def __init__(self, plan, keep, *sends):
        self.plan, self.fine, self.keep = plan, plan.fine, keep
        self.small = False
        if plan.fine:
            self.got = [plan.send(part, plan.cm) for part in sends]
        else:
            self.got = [plan.scatter_plain(keep, sends[0], add_plain)]

    def add_small(self, keep, send):
        if self.fine:
            self.small_parts = [keep, self.plan.send(send, self.plan.cm)]
        else:
            self.got.append(self.plan.scatter_plain(keep, send, add_two))

    def halve(self, name, waits=()):
        if not self.fine:
            return
        count, rows, columns = self.keep.shape
        if not self.small and hasattr(self, "small_parts"):
            self.small = True
            body, columns = k_sum_small, columns + 128
            args = [self.keep, *self.small_parts, *self.got]
        else:
            body = functools.partial(k_sum_half, self.small)
            args = [self.keep, *self.got]
        self.keep, yours = call(body, [((count // 2, rows, columns), BF16)] * 2, *args, waits=waits)
        self.got = [self.plan.exchange(name)(yours)]

    def total(self):
        if not self.fine:
            return self.got[0]
        return self.keep[0].astype(F32) + self.got[0][0].astype(F32)


def finish_late(plan, sb, sa):
    if not plan.fine:
        small = sa.got[1]
        rest = jnp.zeros((small.shape[0], 120), F32)
        return [jnp.concatenate([sb.got[0], sa.got[0], small, rest], axis=1)]
    rows, width = sb.keep.shape[1:]
    whole = width + sa.keep.shape[2]
    own, *others = call(
        k_sum_four, [((rows, whole), F32)] + [((rows, whole), BF16)] * 3, sb.keep, sb.got[0], sa.keep, sa.got[0]
    )
    return [own, plan.exchange("z1")(others[0]), plan.exchange("z2")(others[1]), plan.send(others[2], plan.zl | plan.zh)]


def add_plain(arrived, last):
    total = arrived[0].astype(F32)
    for part in arrived[1:]:
        total = total + part.astype(F32)
    return total if last else total.astype(BF16)


def add_two(arrived, last):
    total = 0.0
    for part in arrived:
        whole = part.astype(F32)
        total = total + (whole[..., :8] + whole[..., 8:16])
    if last:
        return total
    high = lax.reduce_precision(total, 8, 7)
    rest = jnp.zeros(total.shape[:-1] + (112,), F32)
    return jnp.concatenate([high, total - high, rest], axis=-1).astype(BF16)


def fence(*values):
    return lax.optimization_barrier(values)


def device_step(plan, resid_in, w_qkv, w_out, w_up, b_up, w_down, gain_attn, gain_mlp, cotangent):
    rows = w_qkv.shape[0]
    t, d, half = resid_in.shape[0], D, D // 2
    wide3 = 3 * HALF
    CHAIN.clear()
    KEEP.clear()
    first = wide3 + 128
    fine = plan.fine
    me = plan.index().reshape(1)
    bind = lambda body: functools.partial(body, plan)
    turned = [pltpu.VMEM((d, t), F32)] * 2

    def blocks(r, columns, *pieces):
        if not fine:
            return [((1, half * r // rows, columns), BF16)] * 2
        return [((count, r, columns), BF16) for count in (16, *(pieces or (16,)))]

    a, b, u, v = (Gather(plan) for _ in range(4))
    u.begin(w_up, "m1")
    v.begin(w_down, "m1")
    (shard,) = call(
        k_pack, [((rows, first + wide3 + d), BF16)],
        w_qkv, w_out, jnp.concatenate([gain_attn, gain_mlp, b_up]).reshape(1, 6 * rows), free=True,
        scratch=[pltpu.VMEM(shape, BF16) for shape in ((rows, 3 * d), (rows, d), (1, 6 * rows))]
        + [pltpu.SemaphoreType.DMA((3,))],
    )
    got = [plan.send(shard, m) for m in (plan.zl, plan.zh, plan.zl | plan.zh)] if fine else plan.gather_plain(shard)
    resid, cot, dz = call(k_prep, [((t, d), BF16)] * 3, resid_in, cotangent, waits=[me])
    four_a, four_b = stack(plan, shard, got, (first, wide3 + d), [u.got, v.got])
    KEEP.append(resid)
    a.begin(four_a, "m1")
    b.begin(four_b, "m1")
    u.grow("z1")
    v.grow("z1")
    a.grow("m2", [b.got, u.got, v.got])
    KEEP.extend([a.a] if fine else [])
    b.grow("m2")
    KEEP.extend([b.a] if fine else [])
    u.grow("z2")
    a.to_core()
    b.to_core()
    u.grow("m2", [a.got, b.got, *a.near, *b.near])
    u.to_core()
    KEEP.extend([*a.near, *b.near])
    v.grow("z2")
    a_pieces, b_pieces = a.finish(), b.finish()
    qkv0, w0, h1, gains = call(
        bind(k_qkv),
        [((t, wide3), BF16), ((d, wide3), BF16), ((t, d), BF16), ((8, d), F32)],
        me, resid, *a_pieces,
        scratch=[pltpu.VMEM((d, 128), BF16), pltpu.VMEM((d, half), F32)], smem=1, waits=b_pieces[-1:],
    )
    KEEP[:] = [resid, b.a, *b.near] if fine else [resid]
    (attn0,) = call(k_attn, [((t, HALF), BF16)], qkv0)
    qkv1, w1, wo, attn, x2, h2 = call(
        bind(k_second),
        [((t, wide3), BF16), ((d, wide3), BF16), ((d, d), BF16), ((t, d), BF16), ((t, d), F32), ((t, d), BF16)],
        me, resid, h1, attn0, gains, *b_pieces,
        scratch=[pltpu.VMEM((d, half), F32)], smem=1,
    )
    KEEP.clear()
    v.grow("m2", [u.got, *u.near])
    v.to_core(CHAIN[-1])
    bias, spread, pick = call(
        functools.partial(k_bias, rows), [((1, FF), F32), ((half, 4 * half), BF16), ((8, 4 * half), F32)], gains
    )
    wu, act, actt, slope = call(
        bind(k_up),
        [((d, FF), BF16), ((t, FF), BF16), ((FF, t), BF16), ((t, FF), F32)],
        me, h2, bias, *u.finish(),
        scratch=[pltpu.VMEM((t, d), F32), pltpu.VMEM((d, half), F32)], smem=1,
    )
    sv = Scatter(plan, *call(split_dot, blocks(4 * rows, d, 4, 4, 4, 4), actt, dz, waits=v.near))
    h1t, attnt, h2t = call(bind(k_turn), [((d, t), BF16)] * 3, me, h1, attn, h2, scratch=turned, smem=1)
    sv.halve("m1")
    du, gb, w_down_all = call(
        bind(k_du),
        [((t, FF), BF16), ((1, FF), F32), ((FF, d), BF16)],
        me, dz, slope, *v.finish(), scratch=[pltpu.VMEM((t, d), F32)], smem=1,
    )
    su = Scatter(plan, *call(split_dot, blocks(rows, FF, 4, 4, 4, 4), h2t, du))
    dmid, dy, gg, keep_o, send_o = call(
        k_mid,
        [((t, d), F32), ((t, d), BF16), ((1, d), F32)] + blocks(rows, d),
        cot, x2, gains, du, wu, attnt,
        scratch=[pltpu.VMEM((t, d), F32)],
    )
    sv.halve("z2")
    su.halve("m1")
    back_scratch = [pltpu.VMEM((t, HALF), BF16)]
    dqkv1, *parts = call(
        functools.partial(k_attn_back, 1), [((t, wide3), BF16)] + blocks(rows, wide3 + d, 6, 5, 5),
        dy, wo, qkv1, h1t, keep_o, send_o, scratch=back_scratch,
    )
    sb = Scatter(plan, *parts)
    dqkv0, *parts = call(
        functools.partial(k_attn_back, 0), [((t, wide3), BF16)] + blocks(rows, wide3, 8, 8),
        dy, wo, qkv0, h1t, scratch=back_scratch,
    )
    sa = Scatter(plan, *parts)
    sb.halve("m1")
    su.halve("m2")
    dres, *parts = call(
        bind(k_last),
        [((t, d - 1), F32)] + blocks(rows, 128),
        me, resid, dmid, gains, dqkv0, w0, dqkv1, w1, gg, gb, spread, pick,
        scratch=[pltpu.VMEM((t, d), F32), pltpu.VMEM((d, 128), F32)], smem=1,
    )
    sa.add_small(*parts)
    sv.halve("z1")
    sa.halve("m1")
    (out,) = call(k_result, [((t, d - 1), BF16)], x2, act, w_down_all, scratch=[pltpu.VMEM((t, d), F32)])
    su.halve("z2")
    sb.halve("m2")
    sa.halve("m2")
    sv.halve("m2")
    su.halve("z1")
    late = finish_late(plan, sb, sa)
    s_down, s_up = sv.total(), su.total()
    s_qkv, s_out, s_b, s_a, s_m = call(
        functools.partial(k_final, len(late)),
        [((rows, 3 * d), F32), ((rows, d), F32), ((1, 4 * rows), F32), ((1, rows), F32), ((1, rows), F32)],
        *late,
    )
    return (out, dres, s_qkv, s_out, s_up, s_b.reshape(4 * rows), s_down, s_a.reshape(rows), s_m.reshape(rows))


def solution(mesh):
    rows2, rows1 = P(AXES, None), P(AXES)
    in_specs = (rows2, rows2, rows2, rows2, rows1, rows2, rows1, rows1, rows2)
    out_specs = (rows2, rows2, rows2, rows2, rows2, rows1, rows2, rows1, rows1)
    plan = Plan(mesh)

    def on_device(*arrays):
        return device_step(plan, *arrays)

    return jax.shard_map(on_device, mesh=mesh, in_specs=in_specs, out_specs=out_specs, check_vma=False)
```

```python
import functools
import math

import jax
import jax.numpy as jnp
from jax import lax
from jax.experimental import pallas as pl
from jax.experimental.pallas import tpu as pltpu
from jax.sharding import PartitionSpec as P

D = 768
H = 12
HD = 64
FF = 3072
SEQ = 256
HALF = 384
EPS = 1e-05
AXES = ("wide", "narrow")
F32 = jnp.float32
BF16 = jnp.bfloat16
MIB = 1 << 20
LIMIT = 12

VMEM_SPEC = pl.BlockSpec(memory_space=pltpu.VMEM)
SMEM_SPEC = pl.BlockSpec(memory_space=pltpu.SMEM)
ANY_SPEC = pl.BlockSpec(memory_space=pl.ANY)


def dot_nn(a, b):
    return lax.dot_general(a, b, (((1,), (0,)), ((), ())), preferred_element_type=F32)


def dot_nt(a, b):
    return lax.dot_general(a, b, (((1,), (1,)), ((), ())), preferred_element_type=F32)


def dot_tn(a, b):
    return lax.dot_general(a, b, (((0,), (0,)), ((), ())), preferred_element_type=F32)


STEP = 128


def last_lane(shape):
    return lax.broadcasted_iota(jnp.int32, shape, 1) == D - 1


def decomp(padded):
    total = jnp.sum(padded, axis=1, keepdims=True)
    return jnp.where(last_lane(padded.shape), -total, padded)


def inv_rms(values):
    return lax.rsqrt(jnp.mean(values * values, axis=1, keepdims=True) + EPS)


def norm_back(x, r, gain, dh):
    xdh = x * dh
    dx = r * (gain * dh) - x * (r * r * r) * jnp.mean(xdh * gain, axis=1, keepdims=True)
    return dx, xdh * r


def decomp_back(dx):
    return dx - dx[:, D - 1 :]


KEEP = []
CHAIN = []


def call(body, outs, *args, scratch=(), limit=LIMIT, smem=0, waits=(), free=False):
    wait = CHAIN[-1:] + list(waits)
    wait += [k for k in KEEP if not any(k is x for x in (*args, *wait))]
    specs = [SMEM_SPEC] * smem + [ANY_SPEC if free else VMEM_SPEC] * (len(args) - smem) + [ANY_SPEC] * len(wait)

    def run(*refs):
        body(*refs[: len(args)], *refs[len(args) + len(wait) :])

    results = pl.pallas_call(
        run,
        out_shape=[jax.ShapeDtypeStruct(s, d) for s, d in outs],
        in_specs=specs,
        out_specs=[VMEM_SPEC] * len(outs),
        scratch_shapes=list(scratch),
        compiler_params=pltpu.CompilerParams(vmem_limit_bytes=limit * MIB),
        cost_estimate=pl.CostEstimate(flops=1000, bytes_accessed=1000, transcendentals=0),
    )(*args, *wait)
    CHAIN.append(min(results, key=lambda r: r.size * r.dtype.itemsize))
    return results


def assemble_plain(starts, pieces, out_ref):
    at = 0
    for ref in pieces:
        count, rows, _ = ref.shape
        for m in range(count):
            out_ref[pl.ds(pl.multiple_of(starts[at], rows), rows), :] = ref[m]
            at += 1


def assemble(starts, pieces, out_refs, wide_ref, column=0):
    for out_ref in out_refs:
        for begin in range(0, out_ref.shape[1], wide_ref.shape[1]):
            width = min(wide_ref.shape[1], out_ref.shape[1] - begin)
            at = 0
            for ref in pieces:
                count, rows, _ = ref.shape
                for m in range(count):
                    cols = pl.ds(column + begin, width)
                    if not isinstance(column, int):
                        cols = pl.ds(pl.multiple_of(column + begin, 128), width)
                    block = ref[m, :, cols].astype(F32)
                    wide_ref[pl.ds(pl.multiple_of(starts[at], rows), rows), :width] = block
                    at += 1
            out_ref[:, begin : begin + width] = wide_ref[:, :width].astype(BF16)
        column += out_ref.shape[1]


def turn(starts, value, out_ref, t_ref, r_ref):
    turned = value.astype(F32).T
    if len(starts) == 1:
        out_ref[...] = turned.astype(BF16)
        return
    t_ref[...] = turned
    rows = turned.shape[0] // len(starts)
    for s, start in enumerate(starts):
        r_ref[rows * s : rows * (s + 1), :] = t_ref[pl.ds(pl.multiple_of(start, rows), rows), :]
    out_ref[...] = r_ref[...].astype(BF16)


def row_loop(total, step, body):
    def go(i, carry):
        body(pl.multiple_of(i * step, step))
        return carry

    lax.fori_loop(0, total // step, go, 0)


def fold8(rows):
    total = rows[0:8]
    for at in range(8, rows.shape[0], 8):
        total = total + rows[at : at + 8]
    return total


def column_of(row, first, count):
    r_at = lax.broadcasted_iota(jnp.int32, (count, row.shape[1]), 0)
    c_at = lax.broadcasted_iota(jnp.int32, (count, row.shape[1]), 1)
    return jnp.sum(jnp.where(c_at == r_at + first, row, 0.0), axis=1, keepdims=True)


def k_pack(w_any, wo_any, small_any, out_ref, w_ref, wo_ref, small_ref, sems):
    refs = ((w_any, w_ref), (wo_any, wo_ref), (small_any, small_ref))
    copies = [pltpu.make_async_copy(a, b, sems.at[i]) for i, (a, b) in enumerate(refs)]
    for copy in copies:
        copy.start()
    for copy in copies:
        copy.wait()
    rows = w_ref.shape[0]
    for group, start in ((0, 0), (1, 3 * HALF + 128)):
        for part in range(3):
            at = part * D + group * HALF
            out_ref[:, start + part * HALF : start + (part + 1) * HALF] = w_ref[:, at : at + HALF]
    out_ref[:, 6 * HALF + 128 :] = wo_ref[...]
    row = small_ref[...].astype(F32)
    columns = [column_of(row, k * rows, rows) for k in range(6)]
    lane = lax.broadcasted_iota(jnp.int32, (rows, 128), 1)
    small = jnp.zeros((rows, 128), F32)
    for at, column in enumerate(columns):
        small = jnp.where(lane == at, column, small)
    out_ref[:, 3 * HALF : 3 * HALF + 128] = small.astype(BF16)


def k_stack(n, *refs):
    for at, ref in enumerate(refs[:n]):
        start = 0
        for out_ref in refs[n:]:
            out_ref[at] = ref[:, start : start + out_ref.shape[2]]
            start += out_ref.shape[2]


def k_join(first_ref, second_ref, out_ref):
    half = first_ref.shape[0]
    out_ref[:half] = first_ref[...]
    out_ref[half:] = second_ref[...]


def k_qkv(plan, me, resid_ref, *refs):
    n = plan.pieces
    pieces, (qkv_ref, w_ref, h_ref, gains_ref), (tail_ref, wide) = refs[:n], refs[n : n + 4], refs[n + 4 :]
    tokens = resid_ref.shape[0]
    assemble(plan.starts(me[0], plan.LATE, D), pieces, (w_ref, tail_ref), wide)
    tail = tail_ref[...].astype(F32).T
    gains_ref[...] = tail[:8, :]
    gain = tail[0:1, :]

    def norm(at):
        rows = pl.ds(at, STEP)
        x1 = decomp(resid_ref[rows, :].astype(F32))
        h_ref[rows, :] = (x1 * inv_rms(x1) * gain).astype(BF16)

    row_loop(tokens, STEP, norm)
    qkv_ref[...] = dot_nn(h_ref[...], w_ref[...]).astype(BF16)


def attend(qkv_ref, attn_ref, tokens, out_at):
    i_at = lax.broadcasted_iota(jnp.int32, (SEQ, SEQ), 0)
    j_at = lax.broadcasted_iota(jnp.int32, (SEQ, SEQ), 1)
    allowed = j_at <= i_at
    low = lax.broadcasted_iota(jnp.int32, (SEQ, 128), 1) < HD

    def one(seq):
        rows = pl.ds(seq, SEQ)
        for pair in range(HALF // 128):
            cols = slice(128 * pair, 128 * (pair + 1))
            q2 = qkv_ref[rows, cols]
            k2 = qkv_ref[rows, HALF + 128 * pair : HALF + 128 * (pair + 1)]
            v2 = qkv_ref[rows, 2 * HALF + 128 * pair : 2 * HALF + 128 * (pair + 1)]
            mixed = None
            for side in range(2):
                mine = low if side == 0 else jnp.logical_not(low)
                k_one = jnp.where(mine, k2, jnp.zeros_like(k2))
                v_one = jnp.where(mine, v2, jnp.zeros_like(v2))
                scores = jnp.where(allowed, dot_nt(q2, k_one) * (HD ** -0.5), -1e30)
                top = jnp.max(scores, axis=1, keepdims=True)
                powers = jnp.exp(scores - top)
                total = jnp.sum(powers, axis=1, keepdims=True)
                probs = (powers * (1.0 / total)).astype(BF16)
                part = dot_nn(probs, v_one)
                mixed = part if mixed is None else mixed + part
            attn_ref[rows, out_at + 128 * pair : out_at + 128 * (pair + 1)] = mixed.astype(BF16)

    row_loop(tokens, SEQ, one)


def k_attn(qkv_ref, attn_ref):
    attend(qkv_ref, attn_ref, qkv_ref.shape[0], 0)


def k_turn(plan, me, h_ref, attn_ref, h2_ref, ht_ref, attnt_ref, h2t_ref, t_ref, r_ref):
    starts = plan.starts(me[0], plan.SUM, D)
    for ref, out_ref in ((h_ref, ht_ref), (attn_ref, attnt_ref), (h2_ref, h2t_ref)):
        turn(starts, ref[...], out_ref, t_ref, r_ref)


def k_second(plan, me, resid_ref, h_ref, attn0_ref, gains_ref, *refs):
    n = plan.pieces
    pieces, (qkv_ref, w_ref, wo_ref, attn_ref, x2_ref, h2_ref), (wide,) = refs[:n], refs[n : n + 6], refs[n + 6 :]
    tokens = resid_ref.shape[0]
    assemble(plan.starts(me[0], plan.LATE, D), pieces, (w_ref, wo_ref), wide)
    qkv_ref[...] = dot_nn(h_ref[...], w_ref[...]).astype(BF16)
    attn_ref[:, :HALF] = attn0_ref[...]
    attend(qkv_ref, attn_ref, tokens, HALF)
    gain = gains_ref[1:2, :]
    x2_ref[...] = dot_nn(attn_ref[...], wo_ref[...])

    def norm(at):
        rows = pl.ds(at, STEP)
        y = x2_ref[rows, :]
        middle = resid_ref[rows, :].astype(F32) + (y - jnp.mean(y, axis=1, keepdims=True))
        x2 = decomp(jnp.where(last_lane(middle.shape), 0.0, middle))
        x2_ref[rows, :] = x2
        h2_ref[rows, :] = (x2 * inv_rms(x2) * gain).astype(BF16)

    row_loop(tokens, STEP, norm)


GELU_A = math.sqrt(2.0 / math.pi)
GELU_B = 0.044715


def k_up(plan, part, me, h2_ref, bias_ref, dz_ref, *refs):
    n = plan.pieces
    pieces, refs = refs[:n], refs[n:]
    (w_ref, act_ref, slope_ref), grad_refs, (u_ref, wide_ref, actt_ref) = refs[:3], refs[3:-3], refs[-3:]
    tokens = h2_ref.shape[0]
    wide = D
    start = plan.half(me[0], part) * (FF // 2)
    assemble(plan.starts(me[0], plan.EARLY, D), pieces, (w_ref,), wide_ref, start)
    block = tokens // 2
    work = [(tile, half) for tile in range(FF // 2 // wide) for half in range(2)]

    def project(step):
        tile, half = work[step]
        u_ref[step % 2] = dot_nn(h2_ref[half * block : (half + 1) * block, :], w_ref[:, tile * wide : (tile + 1) * wide])

    def gelu(step):
        tile, half = work[step]
        cols = slice(tile * wide, (tile + 1) * wide)
        bias = bias_ref[:, pl.ds(pl.multiple_of(start + tile * wide, 128), wide)]
        for at in range(0, block, 64):
            rows = slice(half * block + at, half * block + at + 64)
            u = u_ref[step % 2, at : at + 64, :] + bias
            square = u * u
            t = jnp.tanh(u * (GELU_A + (GELU_A * GELU_B) * square))
            middle = 0.5 * t + 0.5
            act_ref[rows, cols] = (u * middle).astype(BF16)
            slope = middle + (u * (0.5 - 0.5 * (t * t))) * (GELU_A + (3.0 * GELU_A * GELU_B) * square)
            slope_ref[rows, cols] = slope

    project(0)
    for step in range(len(work)):
        if step + 1 < len(work):
            project(step + 1)
        gelu(step)
    for tile in range(FF // 2 // wide):
        cols = slice(tile * wide, (tile + 1) * wide)
        turned = act_ref[:, cols].T
        if not plan.fine:
            actt_ref[cols, :] = turned
            continue
        rows = FF // plan.count
        for b in range(wide // rows):
            to = pl.multiple_of(plan.down_place(me[0], tile * (wide // rows) + b) * rows, rows)
            actt_ref[pl.ds(to, rows), :] = turned[b * rows : (b + 1) * rows, :]
    at = 0
    for ref in grad_refs:
        count, rows, _ = ref.shape
        for begin in range(0, count * rows, 384):
            product = dot_nn(actt_ref[at + begin : at + begin + 384, :], dz_ref[...]).astype(BF16)
            if rows > 384:
                ref[0, begin : begin + 384, :] = product
            else:
                for j in range(384 // rows):
                    ref[begin // rows + j] = product[j * rows : (j + 1) * rows]
        at += count * rows


def place_of(refs, at):
    for ref in refs:
        if at < ref.shape[0]:
            return ref, at
        at -= ref.shape[0]


def split_dot(left_ref, right_ref, keep_ref, *send_refs):
    half = left_ref.shape[0] // 2
    width = right_ref.shape[1]
    _, rows, _ = keep_ref.shape
    for refs, start in ((send_refs, half), ((keep_ref,), 0)):
        for at in range(0, half, 384):
            part = dot_nn(left_ref[start + at : start + at + 384, :], right_ref[...]).astype(BF16)
            if rows > 384:
                refs[0][0, at : at + 384, :width] = part
                continue
            for j in range(384 // rows):
                ref, place = place_of(refs, at // rows + j)
                ref[place, :, :width] = part[j * rows : (j + 1) * rows]


def k_prep(resid_in, cot_in, resid_ref, cot_ref, dz_ref):
    for ref, source in ((resid_ref, resid_in), (cot_ref, cot_in)):
        ref[:, D - 128 :] = jnp.zeros((ref.shape[0], 128), BF16)
        ref[:, : D - 1] = source[...]

    def go(at):
        at_rows = pl.ds(at, STEP)
        c = cot_ref[at_rows, :].astype(F32)
        dz_ref[at_rows, :] = (c - jnp.mean(c, axis=1, keepdims=True)).astype(BF16)

    row_loop(cot_ref.shape[0], STEP, go)


def k_bias(rows, gains_ref, bias_ref, spread_ref, pick_ref):
    half, full = spread_ref.shape
    column = lax.broadcasted_iota(jnp.int32, (half, 1), 0)
    device = jnp.zeros((half, 1), jnp.int32)
    for j in range(1, half // rows):
        device = device + jnp.where(column >= j * rows, 1, 0)
    first = column + 3 * rows * device
    width = 384
    for at in range(0, full, width):
        f = lax.broadcasted_iota(jnp.int32, (half, width), 1) + at
        hit = f == first
        for k in range(1, 4):
            hit = jnp.logical_or(hit, f == first + k * rows)
        spread_ref[:, at : at + width] = jnp.where(hit, 1.0, 0.0).astype(BF16)
    f = lax.broadcasted_iota(jnp.int32, (1, full), 1)
    group = jnp.zeros((1, full), jnp.int32)
    for j in range(1, full // rows):
        group = group + jnp.where(f >= j * rows, 1, 0)
    row = lax.broadcasted_iota(jnp.int32, (8, full), 0)
    pick_ref[...] = jnp.where((group & 3) + 2 == row, 1.0, 0.0)
    small = gains_ref[...].astype(BF16)
    both = dot_nn(jnp.concatenate([small[:, : D // 2], small[:, D // 2 :]], axis=0), spread_ref[...])
    for part in range(2):
        picked = both[8 * part : 8 * part + 8] * pick_ref[...]
        bias_ref[:, part * (FF // 2) : (part + 1) * (FF // 2)] = jnp.sum(picked, axis=0, keepdims=True)


def k_du(plan, me, dz_ref, slope_a, slope_b, *refs):
    n = plan.pieces
    pieces, (du_ref, gb_ref, w_ref), (z_ref,) = refs[:n], refs[n : n + 3], refs[n + 3 :]
    tokens = dz_ref.shape[0]
    assemble_plain(plan.starts(me[0], plan.EARLY, FF), pieces, w_ref)
    wide = D
    slopes = (slope_a, slope_b)
    work = [(part, tile) for part in range(2) for tile in range(FF // 2 // wide)]

    def columns(step):
        part, tile = work[step]
        return pl.ds(pl.multiple_of(plan.half(me[0], part) * (FF // 2) + tile * wide, 128), wide)

    def project(step):
        z_ref[step % 2] = dot_nt(dz_ref[...], w_ref[columns(step), :])

    def scale(step):
        part, tile = work[step]
        cols = slice(tile * wide, (tile + 1) * wide)
        total = jnp.zeros((8, wide), F32)
        for at in range(0, tokens, 64):
            rows = slice(at, at + 64)
            du = (z_ref[step % 2, rows, :] * slopes[part][rows, cols]).astype(BF16)
            du_ref[rows, columns(step)] = du
            total = total + fold8(du.astype(F32))
        gb_ref[:, columns(step)] = jnp.sum(total, axis=0, keepdims=True)

    project(0)
    for step in range(len(work)):
        if step + 1 < len(work):
            project(step + 1)
        scale(step)


def half_columns(plan, me, part):
    return pl.ds(pl.multiple_of(plan.half(me, part) * (FF // 2), 128), FF // 2)


def k_result(plan, me, x2_ref, act_a, act_b, w_ref, out_ref, z_ref):
    z_ref[...] = dot_nn(act_a[...], w_ref[half_columns(plan, me[0], 0), :])
    z_ref[...] += dot_nn(act_b[...], w_ref[half_columns(plan, me[0], 1), :])

    def result(at):
        rows = pl.ds(at, STEP)
        z = z_ref[rows, :]
        out = (x2_ref[rows, :] + (z - jnp.mean(z, axis=1, keepdims=True))).astype(BF16)
        out_ref[rows, :] = out[:, : D - 1]

    row_loop(act_a.shape[0], STEP, result)


def k_mid(plan, me, cot_ref, x2_ref, gains_ref, du_ref, w_a, w_b, attnt_ref, dmid_ref, dy_ref, gg_ref, keep_ref, send_ref, dh_ref):
    tokens = cot_ref.shape[0]
    block = tokens // 2
    gain = gains_ref[1:2, :]

    def project(part):
        rows = slice(part * block, (part + 1) * block)
        first = dot_nt(du_ref[rows, half_columns(plan, me[0], 0)], w_a[...])
        dh_ref[rows, :] = first + dot_nt(du_ref[rows, half_columns(plan, me[0], 1)], w_b[...])

    def back(part, total):
        for at in range(part * block, (part + 1) * block, STEP):
            rows = slice(at, at + STEP)
            x2 = x2_ref[rows, :]
            dx, summand = norm_back(x2, inv_rms(x2), gain, dh_ref[rows, :])
            dmid = cot_ref[rows, :].astype(F32) + decomp_back(dx)
            dmid_ref[rows, :] = dmid
            dy_ref[rows, :] = (dmid - jnp.mean(dmid, axis=1, keepdims=True)).astype(BF16)
            total = total + fold8(summand)
        return total

    project(0)
    project(1)
    total = back(1, back(0, jnp.zeros((8, D), F32)))
    gg_ref[...] = jnp.sum(total, axis=0, keepdims=True)
    split_dot(attnt_ref, dy_ref, keep_ref, send_ref)


def k_attn_back(group, dy_ref, wo_ref, qkv_ref, ht_ref, *refs):
    *refs, da_ref = refs
    if group == 1:
        keep_o, send_o, *refs = refs
    dqkv_ref, keep_ref, *send_refs = refs
    if group == 1:
        keep_ref[:, :, 3 * HALF :] = keep_o[...]
        at = 0
        for ref in send_refs:
            ref[:, :, 3 * HALF :] = send_o[at : at + ref.shape[0]]
            at += ref.shape[0]
    tokens = dy_ref.shape[0]
    da_ref[...] = dot_nt(dy_ref[...], wo_ref[HALF * group : HALF * (group + 1), :]).astype(BF16)
    j_at = lax.broadcasted_iota(jnp.int32, (SEQ, SEQ), 0)
    i_at = lax.broadcasted_iota(jnp.int32, (SEQ, SEQ), 1)
    allowed = j_at <= i_at
    low = lax.broadcasted_iota(jnp.int32, (SEQ, 128), 1) < HD
    scale = HD ** -0.5

    def one(seq):
        rows = pl.ds(seq, SEQ)
        for pair in range(HALF // 128):
            cols = [slice(HALF * part + 128 * pair, HALF * part + 128 * (pair + 1)) for part in range(3)]
            q2, k2, v2 = (qkv_ref[rows, c] for c in cols)
            d2 = da_ref[rows, cols[0]]
            dq = dk = dv = None
            for side in range(2):
                mine = low if side == 0 else jnp.logical_not(low)
                q1, k1, v1, d1 = (jnp.where(mine, a, jnp.zeros_like(a)) for a in (q2, k2, v2, d2))
                scores = jnp.where(allowed, dot_nt(k1, q2) * scale, -1e30)
                top = jnp.max(scores, axis=0, keepdims=True)
                powers = jnp.exp(scores - top)
                probs = powers * (1.0 / jnp.sum(powers, axis=0, keepdims=True))
                dp = dot_nt(v1, d2)
                inner = jnp.sum(probs * dp, axis=0, keepdims=True)
                ds = (probs * (dp - inner)).astype(BF16)
                parts = (dot_tn(ds, k1), dot_nn(ds, q1), dot_nn(probs.astype(BF16), d1))
                dq, dk, dv = parts if dq is None else (dq + parts[0], dk + parts[1], dv + parts[2])
            dqkv_ref[rows, cols[0]] = (dq * scale).astype(BF16)
            dqkv_ref[rows, cols[1]] = (dk * scale).astype(BF16)
            dqkv_ref[rows, cols[2]] = dv.astype(BF16)

    for seq in range(0, tokens, SEQ):
        one(seq)
    split_dot(ht_ref, dqkv_ref, keep_ref, *send_refs)


def k_last(plan, me, resid_ref, dmid_ref, gains_ref, dq0_ref, w0_ref, dq1_ref, w1_ref, gg_ref, gb_ref, spread_ref, pick_ref, out_ref, keep_ref, send_ref, dh_ref, tail_ref):
    tokens = resid_ref.shape[0]
    block = tokens // 2
    gain = gains_ref[0:1, :]

    def project(part):
        rows = slice(part * block, (part + 1) * block)
        dh_ref[rows, :] = dot_nt(dq0_ref[rows, :], w0_ref[...]) + dot_nt(dq1_ref[rows, :], w1_ref[...])

    def back(part, total):
        for at in range(part * block, (part + 1) * block, STEP):
            rows = slice(at, at + STEP)
            x1 = decomp(resid_ref[rows, :].astype(F32))
            dx, summand = norm_back(x1, inv_rms(x1), gain, dh_ref[rows, :])
            out_ref[rows, :] = (dmid_ref[rows, :] + decomp_back(dx))[:, : D - 1]
            total = total + fold8(summand)
        return total

    project(0)
    project(1)
    total = back(1, back(0, jnp.zeros((8, D), F32)))
    ga = jnp.sum(total, axis=0, keepdims=True)
    g = jnp.concatenate([gb_ref[:, : FF // 2] * pick_ref[...], gb_ref[:, FF // 2 :] * pick_ref[...]], axis=0)
    high = g.astype(BF16)
    lower = (g - high.astype(F32)).astype(BF16)
    both = dot_nt(jnp.concatenate([high, lower], axis=0), spread_ref[...])
    biases = jnp.concatenate([both[:8] + both[16:24], both[8:16] + both[24:]], axis=1)
    row = lax.broadcasted_iota(jnp.int32, (8, D), 0)
    rows8 = jnp.where(row == 0, ga, jnp.where(row == 1, gg_ref[...], biases))
    high = rows8.astype(BF16).astype(F32)
    both = jnp.concatenate([high, rows8 - high, jnp.zeros((112, D), F32)], axis=0)
    tail_ref[...] = both.T
    starts = plan.starts(me[0], plan.SUM, D)
    if len(starts) == 1:
        keep_ref[0] = tail_ref[: D // 2, :].astype(BF16)
        send_ref[0] = tail_ref[D // 2 :, :].astype(BF16)
    else:
        half = len(starts) // 2
        rows = D // len(starts)
        for s, start in enumerate(starts):
            ref, at = (keep_ref, s) if s < half else (send_ref, s - half)
            ref[at] = tail_ref[pl.ds(pl.multiple_of(start, rows), rows), :].astype(BF16)


def renew(value):
    lane = lax.broadcasted_iota(jnp.int32, value.shape, 1)
    total = value + pltpu.roll(value, 120, 1)
    high = total.astype(BF16).astype(F32)
    lower = pltpu.roll(total - high, 8, 1)
    return jnp.where(lane < 8, high, jnp.where(lane < 16, lower, 0.0))


def add_blocks(tail, a, b):
    value = a.astype(F32) + b.astype(F32)
    if not tail:
        return value
    return jnp.concatenate([value[:, :-128], renew(value[:, -128:])], axis=1)


def k_sum_half(tail, keep_ref, *refs):
    *got, mine_ref, yours_ref = refs
    half = mine_ref.shape[0]
    for s in range(half):
        for ref, at in ((yours_ref, half + s), (mine_ref, s)):
            other, place = place_of(got, at)
            ref[s] = add_blocks(tail, keep_ref[at], other[place]).astype(BF16)


def k_sum_down(plan, me, *refs):
    keeps, gots, (mine_ref, yours_ref) = refs[:4], refs[4:8], refs[8:]
    first = ((me[0] >> plan.core) & 1) == 0
    for z2 in range(2):
        for z1 in range(2):
            for m1, out_ref in ((1, yours_ref), (0, mine_ref)):
                for m2 in range(2):
                    sums = []
                    for which in sorted({2 * z2 + z1, 2 * z1 + z2}):
                        sums.append(add_blocks(False, keeps[which][2 * m1 + m2], gots[which][2 * m1 + m2]))
                    if z1 != z2:
                        own, swapped = (sums[0], sums[1]) if z2 == 0 else (sums[1], sums[0])
                        sums = [jnp.where(first, own, swapped)]
                    out_ref[4 * z2 + 2 * z1 + m2] = sums[0].astype(BF16)


def k_sum_small(keep_ref, keep_t, got_t, *refs):
    *got, mine_ref, yours_ref = refs
    half = mine_ref.shape[0]
    width = keep_ref.shape[2]
    for s in range(2 * half):
        ref, at = (mine_ref, s) if s < half else (yours_ref, s - half)
        other, place = place_of(got, s)
        ref[at, :, :width] = add_blocks(False, keep_ref[s], other[place]).astype(BF16)
        ref[at, :, width:] = renew(add_blocks(False, keep_t[s], got_t[s])).astype(BF16)


def k_sum_four(keep_b, got_b, keep_a, got_a, own, one, two, three):
    width = keep_b.shape[2]
    for m, ref in enumerate((own, one, two, three)):
        ref[:, :width] = add_blocks(False, keep_b[m], got_b[m]).astype(ref.dtype)
        ref[:, width:] = add_blocks(True, keep_a[m], got_a[m]).astype(ref.dtype)


def k_final(n, *refs):
    parts, (qkv_ref, out_ref, b_ref, ga_ref, gm_ref) = refs[:n], refs[n:]
    rows = qkv_ref.shape[0]

    def total(start, width):
        value = parts[0][:, start : start + width]
        for part in parts[1:]:
            value = value + part[:, start : start + width].astype(F32)
        return value

    for part in range(3):
        for at, start in ((0, 3 * HALF + D), (HALF, 0)):
            qkv_ref[:, part * D + at : part * D + at + HALF] = total(start + part * HALF, HALF)
    out_ref[...] = total(3 * HALF, D)
    small = total(6 * HALF + D, 128)
    small = small + pltpu.roll(small, 120, 1)
    lane = lax.broadcasted_iota(jnp.int32, (rows, 128), 1)
    row = lax.broadcasted_iota(jnp.int32, (rows, 128), 0)

    def as_row(column, first):
        return jnp.sum(jnp.where(lane == row + first, small[:, column : column + 1], 0.0), axis=0, keepdims=True)

    ga_ref[...] = as_row(0, 0)[:, :rows]
    gm_ref[...] = as_row(1, 0)[:, :rows]
    b_ref[...] = sum(as_row(2 + k, k * rows) for k in range(4))[:, : 4 * rows]


def bits_of(count):
    return count.bit_length() - 1


SWAP = {"m1": "m2", "m2": "m1", "z1": "z2", "z2": "z1", "zl": "zl", "zh": "zh"}


class Plan:
    LATE = ("zl", "zh", "m1", "m2")
    EARLY = ("m1", "z1", "z2", "m2")
    SUM = ("z1", "z2", "m2", "m1")
    SUM_DOWN = ("m2", "z1", "z2", "m1")

    def __init__(self, mesh):
        self.wide, self.narrow = mesh.shape["wide"], mesh.shape["narrow"]
        self.count = self.wide * self.narrow
        self.low = bits_of(self.narrow)
        self.bits = bits_of(self.count)
        self.core = self.low
        outer = list(range(self.low + 1, self.bits))
        self.ys = list(range(self.low))
        self.x_bit, self.z_bits = outer[0], outer[1:]
        self.cm, self.xm, self.ym = 1 << self.core, 1 << self.x_bit, 1
        self.zl, self.zh = (1 << b for b in self.z_bits[:2])
        self.fine = (D // self.count) % 8 == 0 and self.low == 1 and len(self.z_bits) == 2
        self.pieces = 4 if self.fine else 1

    def index(self):
        return lax.axis_index("wide") * self.narrow + lax.axis_index("narrow")

    def send(self, value, mask, other=None):
        masks = [mask, mask if other is None else other]
        return lax.ppermute(value, AXES, [(i, i ^ masks[(i >> self.core) & 1]) for i in range(self.count)])

    def both(self, name):
        low = {"m1": self.xm, "m2": self.ym, "z1": self.zl, "z2": self.zh, "zl": self.zl, "zh": self.zh}
        return low[name], low[SWAP[name]]

    def exchange(self, name):
        return lambda value: self.send(value, *self.both(name))

    def mask(self, me, name):
        first, second = self.both(name)
        return first if first == second else jnp.where(((me >> self.core) & 1) == 0, first, second)

    def starts(self, me, bits, total):
        if not self.fine:
            return [0]
        masks = []
        for names, extra in ((bits, 0), ([SWAP[b] for b in bits], self.cm)):
            ways = [self.mask(me, name) for name in names]
            for block in range(1 << len(bits)):
                whole = extra
                for k, way in enumerate(ways):
                    if (block >> k) & 1:
                        whole = whole | way
                masks.append(whole)
        return [(me ^ m) * (total // self.count) for m in masks]

    def half(self, me, part):
        return ((me >> self.z_bits[1]) & 1) ^ part if self.fine else part

    def down_place(self, me, device):
        diff = (me ^ device) & (self.count // 2 - 1)
        other = (diff & self.cm) != 0
        at = jnp.where(other, 0, 8)
        at = at + jnp.where((diff & self.zl) != 0, 4, 0)
        for name, step in (("m1", 2), ("m2", 1)):
            way = jnp.where(other, self.mask(me, SWAP[name]), self.mask(me, name))
            at = at + jnp.where((diff & way) != 0, step, 0)
        return at

    def pair_up(self, own, other, bit, axis):
        mine = (self.index() >> bit) & 1
        return jnp.where(mine == 1, jnp.stack([other, own], axis), jnp.stack([own, other], axis))

    def gather_plain(self, shard):
        value, held = shard, []
        for b in self.z_bits + [self.x_bit] + self.ys + [self.core]:
            axis = sum(1 for h in held if h > b)
            value = self.pair_up(value, self.send(value, 1 << b), b, axis)
            held.append(b)
        return value.reshape(1, -1, shard.shape[1])

    def scatter_plain(self, keep, send, add):
        me = self.index()
        blocks = jnp.concatenate([keep[0], send[0]], 0)
        value = blocks.reshape((2,) * self.bits + (-1, blocks.shape[1]))
        held = list(range(self.bits - 1, -1, -1))
        for b in [self.core] + self.ys + [self.x_bit] + self.z_bits:
            axis, bit = held.index(b), (me >> b) & 1
            mine = lax.dynamic_index_in_dim(value, bit, axis, keepdims=False)
            yours = lax.dynamic_index_in_dim(value, 1 - bit, axis, keepdims=False)
            held.remove(b)
            value = add([mine, self.send(yours, 1 << b)], not held)
        return value


class Gather:
    def __init__(self, plan):
        self.plan, self.fine = plan, plan.fine

    def begin(self, blocks, name):
        if self.fine:
            self.a = blocks if blocks.ndim == 3 else blocks.reshape((1,) + blocks.shape)
            self.got = self.plan.exchange(name)(self.a)
        else:
            self.got = self.plan.gather_plain(blocks) if blocks.ndim == 2 else blocks

    def grow(self, name, waits=()):
        if self.fine:
            count, rows, columns = self.a.shape
            (self.a,) = call(k_join, [((2 * count, rows, columns), BF16)], self.a, self.got, waits=waits)
            self.got = self.plan.exchange(name)(self.a)

    def to_core(self, *after):
        self.near = [self.plan.send(fence(self.a, *after)[0] if after else self.a, self.plan.cm)] if self.fine else []

    def finish(self, *after):
        if self.fine:
            far = fence(self.got, *after)[0] if after else self.got
            return [self.a, self.got, *self.near, self.plan.send(far, self.plan.cm)]
        return [self.got]


def stack(plan, shard, got, widths, waits):
    if not plan.fine:
        cuts = [sum(widths[:i]) for i in range(len(widths) + 1)]
        return [got[:, :, i:j] for i, j in zip(cuts, cuts[1:])]
    return call(functools.partial(k_stack, 4), [((4, shard.shape[0], w), BF16) for w in widths], shard, *got, waits=waits)


class Scatter:
    def __init__(self, plan, keep, *sends):
        self.plan, self.fine, self.keep = plan, plan.fine, keep
        self.small = False
        if plan.fine:
            self.got = [plan.send(part, plan.cm) for part in sends]
        else:
            self.got = [plan.scatter_plain(keep, sends[0], add_plain)]

    def add_small(self, keep, send):
        if self.fine:
            self.small_parts = [keep, self.plan.send(send, self.plan.cm)]
        else:
            self.got.append(self.plan.scatter_plain(keep, send, add_two))

    def halve(self, name, waits=(), me=None):
        if not self.fine:
            return
        count, rows, columns = (self.keep[0] if isinstance(self.keep, list) else self.keep).shape
        if isinstance(self.keep, list):
            self.keep, yours = call(
                functools.partial(k_sum_down, self.plan), [((8, rows, columns), BF16)] * 2,
                me, *self.keep, *self.got, smem=1, waits=waits,
            )
            self.got = [self.plan.exchange(name)(yours)]
            return
        if not self.small and hasattr(self, "small_parts"):
            self.small = True
            body, columns = k_sum_small, columns + 128
            args = [self.keep, *self.small_parts, *self.got]
        else:
            body = functools.partial(k_sum_half, self.small)
            args = [self.keep, *self.got]
        self.keep, yours = call(body, [((count // 2, rows, columns), BF16)] * 2, *args, waits=waits)
        self.got = [self.plan.exchange(name)(yours)]

    def total(self):
        if not self.fine:
            return self.got[0]
        return self.keep[0].astype(F32) + self.got[0][0].astype(F32)


def finish_late(plan, sb, sa):
    if not plan.fine:
        small = sa.got[1]
        rest = jnp.zeros((small.shape[0], 120), F32)
        return [jnp.concatenate([sb.got[0], sa.got[0], small, rest], axis=1)]
    rows, width = sb.keep.shape[1:]
    whole = width + sa.keep.shape[2]
    own, *others = call(
        k_sum_four, [((rows, whole), F32)] + [((rows, whole), BF16)] * 3, sb.keep, sb.got[0], sa.keep, sa.got[0]
    )
    return [own, plan.exchange("z1")(others[0]), plan.exchange("z2")(others[1]), plan.send(others[2], plan.zl | plan.zh)]


def add_plain(arrived, last):
    total = arrived[0].astype(F32)
    for part in arrived[1:]:
        total = total + part.astype(F32)
    return total if last else total.astype(BF16)


def add_two(arrived, last):
    total = 0.0
    for part in arrived:
        whole = part.astype(F32)
        total = total + (whole[..., :8] + whole[..., 8:16])
    if last:
        return total
    high = lax.reduce_precision(total, 8, 7)
    rest = jnp.zeros(total.shape[:-1] + (112,), F32)
    return jnp.concatenate([high, total - high, rest], axis=-1).astype(BF16)


def fence(*values):
    return lax.optimization_barrier(values)


def device_step(plan, resid_in, w_qkv, w_out, w_up, b_up, w_down, gain_attn, gain_mlp, cotangent):
    rows = w_qkv.shape[0]
    t, d, half = resid_in.shape[0], D, D // 2
    wide3 = 3 * HALF
    CHAIN.clear()
    KEEP.clear()
    first = wide3 + 128
    fine = plan.fine
    me = plan.index().reshape(1)
    bind = lambda body: functools.partial(body, plan)
    turned = [pltpu.VMEM((d, t), F32)] * 2

    def blocks(r, columns, *pieces):
        if not fine:
            return [((1, half * r // rows, columns), BF16)] * 2
        return [((count, r, columns), BF16) for count in (16, *(pieces or (16,)))]

    a, b, u, v = (Gather(plan) for _ in range(4))
    u.begin(w_up, "m1")
    v.begin(w_down, "m1")
    (shard,) = call(
        k_pack, [((rows, first + wide3 + d), BF16)],
        w_qkv, w_out, jnp.concatenate([gain_attn, gain_mlp, b_up]).reshape(1, 6 * rows), free=True,
        scratch=[pltpu.VMEM(shape, BF16) for shape in ((rows, 3 * d), (rows, d), (1, 6 * rows))]
        + [pltpu.SemaphoreType.DMA((3,))],
    )
    got = [plan.send(shard, m) for m in (plan.zl, plan.zh, plan.zl | plan.zh)] if fine else plan.gather_plain(shard)
    resid, cot, dz = call(k_prep, [((t, d), BF16)] * 3, resid_in, cotangent, waits=[me])
    four_a, four_b = stack(plan, shard, got, (first, wide3 + d), [u.got, v.got])
    KEEP.append(resid)
    a.begin(four_a, "m1")
    b.begin(four_b, "m1")
    u.grow("z1")
    v.grow("z1")
    a.grow("m2", [b.got, u.got, v.got])
    KEEP.extend([a.a] if fine else [])
    b.grow("m2")
    KEEP.extend([b.a] if fine else [])
    u.grow("z2")
    a.to_core()
    b.to_core()
    u.grow("m2", [a.got, b.got, *a.near, *b.near])
    u.to_core()
    KEEP.extend([*a.near, *b.near])
    v.grow("z2")
    a_pieces, b_pieces = a.finish(), b.finish()
    qkv0, w0, h1, gains = call(
        bind(k_qkv),
        [((t, wide3), BF16), ((d, wide3), BF16), ((t, d), BF16), ((8, d), F32)],
        me, resid, *a_pieces,
        scratch=[pltpu.VMEM((d, 128), BF16), pltpu.VMEM((d, half), F32)], smem=1, waits=b_pieces[-1:],
    )
    KEEP[:] = [resid, b.a, *b.near] if fine else [resid]
    (attn0,) = call(k_attn, [((t, HALF), BF16)], qkv0)
    qkv1, w1, wo, attn, x2, h2 = call(
        bind(k_second),
        [((t, wide3), BF16), ((d, wide3), BF16), ((d, d), BF16), ((t, d), BF16), ((t, d), F32), ((t, d), BF16)],
        me, resid, h1, attn0, gains, *b_pieces,
        scratch=[pltpu.VMEM((d, half), F32)], smem=1,
    )
    KEEP.clear()
    v.grow("m2", [u.got, *u.near])
    v.to_core(CHAIN[-1])
    bias, spread, pick = call(
        functools.partial(k_bias, rows), [((1, FF), F32), ((half, 4 * half), BF16), ((8, 4 * half), F32)], gains
    )
    u_pieces = u.finish(h2)
    ups = []
    for part in range(2):
        grads = [((4, 4 * rows, d), BF16)] * 4 if fine else [((1, FF // 2, d), BF16)]
        ups.append(call(
            functools.partial(k_up, plan, part),
            [((d, FF // 2), BF16), ((t, FF // 2), BF16), ((t, FF // 2), F32)] + grads,
            me, h2, bias, dz, *u_pieces,
            scratch=[pltpu.VMEM((2, t // 2, d), F32), pltpu.VMEM((d, half), F32), pltpu.VMEM((FF // 2, t), BF16)],
            smem=1, waits=v.near if part else (),
        ))
    wu, act, slope = ([up[i] for up in ups] for i in range(3))
    if fine:
        sv = Scatter(plan, [part for up in ups for part in up[5:7]], *[part for up in ups for part in up[3:5]])
    else:
        sv = Scatter(plan, ups[0][3], ups[1][3])
    h1t, attnt, h2t = call(bind(k_turn), [((d, t), BF16)] * 3, me, h1, attn, h2, scratch=turned, smem=1)
    sv.halve("m1", me=me)
    du, gb, w_down_all = call(
        bind(k_du),
        [((t, FF), BF16), ((1, FF), F32), ((FF, d), BF16)],
        me, dz, *slope, *v.finish(*([sv.keep] if fine else [])), scratch=[pltpu.VMEM((2, t, d), F32)], smem=1,
    )
    su = Scatter(plan, *call(split_dot, blocks(rows, FF, 4, 4, 4, 4), h2t, du))
    dmid, dy, gg, keep_o, send_o = call(
        bind(k_mid),
        [((t, d), F32), ((t, d), BF16), ((1, d), F32)] + blocks(rows, d),
        me, cot, x2, gains, du, *wu, attnt,
        scratch=[pltpu.VMEM((t, d), F32)], smem=1,
    )
    su.halve("m1")
    sv.halve("z2")
    back_scratch = [pltpu.VMEM((t, HALF), BF16)]
    dqkv1, *parts = call(
        functools.partial(k_attn_back, 1), [((t, wide3), BF16)] + blocks(rows, wide3 + d, 6, 5, 5),
        dy, wo, qkv1, h1t, keep_o, send_o, scratch=back_scratch,
    )
    sb = Scatter(plan, *parts)
    dqkv0, *parts = call(
        functools.partial(k_attn_back, 0), [((t, wide3), BF16)] + blocks(rows, wide3, 8, 8),
        dy, wo, qkv0, h1t, scratch=back_scratch,
    )
    sa = Scatter(plan, *parts)
    sb.halve("m1")
    su.halve("m2")
    dres, *parts = call(
        bind(k_last),
        [((t, d - 1), F32)] + blocks(rows, 128),
        me, resid, dmid, gains, dqkv0, w0, dqkv1, w1, gg, gb, spread, pick,
        scratch=[pltpu.VMEM((t, d), F32), pltpu.VMEM((d, 128), F32)], smem=1,
    )
    sa.add_small(*parts)
    sv.halve("z1")
    sa.halve("m1")
    (out,) = call(
        bind(k_result), [((t, d - 1), BF16)], me, x2, *act, w_down_all, scratch=[pltpu.VMEM((t, d), F32)], smem=1
    )
    su.halve("z2")
    sb.halve("m2")
    sa.halve("m2")
    sv.halve("m2")
    su.halve("z1")
    late = finish_late(plan, sb, sa)
    s_down, s_up = sv.total(), su.total()
    s_qkv, s_out, s_b, s_a, s_m = call(
        functools.partial(k_final, len(late)),
        [((rows, 3 * d), F32), ((rows, d), F32), ((1, 4 * rows), F32), ((1, rows), F32), ((1, rows), F32)],
        *late,
    )
    return (out, dres, s_qkv, s_out, s_up, s_b.reshape(4 * rows), s_down, s_a.reshape(rows), s_m.reshape(rows))


def solution(mesh):
    rows2, rows1 = P(AXES, None), P(AXES)
    in_specs = (rows2, rows2, rows2, rows2, rows1, rows2, rows1, rows1, rows2)
    out_specs = (rows2, rows2, rows2, rows2, rows2, rows1, rows2, rows1, rows1)
    plan = Plan(mesh)

    def on_device(*arrays):
        return device_step(plan, *arrays)

    return jax.shard_map(on_device, mesh=mesh, in_specs=in_specs, out_specs=out_specs, check_vma=False)
```

```python
import functools
import math

import jax
import jax.numpy as jnp
from jax import lax
from jax.experimental import pallas as pl
from jax.experimental.pallas import tpu as pltpu
from jax.sharding import PartitionSpec as P

D = 768
H = 12
HD = 64
FF = 3072
SEQ = 256
HALF = 384
EPS = 1e-05
AXES = ("wide", "narrow")
F32 = jnp.float32
BF16 = jnp.bfloat16
MIB = 1 << 20
LIMIT = 10

VMEM_SPEC = pl.BlockSpec(memory_space=pltpu.VMEM)
SMEM_SPEC = pl.BlockSpec(memory_space=pltpu.SMEM)
ANY_SPEC = pl.BlockSpec(memory_space=pl.ANY)


def dot_nn(a, b):
    return lax.dot_general(a, b, (((1,), (0,)), ((), ())), preferred_element_type=F32)


def dot_nt(a, b):
    return lax.dot_general(a, b, (((1,), (1,)), ((), ())), preferred_element_type=F32)


def dot_tn(a, b):
    return lax.dot_general(a, b, (((0,), (0,)), ((), ())), preferred_element_type=F32)


STEP = 128


def last_lane(shape):
    return lax.broadcasted_iota(jnp.int32, shape, 1) == D - 1


def decomp(padded):
    total = jnp.sum(padded, axis=1, keepdims=True)
    return jnp.where(last_lane(padded.shape), -total, padded)


def inv_rms(values):
    return lax.rsqrt(jnp.mean(values * values, axis=1, keepdims=True) + EPS)


def norm_back(x, r, gain, dh):
    xdh = x * dh
    dx = r * (gain * dh) - x * (r * r * r) * jnp.mean(xdh * gain, axis=1, keepdims=True)
    return dx, xdh * r


def decomp_back(dx):
    return dx - dx[:, D - 1 :]


KEEP = []
CHAIN = []


def call(body, outs, *args, scratch=(), limit=LIMIT, smem=0, waits=(), free=False):
    wait = CHAIN[-1:] + list(waits)
    wait += [k for k in KEEP if not any(k is x for x in (*args, *wait))]
    specs = [SMEM_SPEC] * smem + [ANY_SPEC if free else VMEM_SPEC] * (len(args) - smem) + [ANY_SPEC] * len(wait)

    def run(*refs):
        body(*refs[: len(args)], *refs[len(args) + len(wait) :])

    results = pl.pallas_call(
        run,
        out_shape=[jax.ShapeDtypeStruct(s, d) for s, d in outs],
        in_specs=specs,
        out_specs=[VMEM_SPEC] * len(outs),
        scratch_shapes=list(scratch),
        compiler_params=pltpu.CompilerParams(vmem_limit_bytes=limit * MIB),
        cost_estimate=pl.CostEstimate(flops=1000, bytes_accessed=1000, transcendentals=0),
    )(*args, *wait)
    CHAIN.append(min(results, key=lambda r: r.size * r.dtype.itemsize))
    return results


def assemble_plain(starts, pieces, out_ref):
    at = 0
    for ref in pieces:
        count, rows, _ = ref.shape
        for m in range(count):
            out_ref[pl.ds(pl.multiple_of(starts[at], rows), rows), :] = ref[m]
            at += 1


def assemble(starts, pieces, out_refs, wide_ref, column=0):
    for out_ref in out_refs:
        for begin in range(0, out_ref.shape[1], wide_ref.shape[1]):
            width = min(wide_ref.shape[1], out_ref.shape[1] - begin)
            at = 0
            for ref in pieces:
                count, rows, _ = ref.shape
                for m in range(count):
                    cols = pl.ds(column + begin, width)
                    if not isinstance(column, int):
                        cols = pl.ds(pl.multiple_of(column + begin, 128), width)
                    block = ref[m, :, cols].astype(F32)
                    wide_ref[pl.ds(pl.multiple_of(starts[at], rows), rows), :width] = block
                    at += 1
            out_ref[:, begin : begin + width] = wide_ref[:, :width].astype(BF16)
        column += out_ref.shape[1]


def turn(starts, value, out_ref, t_ref, r_ref):
    turned = value.astype(F32).T
    if len(starts) == 1:
        out_ref[...] = turned.astype(BF16)
        return
    t_ref[...] = turned
    rows = turned.shape[0] // len(starts)
    for s, start in enumerate(starts):
        r_ref[rows * s : rows * (s + 1), :] = t_ref[pl.ds(pl.multiple_of(start, rows), rows), :]
    out_ref[...] = r_ref[...].astype(BF16)


def row_loop(total, step, body):
    def go(i, carry):
        body(pl.multiple_of(i * step, step))
        return carry

    lax.fori_loop(0, total // step, go, 0)


def fold8(rows):
    total = rows[0:8]
    for at in range(8, rows.shape[0], 8):
        total = total + rows[at : at + 8]
    return total


def column_of(row, first, count):
    r_at = lax.broadcasted_iota(jnp.int32, (count, row.shape[1]), 0)
    c_at = lax.broadcasted_iota(jnp.int32, (count, row.shape[1]), 1)
    return jnp.sum(jnp.where(c_at == r_at + first, row, 0.0), axis=1, keepdims=True)


def k_pack(w_any, wo_any, small_any, out_ref, w_ref, wo_ref, small_ref, sems):
    refs = ((w_any, w_ref), (wo_any, wo_ref), (small_any, small_ref))
    copies = [pltpu.make_async_copy(a, b, sems.at[i]) for i, (a, b) in enumerate(refs)]
    for copy in copies:
        copy.start()
    for copy in copies:
        copy.wait()
    rows = w_ref.shape[0]
    for group, start in ((0, 0), (1, 3 * HALF + 128)):
        for part in range(3):
            at = part * D + group * HALF
            out_ref[:, start + part * HALF : start + (part + 1) * HALF] = w_ref[:, at : at + HALF]
    out_ref[:, 6 * HALF + 128 :] = wo_ref[...]
    row = small_ref[...].astype(F32)
    columns = [column_of(row, k * rows, rows) for k in range(6)]
    lane = lax.broadcasted_iota(jnp.int32, (rows, 128), 1)
    small = jnp.zeros((rows, 128), F32)
    for at, column in enumerate(columns):
        small = jnp.where(lane == at, column, small)
    out_ref[:, 3 * HALF : 3 * HALF + 128] = small.astype(BF16)


def k_stack(n, *refs):
    for at, ref in enumerate(refs[:n]):
        start = 0
        for out_ref in refs[n:]:
            out_ref[at] = ref[:, start : start + out_ref.shape[2]]
            start += out_ref.shape[2]


def k_join(first_ref, second_ref, out_ref):
    half = first_ref.shape[0]
    out_ref[:half] = first_ref[...]
    out_ref[half:] = second_ref[...]


def k_qkv(plan, me, resid_ref, *refs):
    n = plan.pieces
    pieces, (qkv_ref, w_ref, h_ref, gains_ref), (tail_ref, wide) = refs[:n], refs[n : n + 4], refs[n + 4 :]
    tokens = resid_ref.shape[0]
    assemble(plan.starts(me[0], plan.LATE, D), pieces, (w_ref, tail_ref), wide)
    tail = tail_ref[...].astype(F32).T
    gains_ref[...] = tail[:8, :]
    gain = tail[0:1, :]

    for at in range(0, tokens, STEP):
        rows = slice(at, at + STEP)
        x1 = decomp(resid_ref[rows, :].astype(F32))
        h_ref[rows, :] = (x1 * inv_rms(x1) * gain).astype(BF16)
    for at in range(0, tokens, SEQ):
        rows = slice(at, at + SEQ)
        qkv_ref[rows, :] = dot_nn(h_ref[rows, :], w_ref[...]).astype(BF16)


def attend(qkv_ref, attn_ref, tokens, out_at):
    i_at = lax.broadcasted_iota(jnp.int32, (SEQ, SEQ), 0)
    j_at = lax.broadcasted_iota(jnp.int32, (SEQ, SEQ), 1)
    allowed = j_at <= i_at
    low = lax.broadcasted_iota(jnp.int32, (SEQ, 128), 1) < HD

    def one(seq):
        rows = pl.ds(seq, SEQ)
        for pair in range(HALF // 128):
            cols = slice(128 * pair, 128 * (pair + 1))
            q2 = qkv_ref[rows, cols]
            k2 = qkv_ref[rows, HALF + 128 * pair : HALF + 128 * (pair + 1)]
            v2 = qkv_ref[rows, 2 * HALF + 128 * pair : 2 * HALF + 128 * (pair + 1)]
            mixed = None
            for side in range(2):
                mine = low if side == 0 else jnp.logical_not(low)
                k_one = jnp.where(mine, k2, jnp.zeros_like(k2))
                v_one = jnp.where(mine, v2, jnp.zeros_like(v2))
                scores = jnp.where(allowed, dot_nt(q2, k_one) * (HD ** -0.5), -1e30)
                top = jnp.max(scores, axis=1, keepdims=True)
                powers = jnp.exp(scores - top)
                total = jnp.sum(powers, axis=1, keepdims=True)
                probs = (powers * (1.0 / total)).astype(BF16)
                part = dot_nn(probs, v_one)
                mixed = part if mixed is None else mixed + part
            attn_ref[rows, out_at + 128 * pair : out_at + 128 * (pair + 1)] = mixed.astype(BF16)

    for seq in range(0, tokens, SEQ):
        one(seq)


def k_attn(qkv_ref, attn_ref):
    attend(qkv_ref, attn_ref, qkv_ref.shape[0], 0)


def k_turn(plan, me, h_ref, attn_ref, h2_ref, ht_ref, attnt_ref, h2t_ref, t_ref, r_ref):
    starts = plan.starts(me[0], plan.SUM, D)
    for ref, out_ref in ((h_ref, ht_ref), (attn_ref, attnt_ref), (h2_ref, h2t_ref)):
        turn(starts, ref[...], out_ref, t_ref, r_ref)


def k_second(plan, me, resid_ref, h_ref, attn0_ref, gains_ref, *refs):
    n = plan.pieces
    pieces, (qkv_ref, w_ref, wo_ref, attn_ref, x2_ref, h2_ref), (wide,) = refs[:n], refs[n : n + 6], refs[n + 6 :]
    tokens = resid_ref.shape[0]
    assemble(plan.starts(me[0], plan.LATE, D), pieces, (w_ref, wo_ref), wide)
    for at in range(0, tokens, SEQ):
        rows = slice(at, at + SEQ)
        qkv_ref[rows, :] = dot_nn(h_ref[rows, :], w_ref[...]).astype(BF16)
    attn_ref[:, :HALF] = attn0_ref[...]
    attend(qkv_ref, attn_ref, tokens, HALF)
    gain = gains_ref[1:2, :]
    for at in range(0, tokens, SEQ):
        rows = slice(at, at + SEQ)
        x2_ref[rows, :] = dot_nn(attn_ref[rows, :], wo_ref[...])
    for at in range(0, tokens, STEP):
        rows = slice(at, at + STEP)
        y = x2_ref[rows, :]
        middle = resid_ref[rows, :].astype(F32) + (y - jnp.mean(y, axis=1, keepdims=True))
        x2 = decomp(jnp.where(last_lane(middle.shape), 0.0, middle))
        x2_ref[rows, :] = x2
        h2_ref[rows, :] = (x2 * inv_rms(x2) * gain).astype(BF16)


GELU_A = math.sqrt(2.0 / math.pi)
GELU_B = 0.044715


def k_up(plan, part, me, h2_ref, bias_ref, dz_ref, *refs):
    n = plan.pieces
    pieces, refs = refs[:n], refs[n:]
    (w_ref, act_ref, slope_ref), grad_refs, (u_ref, wide_ref, actt_ref) = refs[:3], refs[3:-3], refs[-3:]
    tokens = h2_ref.shape[0]
    wide = D
    start = plan.half(me[0], part) * (FF // 2)
    assemble(plan.starts(me[0], plan.EARLY, D), pieces, (w_ref,), wide_ref, start)
    block = tokens // 2
    work = [(tile, half) for tile in range(FF // 2 // wide) for half in range(2)]

    def project(step):
        tile, half = work[step]
        u_ref[step % 2] = dot_nn(h2_ref[half * block : (half + 1) * block, :], w_ref[:, tile * wide : (tile + 1) * wide])

    def gelu(step):
        tile, half = work[step]
        cols = slice(tile * wide, (tile + 1) * wide)
        bias = bias_ref[:, pl.ds(pl.multiple_of(start + tile * wide, 128), wide)]
        for at in range(0, block, 64):
            rows = slice(half * block + at, half * block + at + 64)
            u = u_ref[step % 2, at : at + 64, :] + bias
            square = u * u
            t = jnp.tanh(u * (GELU_A + (GELU_A * GELU_B) * square))
            middle = 0.5 * t + 0.5
            act_ref[rows, cols] = (u * middle).astype(BF16)
            slope = middle + (u * (0.5 - 0.5 * (t * t))) * (GELU_A + (3.0 * GELU_A * GELU_B) * square)
            slope_ref[rows, cols] = slope

    project(0)
    for step in range(len(work)):
        if step + 1 < len(work):
            project(step + 1)
        gelu(step)
    for tile in range(FF // 2 // wide):
        cols = slice(tile * wide, (tile + 1) * wide)
        turned = act_ref[:, cols].T
        if not plan.fine:
            actt_ref[cols, :] = turned
            continue
        rows = FF // plan.count
        for b in range(wide // rows):
            to = pl.multiple_of(plan.down_place(me[0], tile * (wide // rows) + b) * rows, rows)
            actt_ref[pl.ds(to, rows), :] = turned[b * rows : (b + 1) * rows, :]
    at = 0
    for ref in grad_refs:
        count, rows, _ = ref.shape
        for begin in range(0, count * rows, 384):
            product = dot_nn(actt_ref[at + begin : at + begin + 384, :], dz_ref[...]).astype(BF16)
            if rows > 384:
                ref[0, begin : begin + 384, :] = product
            else:
                for j in range(384 // rows):
                    ref[begin // rows + j] = product[j * rows : (j + 1) * rows]
        at += count * rows


def place_of(refs, at):
    for ref in refs:
        if at < ref.shape[0]:
            return ref, at
        at -= ref.shape[0]


def split_dot(left_ref, right_ref, keep_ref, *send_refs):
    half = left_ref.shape[0] // 2
    width = right_ref.shape[1]
    _, rows, _ = keep_ref.shape
    for refs, start in ((send_refs, half), ((keep_ref,), 0)):
        for at in range(0, half, 384):
            part = dot_nn(left_ref[start + at : start + at + 384, :], right_ref[...]).astype(BF16)
            if rows > 384:
                refs[0][0, at : at + 384, :width] = part
                continue
            for j in range(384 // rows):
                ref, place = place_of(refs, at // rows + j)
                ref[place, :, :width] = part[j * rows : (j + 1) * rows]


def k_prep(resid_in, cot_in, resid_ref, cot_ref, dz_ref):
    for ref, source in ((resid_ref, resid_in), (cot_ref, cot_in)):
        ref[:, D - 128 :] = jnp.zeros((ref.shape[0], 128), BF16)
        ref[:, : D - 1] = source[...]

    def go(at):
        at_rows = pl.ds(at, STEP)
        c = cot_ref[at_rows, :].astype(F32)
        dz_ref[at_rows, :] = (c - jnp.mean(c, axis=1, keepdims=True)).astype(BF16)

    row_loop(cot_ref.shape[0], STEP, go)


def k_bias(rows, gains_ref, bias_ref, spread_ref, pick_ref):
    half, full = spread_ref.shape
    column = lax.broadcasted_iota(jnp.int32, (half, 1), 0)
    device = jnp.zeros((half, 1), jnp.int32)
    for j in range(1, half // rows):
        device = device + jnp.where(column >= j * rows, 1, 0)
    first = column + 3 * rows * device
    width = 384
    for at in range(0, full, width):
        f = lax.broadcasted_iota(jnp.int32, (half, width), 1) + at
        hit = f == first
        for k in range(1, 4):
            hit = jnp.logical_or(hit, f == first + k * rows)
        spread_ref[:, at : at + width] = jnp.where(hit, 1.0, 0.0).astype(BF16)
    f = lax.broadcasted_iota(jnp.int32, (1, full), 1)
    group = jnp.zeros((1, full), jnp.int32)
    for j in range(1, full // rows):
        group = group + jnp.where(f >= j * rows, 1, 0)
    row = lax.broadcasted_iota(jnp.int32, (8, full), 0)
    pick_ref[...] = jnp.where((group & 3) + 2 == row, 1.0, 0.0)
    small = gains_ref[...].astype(BF16)
    both = dot_nn(jnp.concatenate([small[:, : D // 2], small[:, D // 2 :]], axis=0), spread_ref[...])
    for part in range(2):
        picked = both[8 * part : 8 * part + 8] * pick_ref[...]
        bias_ref[:, part * (FF // 2) : (part + 1) * (FF // 2)] = jnp.sum(picked, axis=0, keepdims=True)


def k_du(plan, me, dz_ref, slope_a, slope_b, *refs):
    n = plan.pieces
    pieces, (du_ref, gb_ref, w_ref), (z_ref,) = refs[:n], refs[n : n + 3], refs[n + 3 :]
    tokens = dz_ref.shape[0]
    assemble_plain(plan.starts(me[0], plan.EARLY, FF), pieces, w_ref)
    wide = D
    slopes = (slope_a, slope_b)
    work = [(part, tile) for part in range(2) for tile in range(FF // 2 // wide)]

    def columns(step):
        part, tile = work[step]
        return pl.ds(pl.multiple_of(plan.half(me[0], part) * (FF // 2) + tile * wide, 128), wide)

    def project(step):
        z_ref[step % 2] = dot_nt(dz_ref[...], w_ref[columns(step), :])

    def scale(step):
        part, tile = work[step]
        cols = slice(tile * wide, (tile + 1) * wide)
        total = jnp.zeros((8, wide), F32)
        for at in range(0, tokens, 64):
            rows = slice(at, at + 64)
            du = (z_ref[step % 2, rows, :] * slopes[part][rows, cols]).astype(BF16)
            du_ref[rows, columns(step)] = du
            total = total + fold8(du.astype(F32))
        gb_ref[:, columns(step)] = jnp.sum(total, axis=0, keepdims=True)

    project(0)
    for step in range(len(work)):
        if step + 1 < len(work):
            project(step + 1)
        scale(step)


def half_columns(plan, me, part):
    return pl.ds(pl.multiple_of(plan.half(me, part) * (FF // 2), 128), FF // 2)


def k_result(plan, me, x2_ref, act_a, act_b, w_ref, out_ref, z_ref):
    z_ref[...] = dot_nn(act_a[...], w_ref[half_columns(plan, me[0], 0), :])
    z_ref[...] += dot_nn(act_b[...], w_ref[half_columns(plan, me[0], 1), :])

    def result(at):
        rows = pl.ds(at, STEP)
        z = z_ref[rows, :]
        out = (x2_ref[rows, :] + (z - jnp.mean(z, axis=1, keepdims=True))).astype(BF16)
        out_ref[rows, :] = out[:, : D - 1]

    row_loop(act_a.shape[0], STEP, result)


def k_mid(plan, me, cot_ref, x2_ref, gains_ref, du_ref, w_a, w_b, attnt_ref, dmid_ref, dy_ref, gg_ref, keep_ref, send_ref, dh_ref):
    tokens = cot_ref.shape[0]
    block = tokens // 2
    gain = gains_ref[1:2, :]

    def project(part):
        rows = slice(part * block, (part + 1) * block)
        first = dot_nt(du_ref[rows, half_columns(plan, me[0], 0)], w_a[...])
        dh_ref[rows, :] = first + dot_nt(du_ref[rows, half_columns(plan, me[0], 1)], w_b[...])

    def back(part, total):
        for at in range(part * block, (part + 1) * block, STEP):
            rows = slice(at, at + STEP)
            x2 = x2_ref[rows, :]
            dx, summand = norm_back(x2, inv_rms(x2), gain, dh_ref[rows, :])
            dmid = cot_ref[rows, :].astype(F32) + decomp_back(dx)
            dmid_ref[rows, :] = dmid
            dy_ref[rows, :] = (dmid - jnp.mean(dmid, axis=1, keepdims=True)).astype(BF16)
            total = total + fold8(summand)
        return total

    project(0)
    project(1)
    total = back(1, back(0, jnp.zeros((8, D), F32)))
    gg_ref[...] = jnp.sum(total, axis=0, keepdims=True)
    split_dot(attnt_ref, dy_ref, keep_ref, send_ref)


def k_attn_back(group, dy_ref, wo_ref, qkv_ref, ht_ref, *refs):
    *refs, da_ref = refs
    if group == 1:
        keep_o, send_o, *refs = refs
    dqkv_ref, keep_ref, *send_refs = refs
    if group == 1:
        keep_ref[:, :, 3 * HALF :] = keep_o[...]
        at = 0
        for ref in send_refs:
            ref[:, :, 3 * HALF :] = send_o[at : at + ref.shape[0]]
            at += ref.shape[0]
    tokens = dy_ref.shape[0]
    da_ref[...] = dot_nt(dy_ref[...], wo_ref[HALF * group : HALF * (group + 1), :]).astype(BF16)
    j_at = lax.broadcasted_iota(jnp.int32, (SEQ, SEQ), 0)
    i_at = lax.broadcasted_iota(jnp.int32, (SEQ, SEQ), 1)
    allowed = j_at <= i_at
    low = lax.broadcasted_iota(jnp.int32, (SEQ, 128), 1) < HD
    scale = HD ** -0.5

    def one(seq):
        rows = pl.ds(seq, SEQ)
        for pair in range(HALF // 128):
            cols = [slice(HALF * part + 128 * pair, HALF * part + 128 * (pair + 1)) for part in range(3)]
            q2, k2, v2 = (qkv_ref[rows, c] for c in cols)
            d2 = da_ref[rows, cols[0]]
            dq = dk = dv = None
            for side in range(2):
                mine = low if side == 0 else jnp.logical_not(low)
                q1, k1, v1, d1 = (jnp.where(mine, a, jnp.zeros_like(a)) for a in (q2, k2, v2, d2))
                scores = jnp.where(allowed, dot_nt(k1, q2) * scale, -1e30)
                top = jnp.max(scores, axis=0, keepdims=True)
                powers = jnp.exp(scores - top)
                probs = powers * (1.0 / jnp.sum(powers, axis=0, keepdims=True))
                dp = dot_nt(v1, d2)
                inner = jnp.sum(probs * dp, axis=0, keepdims=True)
                ds = (probs * (dp - inner)).astype(BF16)
                parts = (dot_tn(ds, k1), dot_nn(ds, q1), dot_nn(probs.astype(BF16), d1))
                dq, dk, dv = parts if dq is None else (dq + parts[0], dk + parts[1], dv + parts[2])
            dqkv_ref[rows, cols[0]] = (dq * scale).astype(BF16)
            dqkv_ref[rows, cols[1]] = (dk * scale).astype(BF16)
            dqkv_ref[rows, cols[2]] = dv.astype(BF16)

    for seq in range(0, tokens, SEQ):
        one(seq)
    split_dot(ht_ref, dqkv_ref, keep_ref, *send_refs)


def k_last(plan, me, resid_ref, dmid_ref, gains_ref, dq0_ref, w0_ref, dq1_ref, w1_ref, gg_ref, gb_ref, spread_ref, pick_ref, out_ref, keep_ref, send_ref, dh_ref, tail_ref):
    tokens = resid_ref.shape[0]
    block = tokens // 2
    gain = gains_ref[0:1, :]

    def project(part):
        rows = slice(part * block, (part + 1) * block)
        dh_ref[rows, :] = dot_nt(dq0_ref[rows, :], w0_ref[...]) + dot_nt(dq1_ref[rows, :], w1_ref[...])

    def back(part, total):
        for at in range(part * block, (part + 1) * block, STEP):
            rows = slice(at, at + STEP)
            x1 = decomp(resid_ref[rows, :].astype(F32))
            dx, summand = norm_back(x1, inv_rms(x1), gain, dh_ref[rows, :])
            out_ref[rows, :] = (dmid_ref[rows, :] + decomp_back(dx))[:, : D - 1]
            total = total + fold8(summand)
        return total

    project(0)
    project(1)
    total = back(1, back(0, jnp.zeros((8, D), F32)))
    ga = jnp.sum(total, axis=0, keepdims=True)
    g = jnp.concatenate([gb_ref[:, : FF // 2] * pick_ref[...], gb_ref[:, FF // 2 :] * pick_ref[...]], axis=0)
    high = g.astype(BF16)
    lower = (g - high.astype(F32)).astype(BF16)
    both = dot_nt(jnp.concatenate([high, lower], axis=0), spread_ref[...])
    biases = jnp.concatenate([both[:8] + both[16:24], both[8:16] + both[24:]], axis=1)
    row = lax.broadcasted_iota(jnp.int32, (8, D), 0)
    rows8 = jnp.where(row == 0, ga, jnp.where(row == 1, gg_ref[...], biases))
    high = rows8.astype(BF16).astype(F32)
    both = jnp.concatenate([high, rows8 - high, jnp.zeros((112, D), F32)], axis=0)
    tail_ref[...] = both.T
    starts = plan.starts(me[0], plan.SUM, D)
    if len(starts) == 1:
        keep_ref[0] = tail_ref[: D // 2, :].astype(BF16)
        send_ref[0] = tail_ref[D // 2 :, :].astype(BF16)
    else:
        half = len(starts) // 2
        rows = D // len(starts)
        for s, start in enumerate(starts):
            ref, at = (keep_ref, s) if s < half else (send_ref, s - half)
            ref[at] = tail_ref[pl.ds(pl.multiple_of(start, rows), rows), :].astype(BF16)


def renew(value):
    lane = lax.broadcasted_iota(jnp.int32, value.shape, 1)
    total = value + pltpu.roll(value, 120, 1)
    high = total.astype(BF16).astype(F32)
    lower = pltpu.roll(total - high, 8, 1)
    return jnp.where(lane < 8, high, jnp.where(lane < 16, lower, 0.0))


def add_blocks(tail, a, b):
    value = a.astype(F32) + b.astype(F32)
    if not tail:
        return value
    return jnp.concatenate([value[:, :-128], renew(value[:, -128:])], axis=1)


def k_sum_half(tail, keep_ref, *refs):
    *got, mine_ref, yours_ref = refs
    half = mine_ref.shape[0]
    for s in range(half):
        for ref, at in ((yours_ref, half + s), (mine_ref, s)):
            other, place = place_of(got, at)
            ref[s] = add_blocks(tail, keep_ref[at], other[place]).astype(BF16)


def k_sum_down(plan, me, *refs):
    keeps, gots, (mine_ref, yours_ref) = refs[:4], refs[4:8], refs[8:]
    first = ((me[0] >> plan.core) & 1) == 0
    for z2 in range(2):
        for z1 in range(2):
            for m1, out_ref in ((1, yours_ref), (0, mine_ref)):
                for m2 in range(2):
                    sums = []
                    for which in sorted({2 * z2 + z1, 2 * z1 + z2}):
                        sums.append(add_blocks(False, keeps[which][2 * m1 + m2], gots[which][2 * m1 + m2]))
                    if z1 != z2:
                        own, swapped = (sums[0], sums[1]) if z2 == 0 else (sums[1], sums[0])
                        sums = [jnp.where(first, own, swapped)]
                    out_ref[4 * z2 + 2 * z1 + m2] = sums[0].astype(BF16)


def k_sum_small(keep_ref, keep_t, got_t, *refs):
    *got, mine_ref, yours_ref = refs
    half = mine_ref.shape[0]
    width = keep_ref.shape[2]
    for s in range(2 * half):
        ref, at = (mine_ref, s) if s < half else (yours_ref, s - half)
        other, place = place_of(got, s)
        ref[at, :, :width] = add_blocks(False, keep_ref[s], other[place]).astype(BF16)
        ref[at, :, width:] = renew(add_blocks(False, keep_t[s], got_t[s])).astype(BF16)


def k_sum_four(keep_b, got_b, keep_a, got_a, own, one, two, three):
    width = keep_b.shape[2]
    for m, ref in enumerate((own, one, two, three)):
        ref[:, :width] = add_blocks(False, keep_b[m], got_b[m]).astype(ref.dtype)
        ref[:, width:] = add_blocks(True, keep_a[m], got_a[m]).astype(ref.dtype)


def k_final(n, *refs):
    parts, (qkv_ref, out_ref, b_ref, ga_ref, gm_ref) = refs[:n], refs[n:]
    rows = qkv_ref.shape[0]

    def total(start, width):
        value = parts[0][:, start : start + width]
        for part in parts[1:]:
            value = value + part[:, start : start + width].astype(F32)
        return value

    for part in range(3):
        for at, start in ((0, 3 * HALF + D), (HALF, 0)):
            qkv_ref[:, part * D + at : part * D + at + HALF] = total(start + part * HALF, HALF)
    out_ref[...] = total(3 * HALF, D)
    small = total(6 * HALF + D, 128)
    small = small + pltpu.roll(small, 120, 1)
    lane = lax.broadcasted_iota(jnp.int32, (rows, 128), 1)
    row = lax.broadcasted_iota(jnp.int32, (rows, 128), 0)

    def as_row(column, first):
        return jnp.sum(jnp.where(lane == row + first, small[:, column : column + 1], 0.0), axis=0, keepdims=True)

    ga_ref[...] = as_row(0, 0)[:, :rows]
    gm_ref[...] = as_row(1, 0)[:, :rows]
    b_ref[...] = sum(as_row(2 + k, k * rows) for k in range(4))[:, : 4 * rows]


def bits_of(count):
    return count.bit_length() - 1


SWAP = {"m1": "m2", "m2": "m1", "z1": "z2", "z2": "z1", "zl": "zl", "zh": "zh"}


class Plan:
    LATE = ("zl", "zh", "m1", "m2")
    EARLY = ("m1", "z1", "z2", "m2")
    SUM = ("z1", "z2", "m2", "m1")
    SUM_DOWN = ("m2", "z1", "z2", "m1")

    def __init__(self, mesh):
        self.wide, self.narrow = mesh.shape["wide"], mesh.shape["narrow"]
        self.count = self.wide * self.narrow
        self.low = bits_of(self.narrow)
        self.bits = bits_of(self.count)
        self.core = self.low
        outer = list(range(self.low + 1, self.bits))
        self.ys = list(range(self.low))
        self.x_bit, self.z_bits = outer[0], outer[1:]
        self.cm, self.xm, self.ym = 1 << self.core, 1 << self.x_bit, 1
        self.zl, self.zh = (1 << b for b in self.z_bits[:2])
        self.fine = (D // self.count) % 8 == 0 and self.low == 1 and len(self.z_bits) == 2
        self.pieces = 4 if self.fine else 1

    def index(self):
        return lax.axis_index("wide") * self.narrow + lax.axis_index("narrow")

    def send(self, value, mask, other=None):
        masks = [mask, mask if other is None else other]
        return lax.ppermute(value, AXES, [(i, i ^ masks[(i >> self.core) & 1]) for i in range(self.count)])

    def both(self, name):
        low = {"m1": self.xm, "m2": self.ym, "z1": self.zl, "z2": self.zh, "zl": self.zl, "zh": self.zh}
        return low[name], low[SWAP[name]]

    def exchange(self, name):
        return lambda value: self.send(value, *self.both(name))

    def mask(self, me, name):
        first, second = self.both(name)
        return first if first == second else jnp.where(((me >> self.core) & 1) == 0, first, second)

    def starts(self, me, bits, total):
        if not self.fine:
            return [0]
        masks = []
        for names, extra in ((bits, 0), ([SWAP[b] for b in bits], self.cm)):
            ways = [self.mask(me, name) for name in names]
            for block in range(1 << len(bits)):
                whole = extra
                for k, way in enumerate(ways):
                    if (block >> k) & 1:
                        whole = whole | way
                masks.append(whole)
        return [(me ^ m) * (total // self.count) for m in masks]

    def half(self, me, part):
        return ((me >> self.z_bits[1]) & 1) ^ part if self.fine else part

    def down_place(self, me, device):
        diff = (me ^ device) & (self.count // 2 - 1)
        other = (diff & self.cm) != 0
        at = jnp.where(other, 0, 8)
        at = at + jnp.where((diff & self.zl) != 0, 4, 0)
        for name, step in (("m1", 2), ("m2", 1)):
            way = jnp.where(other, self.mask(me, SWAP[name]), self.mask(me, name))
            at = at + jnp.where((diff & way) != 0, step, 0)
        return at

    def pair_up(self, own, other, bit, axis):
        mine = (self.index() >> bit) & 1
        return jnp.where(mine == 1, jnp.stack([other, own], axis), jnp.stack([own, other], axis))

    def gather_plain(self, shard):
        value, held = shard, []
        for b in self.z_bits + [self.x_bit] + self.ys + [self.core]:
            axis = sum(1 for h in held if h > b)
            value = self.pair_up(value, self.send(value, 1 << b), b, axis)
            held.append(b)
        return value.reshape(1, -1, shard.shape[1])

    def scatter_plain(self, keep, send, add):
        me = self.index()
        blocks = jnp.concatenate([keep[0], send[0]], 0)
        value = blocks.reshape((2,) * self.bits + (-1, blocks.shape[1]))
        held = list(range(self.bits - 1, -1, -1))
        for b in [self.core] + self.ys + [self.x_bit] + self.z_bits:
            axis, bit = held.index(b), (me >> b) & 1
            mine = lax.dynamic_index_in_dim(value, bit, axis, keepdims=False)
            yours = lax.dynamic_index_in_dim(value, 1 - bit, axis, keepdims=False)
            held.remove(b)
            value = add([mine, self.send(yours, 1 << b)], not held)
        return value


class Gather:
    def __init__(self, plan):
        self.plan, self.fine = plan, plan.fine

    def begin(self, blocks, name):
        if self.fine:
            self.a = blocks if blocks.ndim == 3 else blocks.reshape((1,) + blocks.shape)
            self.got = self.plan.exchange(name)(self.a)
        else:
            self.got = self.plan.gather_plain(blocks) if blocks.ndim == 2 else blocks

    def grow(self, name, waits=()):
        if self.fine:
            count, rows, columns = self.a.shape
            (self.a,) = call(k_join, [((2 * count, rows, columns), BF16)], self.a, self.got, waits=waits)
            self.got = self.plan.exchange(name)(self.a)

    def to_core(self, *after):
        self.near = [self.plan.send(fence(self.a, *after)[0] if after else self.a, self.plan.cm)] if self.fine else []

    def finish(self, *after):
        if self.fine:
            far = fence(self.got, *after)[0] if after else self.got
            return [self.a, self.got, *self.near, self.plan.send(far, self.plan.cm)]
        return [self.got]


def stack(plan, shard, got, widths, waits):
    if not plan.fine:
        cuts = [sum(widths[:i]) for i in range(len(widths) + 1)]
        return [got[:, :, i:j] for i, j in zip(cuts, cuts[1:])]
    return call(functools.partial(k_stack, 4), [((4, shard.shape[0], w), BF16) for w in widths], shard, *got, waits=waits)


class Scatter:
    def __init__(self, plan, keep, *sends):
        self.plan, self.fine, self.keep = plan, plan.fine, keep
        self.small = False
        if plan.fine:
            self.got = [plan.send(part, plan.cm) for part in sends]
        else:
            self.got = [plan.scatter_plain(keep, sends[0], add_plain)]

    def add_small(self, keep, send):
        if self.fine:
            self.small_parts = [keep, self.plan.send(send, self.plan.cm)]
        else:
            self.got.append(self.plan.scatter_plain(keep, send, add_two))

    def halve(self, name, waits=(), me=None):
        if not self.fine:
            return
        count, rows, columns = (self.keep[0] if isinstance(self.keep, list) else self.keep).shape
        if isinstance(self.keep, list):
            self.keep, yours = call(
                functools.partial(k_sum_down, self.plan), [((8, rows, columns), BF16)] * 2,
                me, *self.keep, *self.got, smem=1, waits=waits,
            )
            self.got = [self.plan.exchange(name)(yours)]
            return
        if not self.small and hasattr(self, "small_parts"):
            self.small = True
            body, columns = k_sum_small, columns + 128
            args = [self.keep, *self.small_parts, *self.got]
        else:
            body = functools.partial(k_sum_half, self.small)
            args = [self.keep, *self.got]
        self.keep, yours = call(body, [((count // 2, rows, columns), BF16)] * 2, *args, waits=waits)
        self.got = [self.plan.exchange(name)(yours)]

    def total(self):
        if not self.fine:
            return self.got[0]
        return self.keep[0].astype(F32) + self.got[0][0].astype(F32)


def finish_late(plan, sb, sa):
    if not plan.fine:
        small = sa.got[1]
        rest = jnp.zeros((small.shape[0], 120), F32)
        return [jnp.concatenate([sb.got[0], sa.got[0], small, rest], axis=1)]
    rows, width = sb.keep.shape[1:]
    whole = width + sa.keep.shape[2]
    own, *others = call(
        k_sum_four, [((rows, whole), F32)] + [((rows, whole), BF16)] * 3, sb.keep, sb.got[0], sa.keep, sa.got[0]
    )
    return [own, plan.exchange("z1")(others[0]), plan.exchange("z2")(others[1]), plan.send(others[2], plan.zl | plan.zh)]


def add_plain(arrived, last):
    total = arrived[0].astype(F32)
    for part in arrived[1:]:
        total = total + part.astype(F32)
    return total if last else total.astype(BF16)


def add_two(arrived, last):
    total = 0.0
    for part in arrived:
        whole = part.astype(F32)
        total = total + (whole[..., :8] + whole[..., 8:16])
    if last:
        return total
    high = lax.reduce_precision(total, 8, 7)
    rest = jnp.zeros(total.shape[:-1] + (112,), F32)
    return jnp.concatenate([high, total - high, rest], axis=-1).astype(BF16)


def fence(*values):
    return lax.optimization_barrier(values)


def device_step(plan, resid_in, w_qkv, w_out, w_up, b_up, w_down, gain_attn, gain_mlp, cotangent):
    rows = w_qkv.shape[0]
    t, d, half = resid_in.shape[0], D, D // 2
    wide3 = 3 * HALF
    CHAIN.clear()
    KEEP.clear()
    first = wide3 + 128
    fine = plan.fine
    me = plan.index().reshape(1)
    bind = lambda body: functools.partial(body, plan)
    turned = [pltpu.VMEM((d, t), F32)] * 2

    def blocks(r, columns, *pieces):
        if not fine:
            return [((1, half * r // rows, columns), BF16)] * 2
        return [((count, r, columns), BF16) for count in (16, *(pieces or (16,)))]

    a, b, u, v = (Gather(plan) for _ in range(4))
    u.begin(w_up, "m1")
    v.begin(w_down, "m1")
    (shard,) = call(
        k_pack, [((rows, first + wide3 + d), BF16)],
        w_qkv, w_out, jnp.concatenate([gain_attn, gain_mlp, b_up]).reshape(1, 6 * rows), free=True,
        scratch=[pltpu.VMEM(shape, BF16) for shape in ((rows, 3 * d), (rows, d), (1, 6 * rows))]
        + [pltpu.SemaphoreType.DMA((3,))],
    )
    got = [plan.send(shard, m) for m in (plan.zl, plan.zh, plan.zl | plan.zh)] if fine else plan.gather_plain(shard)
    resid, cot, dz = call(k_prep, [((t, d), BF16)] * 3, resid_in, cotangent, waits=[me])
    four_a, four_b = stack(plan, shard, got, (first, wide3 + d), [u.got, v.got])
    KEEP.append(resid)
    a.begin(four_a, "m1")
    b.begin(four_b, "m1")
    u.grow("z1")
    v.grow("z1")
    a.grow("m2", [b.got, u.got, v.got])
    KEEP.extend([a.a] if fine else [])
    b.grow("m2")
    KEEP.extend([b.a] if fine else [])
    u.grow("z2")
    a.to_core()
    b.to_core()
    u.grow("m2", [a.got, b.got, *a.near, *b.near])
    u.to_core()
    KEEP.extend([*a.near, *b.near])
    v.grow("z2")
    a_pieces, b_pieces = a.finish(), b.finish()
    qkv0, w0, h1, gains = call(
        bind(k_qkv),
        [((t, wide3), BF16), ((d, wide3), BF16), ((t, d), BF16), ((8, d), F32)],
        me, resid, *a_pieces,
        scratch=[pltpu.VMEM((d, 128), BF16), pltpu.VMEM((d, half), F32)], smem=1, waits=b_pieces[-1:],
    )
    KEEP[:] = [resid, b.a, *b.near] if fine else [resid]
    (attn0,) = call(k_attn, [((t, HALF), BF16)], qkv0)
    qkv1, w1, wo, attn, x2, h2 = call(
        bind(k_second),
        [((t, wide3), BF16), ((d, wide3), BF16), ((d, d), BF16), ((t, d), BF16), ((t, d), F32), ((t, d), BF16)],
        me, resid, h1, attn0, gains, *b_pieces,
        scratch=[pltpu.VMEM((d, half), F32)], smem=1,
    )
    KEEP.clear()
    bias, spread, pick = call(
        functools.partial(k_bias, rows), [((1, FF), F32), ((half, 4 * half), BF16), ((8, 4 * half), F32)], gains
    )
    v.grow("m2", [u.got, *u.near])
    v.to_core(CHAIN[-1])
    u_pieces = u.finish(h2)
    ups = []
    for part in range(2):
        grads = [((4, 4 * rows, d), BF16)] * 4 if fine else [((1, FF // 2, d), BF16)]
        ups.append(call(
            functools.partial(k_up, plan, part),
            [((d, FF // 2), BF16), ((t, FF // 2), BF16), ((t, FF // 2), F32)] + grads,
            me, h2, bias, dz, *u_pieces,
            scratch=[pltpu.VMEM((2, t // 2, d), F32), pltpu.VMEM((d, half), F32), pltpu.VMEM((FF // 2, t), BF16)],
            smem=1, waits=v.near if part else (),
        ))
    wu, act, slope = ([up[i] for up in ups] for i in range(3))
    if fine:
        sv = Scatter(plan, [part for up in ups for part in up[5:7]], *[part for up in ups for part in up[3:5]])
    else:
        sv = Scatter(plan, ups[0][3], ups[1][3])
    h1t, attnt, h2t = call(bind(k_turn), [((d, t), BF16)] * 3, me, h1, attn, h2, scratch=turned, smem=1)
    sv.halve("m1", me=me)
    du, gb, w_down_all = call(
        bind(k_du),
        [((t, FF), BF16), ((1, FF), F32), ((FF, d), BF16)],
        me, dz, *slope, *v.finish(*([sv.keep] if fine else [])), scratch=[pltpu.VMEM((2, t, d), F32)], smem=1,
    )
    su = Scatter(plan, *call(split_dot, blocks(rows, FF, 4, 4, 4, 4), h2t, du))
    dmid, dy, gg, keep_o, send_o = call(
        bind(k_mid),
        [((t, d), F32), ((t, d), BF16), ((1, d), F32)] + blocks(rows, d),
        me, cot, x2, gains, du, *wu, attnt,
        scratch=[pltpu.VMEM((t, d), F32)], smem=1,
    )
    su.halve("m1")
    sv.halve("z2")
    back_scratch = [pltpu.VMEM((t, HALF), BF16)]
    dqkv1, *parts = call(
        functools.partial(k_attn_back, 1), [((t, wide3), BF16)] + blocks(rows, wide3 + d, 6, 5, 5),
        dy, wo, qkv1, h1t, keep_o, send_o, scratch=back_scratch,
    )
    sb = Scatter(plan, *parts)
    dqkv0, *parts = call(
        functools.partial(k_attn_back, 0), [((t, wide3), BF16)] + blocks(rows, wide3, 8, 8),
        dy, wo, qkv0, h1t, scratch=back_scratch,
    )
    sa = Scatter(plan, *parts)
    sb.halve("m1")
    su.halve("m2")
    dres, *parts = call(
        bind(k_last),
        [((t, d - 1), F32)] + blocks(rows, 128),
        me, resid, dmid, gains, dqkv0, w0, dqkv1, w1, gg, gb, spread, pick,
        scratch=[pltpu.VMEM((t, d), F32), pltpu.VMEM((d, 128), F32)], smem=1,
    )
    sa.add_small(*parts)
    sv.halve("z1")
    sa.halve("m1")
    (out,) = call(
        bind(k_result), [((t, d - 1), BF16)], me, x2, *act, w_down_all, scratch=[pltpu.VMEM((t, d), F32)], smem=1
    )
    su.halve("z2")
    sb.halve("m2")
    sa.halve("m2")
    sv.halve("m2")
    su.halve("z1")
    late = finish_late(plan, sb, sa)
    s_down, s_up = sv.total(), su.total()
    s_qkv, s_out, s_b, s_a, s_m = call(
        functools.partial(k_final, len(late)),
        [((rows, 3 * d), F32), ((rows, d), F32), ((1, 4 * rows), F32), ((1, rows), F32), ((1, rows), F32)],
        *late,
    )
    return (out, dres, s_qkv, s_out, s_up, s_b.reshape(4 * rows), s_down, s_a.reshape(rows), s_m.reshape(rows))


def solution(mesh):
    rows2, rows1 = P(AXES, None), P(AXES)
    in_specs = (rows2, rows2, rows2, rows2, rows1, rows2, rows1, rows1, rows2)
    out_specs = (rows2, rows2, rows2, rows2, rows2, rows1, rows2, rows1, rows1)
    plan = Plan(mesh)

    def on_device(*arrays):
        return device_step(plan, *arrays)

    return jax.shard_map(on_device, mesh=mesh, in_specs=in_specs, out_specs=out_specs, check_vma=False)
```

```python
import functools
import math

import jax
import jax.numpy as jnp
from jax import lax
from jax.experimental import pallas as pl
from jax.experimental.pallas import tpu as pltpu
from jax.sharding import PartitionSpec as P

D = 768
H = 12
HD = 64
FF = 3072
SEQ = 256
HALF = 384
EPS = 1e-05
AXES = ("wide", "narrow")
F32 = jnp.float32
BF16 = jnp.bfloat16
MIB = 1 << 20
LIMIT = 12

VMEM_SPEC = pl.BlockSpec(memory_space=pltpu.VMEM)
SMEM_SPEC = pl.BlockSpec(memory_space=pltpu.SMEM)
ANY_SPEC = pl.BlockSpec(memory_space=pl.ANY)
HBM_SPEC = pl.BlockSpec(memory_space=pltpu.HBM)


def dot_nn(a, b):
    return lax.dot_general(a, b, (((1,), (0,)), ((), ())), preferred_element_type=F32)


def dot_nt(a, b):
    return lax.dot_general(a, b, (((1,), (1,)), ((), ())), preferred_element_type=F32)


def dot_tn(a, b):
    return lax.dot_general(a, b, (((0,), (0,)), ((), ())), preferred_element_type=F32)


STEP = 128


def last_lane(shape):
    return lax.broadcasted_iota(jnp.int32, shape, 1) == D - 1


def decomp(padded):
    total = jnp.sum(padded, axis=1, keepdims=True)
    return jnp.where(last_lane(padded.shape), -total, padded)


def inv_rms(values):
    return lax.rsqrt(jnp.mean(values * values, axis=1, keepdims=True) + EPS)


def norm_back(x, r, gain, dh):
    xdh = x * dh
    dx = r * (gain * dh) - x * (r * r * r) * jnp.mean(xdh * gain, axis=1, keepdims=True)
    return dx, xdh * r


def decomp_back(dx):
    return dx - dx[:, D - 1 :]


KEEP = []
CHAIN = []


def call(body, outs, *args, scratch=(), limit=LIMIT, smem=0, waits=(), free=False, far=False):
    wait = CHAIN[-1:] + list(waits)
    wait += [k for k in KEEP if not any(k is x for x in (*args, *wait))]
    specs = [SMEM_SPEC] * smem + [ANY_SPEC if free else VMEM_SPEC] * (len(args) - smem) + [ANY_SPEC] * len(wait)

    def run(*refs):
        body(*refs[: len(args)], *refs[len(args) + len(wait) :])

    results = pl.pallas_call(
        run,
        out_shape=[jax.ShapeDtypeStruct(s, d) for s, d in outs],
        in_specs=specs,
        out_specs=[HBM_SPEC if far else VMEM_SPEC] * len(outs),
        scratch_shapes=list(scratch),
        compiler_params=pltpu.CompilerParams(vmem_limit_bytes=limit * MIB),
        cost_estimate=pl.CostEstimate(flops=1000, bytes_accessed=1000, transcendentals=0),
    )(*args, *wait)
    CHAIN.append(min(results, key=lambda r: r.size * r.dtype.itemsize))
    return results


def assemble_plain(starts, pieces, out_ref):
    at = 0
    for ref in pieces:
        count, rows, _ = ref.shape
        for m in range(count):
            out_ref[pl.ds(pl.multiple_of(starts[at], rows), rows), :] = ref[m]
            at += 1


def assemble(starts, pieces, out_refs, wide_ref, column=0):
    for out_ref in out_refs:
        for begin in range(0, out_ref.shape[1], wide_ref.shape[1]):
            width = min(wide_ref.shape[1], out_ref.shape[1] - begin)
            at = 0
            for ref in pieces:
                count, rows, _ = ref.shape
                for m in range(count):
                    cols = pl.ds(column + begin, width)
                    if not isinstance(column, int):
                        cols = pl.ds(pl.multiple_of(column + begin, 128), width)
                    block = ref[m, :, cols].astype(F32)
                    wide_ref[pl.ds(pl.multiple_of(starts[at], rows), rows), :width] = block
                    at += 1
            out_ref[:, begin : begin + width] = wide_ref[:, :width].astype(BF16)
        column += out_ref.shape[1]


def turn(starts, value, out_ref, t_ref, r_ref):
    turned = value.astype(F32).T
    if len(starts) == 1:
        out_ref[...] = turned.astype(BF16)
        return
    t_ref[...] = turned
    rows = turned.shape[0] // len(starts)
    for s, start in enumerate(starts):
        r_ref[rows * s : rows * (s + 1), :] = t_ref[pl.ds(pl.multiple_of(start, rows), rows), :]
    out_ref[...] = r_ref[...].astype(BF16)


def row_loop(total, step, body):
    def go(i, carry):
        body(pl.multiple_of(i * step, step))
        return carry

    lax.fori_loop(0, total // step, go, 0)


def fold8(rows):
    total = rows[0:8]
    for at in range(8, rows.shape[0], 8):
        total = total + rows[at : at + 8]
    return total


def column_of(row, first, count):
    r_at = lax.broadcasted_iota(jnp.int32, (count, row.shape[1]), 0)
    c_at = lax.broadcasted_iota(jnp.int32, (count, row.shape[1]), 1)
    return jnp.sum(jnp.where(c_at == r_at + first, row, 0.0), axis=1, keepdims=True)


def k_pack(w_any, wo_any, small_any, out_ref, w_ref, wo_ref, small_ref, sems):
    refs = ((w_any, w_ref), (wo_any, wo_ref), (small_any, small_ref))
    copies = [pltpu.make_async_copy(a, b, sems.at[i]) for i, (a, b) in enumerate(refs)]
    for copy in copies:
        copy.start()
    for copy in copies:
        copy.wait()
    rows = w_ref.shape[0]
    for group, start in ((0, 0), (1, 3 * HALF + 128)):
        for part in range(3):
            at = part * D + group * HALF
            out_ref[:, start + part * HALF : start + (part + 1) * HALF] = w_ref[:, at : at + HALF]
    out_ref[:, 6 * HALF + 128 :] = wo_ref[...]
    row = small_ref[...].astype(F32)
    columns = [column_of(row, k * rows, rows) for k in range(6)]
    lane = lax.broadcasted_iota(jnp.int32, (rows, 128), 1)
    small = jnp.zeros((rows, 128), F32)
    for at, column in enumerate(columns):
        small = jnp.where(lane == at, column, small)
    out_ref[:, 3 * HALF : 3 * HALF + 128] = small.astype(BF16)


def k_stack(n, *refs):
    for at, ref in enumerate(refs[:n]):
        start = 0
        for out_ref in refs[n:]:
            out_ref[at] = ref[:, start : start + out_ref.shape[2]]
            start += out_ref.shape[2]


def k_join(first_ref, second_ref, out_ref):
    half = first_ref.shape[0]
    out_ref[:half] = first_ref[...]
    out_ref[half:] = second_ref[...]


def k_qkv(plan, me, resid_ref, *refs):
    n = plan.pieces
    pieces, (qkv_ref, w_ref, h_ref, gains_ref), (tail_ref, wide) = refs[:n], refs[n : n + 4], refs[n + 4 :]
    tokens = resid_ref.shape[0]
    assemble(plan.starts(me[0], plan.LATE, D), pieces, (w_ref, tail_ref), wide)
    tail = tail_ref[...].astype(F32).T
    gains_ref[...] = tail[:8, :]
    gain = tail[0:1, :]

    def norm(at):
        rows = pl.ds(at, STEP)
        x1 = decomp(resid_ref[rows, :].astype(F32))
        h_ref[rows, :] = (x1 * inv_rms(x1) * gain).astype(BF16)

    row_loop(tokens, STEP, norm)
    qkv_ref[...] = dot_nn(h_ref[...], w_ref[...]).astype(BF16)


def attend(qkv_ref, attn_ref, tokens, out_at):
    i_at = lax.broadcasted_iota(jnp.int32, (SEQ, SEQ), 0)
    j_at = lax.broadcasted_iota(jnp.int32, (SEQ, SEQ), 1)
    allowed = j_at <= i_at
    low = lax.broadcasted_iota(jnp.int32, (SEQ, 128), 1) < HD

    def one(seq):
        rows = pl.ds(seq, SEQ)
        for pair in range(HALF // 128):
            cols = slice(128 * pair, 128 * (pair + 1))
            q2 = qkv_ref[rows, cols]
            k2 = qkv_ref[rows, HALF + 128 * pair : HALF + 128 * (pair + 1)]
            v2 = qkv_ref[rows, 2 * HALF + 128 * pair : 2 * HALF + 128 * (pair + 1)]
            mixed = None
            for side in range(2):
                mine = low if side == 0 else jnp.logical_not(low)
                k_one = jnp.where(mine, k2, jnp.zeros_like(k2))
                v_one = jnp.where(mine, v2, jnp.zeros_like(v2))
                scores = jnp.where(allowed, dot_nt(q2, k_one) * (HD ** -0.5), -1e30)
                top = jnp.max(scores, axis=1, keepdims=True)
                powers = jnp.exp(scores - top)
                total = jnp.sum(powers, axis=1, keepdims=True)
                probs = (powers * (1.0 / total)).astype(BF16)
                part = dot_nn(probs, v_one)
                mixed = part if mixed is None else mixed + part
            attn_ref[rows, out_at + 128 * pair : out_at + 128 * (pair + 1)] = mixed.astype(BF16)

    row_loop(tokens, SEQ, one)


def k_attn(qkv_ref, attn_ref):
    attend(qkv_ref, attn_ref, qkv_ref.shape[0], 0)


def k_turn(plan, me, h_ref, attn_ref, h2_ref, ht_ref, attnt_ref, h2t_ref, t_ref, r_ref):
    starts = plan.starts(me[0], plan.SUM, D)
    for ref, out_ref in ((h_ref, ht_ref), (attn_ref, attnt_ref), (h2_ref, h2t_ref)):
        turn(starts, ref[...], out_ref, t_ref, r_ref)


def k_second(plan, me, resid_ref, h_ref, attn0_ref, gains_ref, *refs):
    n = plan.pieces
    pieces, (qkv_ref, w_ref, wo_ref, attn_ref, x2_ref, h2_ref), (wide,) = refs[:n], refs[n : n + 6], refs[n + 6 :]
    tokens = resid_ref.shape[0]
    assemble(plan.starts(me[0], plan.LATE, D), pieces, (w_ref, wo_ref), wide)
    qkv_ref[...] = dot_nn(h_ref[...], w_ref[...]).astype(BF16)
    attn_ref[:, :HALF] = attn0_ref[...]
    attend(qkv_ref, attn_ref, tokens, HALF)
    gain = gains_ref[1:2, :]
    x2_ref[...] = dot_nn(attn_ref[...], wo_ref[...])

    def norm(at):
        rows = pl.ds(at, STEP)
        y = x2_ref[rows, :]
        middle = resid_ref[rows, :].astype(F32) + (y - jnp.mean(y, axis=1, keepdims=True))
        x2 = decomp(jnp.where(last_lane(middle.shape), 0.0, middle))
        x2_ref[rows, :] = x2
        h2_ref[rows, :] = (x2 * inv_rms(x2) * gain).astype(BF16)

    row_loop(tokens, STEP, norm)


GELU_A = math.sqrt(2.0 / math.pi)
GELU_B = 0.044715


def k_up(plan, part, me, h2_ref, bias_ref, dz_ref, *refs):
    n = plan.pieces
    pieces, refs = refs[:n], refs[n:]
    (w_ref, act_ref, slope_ref), grad_refs, (u_ref, wide_ref, actt_ref) = refs[:3], refs[3:-3], refs[-3:]
    tokens = h2_ref.shape[0]
    wide = D
    start = plan.half(me[0], part) * (FF // 2)
    assemble(plan.starts(me[0], plan.EARLY, D), pieces, (w_ref,), wide_ref, start)
    block = tokens // 2
    work = [(tile, half) for tile in range(FF // 2 // wide) for half in range(2)]

    def project(step):
        tile, half = work[step]
        u_ref[step % 2] = dot_nn(h2_ref[half * block : (half + 1) * block, :], w_ref[:, tile * wide : (tile + 1) * wide])

    def gelu(step):
        tile, half = work[step]
        cols = slice(tile * wide, (tile + 1) * wide)
        bias = bias_ref[:, pl.ds(pl.multiple_of(start + tile * wide, 128), wide)]
        for at in range(0, block, 64):
            rows = slice(half * block + at, half * block + at + 64)
            u = u_ref[step % 2, at : at + 64, :] + bias
            square = u * u
            t = jnp.tanh(u * (GELU_A + (GELU_A * GELU_B) * square))
            middle = 0.5 * t + 0.5
            act_ref[rows, cols] = (u * middle).astype(BF16)
            slope = middle + (u * (0.5 - 0.5 * (t * t))) * (GELU_A + (3.0 * GELU_A * GELU_B) * square)
            slope_ref[rows, cols] = slope

    project(0)
    for step in range(len(work)):
        if step + 1 < len(work):
            project(step + 1)
        gelu(step)
    for tile in range(FF // 2 // wide):
        cols = slice(tile * wide, (tile + 1) * wide)
        turned = act_ref[:, cols].T
        if not plan.fine:
            actt_ref[cols, :] = turned
            continue
        rows = FF // plan.count
        for b in range(wide // rows):
            to = pl.multiple_of(plan.down_place(me[0], tile * (wide // rows) + b) * rows, rows)
            actt_ref[pl.ds(to, rows), :] = turned[b * rows : (b + 1) * rows, :]
    at = 0
    for ref in grad_refs:
        count, rows, _ = ref.shape
        for begin in range(0, count * rows, 384):
            product = dot_nn(actt_ref[at + begin : at + begin + 384, :], dz_ref[...]).astype(BF16)
            if rows > 384:
                ref[0, begin : begin + 384, :] = product
            else:
                for j in range(384 // rows):
                    ref[begin // rows + j] = product[j * rows : (j + 1) * rows]
        at += count * rows


def place_of(refs, at):
    for ref in refs:
        if at < ref.shape[0]:
            return ref, at
        at -= ref.shape[0]


def split_dot(left_ref, right_ref, keep_ref, *send_refs):
    half = left_ref.shape[0] // 2
    width = right_ref.shape[1]
    _, rows, _ = keep_ref.shape
    for refs, start in ((send_refs, half), ((keep_ref,), 0)):
        for at in range(0, half, 384):
            part = dot_nn(left_ref[start + at : start + at + 384, :], right_ref[...]).astype(BF16)
            if rows > 384:
                refs[0][0, at : at + 384, :width] = part
                continue
            for j in range(384 // rows):
                ref, place = place_of(refs, at // rows + j)
                ref[place, :, :width] = part[j * rows : (j + 1) * rows]


def k_prep(resid_in, cot_in, resid_ref, cot_ref, dz_ref):
    for ref, source in ((resid_ref, resid_in), (cot_ref, cot_in)):
        ref[:, D - 128 :] = jnp.zeros((ref.shape[0], 128), BF16)
        ref[:, : D - 1] = source[...]

    def go(at):
        at_rows = pl.ds(at, STEP)
        c = cot_ref[at_rows, :].astype(F32)
        dz_ref[at_rows, :] = (c - jnp.mean(c, axis=1, keepdims=True)).astype(BF16)

    row_loop(cot_ref.shape[0], STEP, go)


def k_bias(rows, gains_ref, bias_ref, spread_ref, pick_ref):
    half, full = spread_ref.shape
    column = lax.broadcasted_iota(jnp.int32, (half, 1), 0)
    device = jnp.zeros((half, 1), jnp.int32)
    for j in range(1, half // rows):
        device = device + jnp.where(column >= j * rows, 1, 0)
    first = column + 3 * rows * device
    width = 384
    for at in range(0, full, width):
        f = lax.broadcasted_iota(jnp.int32, (half, width), 1) + at
        hit = f == first
        for k in range(1, 4):
            hit = jnp.logical_or(hit, f == first + k * rows)
        spread_ref[:, at : at + width] = jnp.where(hit, 1.0, 0.0).astype(BF16)
    f = lax.broadcasted_iota(jnp.int32, (1, full), 1)
    group = jnp.zeros((1, full), jnp.int32)
    for j in range(1, full // rows):
        group = group + jnp.where(f >= j * rows, 1, 0)
    row = lax.broadcasted_iota(jnp.int32, (8, full), 0)
    pick_ref[...] = jnp.where((group & 3) + 2 == row, 1.0, 0.0)
    small = gains_ref[...].astype(BF16)
    both = dot_nn(jnp.concatenate([small[:, : D // 2], small[:, D // 2 :]], axis=0), spread_ref[...])
    for part in range(2):
        picked = both[8 * part : 8 * part + 8] * pick_ref[...]
        bias_ref[:, part * (FF // 2) : (part + 1) * (FF // 2)] = jnp.sum(picked, axis=0, keepdims=True)


def k_du(plan, me, dz_ref, slope_a, slope_b, *refs):
    n = plan.pieces
    pieces, (du_ref, gb_ref, w_ref), (z_ref,) = refs[:n], refs[n : n + 3], refs[n + 3 :]
    tokens = dz_ref.shape[0]
    assemble_plain(plan.starts(me[0], plan.EARLY, FF), pieces, w_ref)
    wide = D
    slopes = (slope_a, slope_b)
    work = [(part, tile) for part in range(2) for tile in range(FF // 2 // wide)]

    def columns(step):
        part, tile = work[step]
        return pl.ds(pl.multiple_of(plan.half(me[0], part) * (FF // 2) + tile * wide, 128), wide)

    def project(step):
        z_ref[step % 2] = dot_nt(dz_ref[...], w_ref[columns(step), :])

    def scale(step):
        part, tile = work[step]
        cols = slice(tile * wide, (tile + 1) * wide)
        total = jnp.zeros((8, wide), F32)
        for at in range(0, tokens, 64):
            rows = slice(at, at + 64)
            du = (z_ref[step % 2, rows, :] * slopes[part][rows, cols]).astype(BF16)
            du_ref[rows, columns(step)] = du
            total = total + fold8(du.astype(F32))
        gb_ref[:, columns(step)] = jnp.sum(total, axis=0, keepdims=True)

    project(0)
    for step in range(len(work)):
        if step + 1 < len(work):
            project(step + 1)
        scale(step)


def half_columns(plan, me, part):
    return pl.ds(pl.multiple_of(plan.half(me, part) * (FF // 2), 128), FF // 2)


def k_result(plan, me, x2_ref, act_a, act_b, w_ref, out_any, z_ref, out_ref, sem):
    z_ref[...] = dot_nn(act_a[...], w_ref[half_columns(plan, me[0], 0), :])
    z_ref[...] += dot_nn(act_b[...], w_ref[half_columns(plan, me[0], 1), :])

    def result(at):
        rows = pl.ds(at, STEP)
        z = z_ref[rows, :]
        out = (x2_ref[rows, :] + (z - jnp.mean(z, axis=1, keepdims=True))).astype(BF16)
        out_ref[rows, :] = out[:, : D - 1]

    row_loop(act_a.shape[0], STEP, result)
    copy = pltpu.make_async_copy(out_ref, out_any, sem)
    copy.start()
    copy.wait()


def k_mid(plan, me, cot_ref, x2_ref, gains_ref, du_ref, w_a, w_b, attnt_ref, dmid_ref, dy_ref, gg_ref, keep_ref, send_ref, dh_ref):
    tokens = cot_ref.shape[0]
    block = tokens // 2
    gain = gains_ref[1:2, :]

    def project(part):
        rows = slice(part * block, (part + 1) * block)
        first = dot_nt(du_ref[rows, half_columns(plan, me[0], 0)], w_a[...])
        dh_ref[rows, :] = first + dot_nt(du_ref[rows, half_columns(plan, me[0], 1)], w_b[...])

    def back(part, total):
        for at in range(part * block, (part + 1) * block, STEP):
            rows = slice(at, at + STEP)
            x2 = x2_ref[rows, :]
            dx, summand = norm_back(x2, inv_rms(x2), gain, dh_ref[rows, :])
            dmid = cot_ref[rows, :].astype(F32) + decomp_back(dx)
            dmid_ref[rows, :] = dmid
            dy_ref[rows, :] = (dmid - jnp.mean(dmid, axis=1, keepdims=True)).astype(BF16)
            total = total + fold8(summand)
        return total

    project(0)
    project(1)
    total = back(1, back(0, jnp.zeros((8, D), F32)))
    gg_ref[...] = jnp.sum(total, axis=0, keepdims=True)
    split_dot(attnt_ref, dy_ref, keep_ref, send_ref)


def k_attn_back(group, dy_ref, wo_ref, qkv_ref, ht_ref, *refs):
    *refs, da_ref = refs
    if group == 1:
        keep_o, send_o, *refs = refs
    dqkv_ref, keep_ref, *send_refs = refs
    if group == 1:
        keep_ref[:, :, 3 * HALF :] = keep_o[...]
        at = 0
        for ref in send_refs:
            ref[:, :, 3 * HALF :] = send_o[at : at + ref.shape[0]]
            at += ref.shape[0]
    tokens = dy_ref.shape[0]
    da_ref[...] = dot_nt(dy_ref[...], wo_ref[HALF * group : HALF * (group + 1), :]).astype(BF16)
    j_at = lax.broadcasted_iota(jnp.int32, (SEQ, SEQ), 0)
    i_at = lax.broadcasted_iota(jnp.int32, (SEQ, SEQ), 1)
    allowed = j_at <= i_at
    low = lax.broadcasted_iota(jnp.int32, (SEQ, 128), 1) < HD
    scale = HD ** -0.5

    def one(seq):
        rows = pl.ds(seq, SEQ)
        for pair in range(HALF // 128):
            cols = [slice(HALF * part + 128 * pair, HALF * part + 128 * (pair + 1)) for part in range(3)]
            q2, k2, v2 = (qkv_ref[rows, c] for c in cols)
            d2 = da_ref[rows, cols[0]]
            dq = dk = dv = None
            for side in range(2):
                mine = low if side == 0 else jnp.logical_not(low)
                q1, k1, v1, d1 = (jnp.where(mine, a, jnp.zeros_like(a)) for a in (q2, k2, v2, d2))
                scores = jnp.where(allowed, dot_nt(k1, q2) * scale, -1e30)
                top = jnp.max(scores, axis=0, keepdims=True)
                powers = jnp.exp(scores - top)
                probs = powers * (1.0 / jnp.sum(powers, axis=0, keepdims=True))
                dp = dot_nt(v1, d2)
                inner = jnp.sum(probs * dp, axis=0, keepdims=True)
                ds = (probs * (dp - inner)).astype(BF16)
                parts = (dot_tn(ds, k1), dot_nn(ds, q1), dot_nn(probs.astype(BF16), d1))
                dq, dk, dv = parts if dq is None else (dq + parts[0], dk + parts[1], dv + parts[2])
            dqkv_ref[rows, cols[0]] = (dq * scale).astype(BF16)
            dqkv_ref[rows, cols[1]] = (dk * scale).astype(BF16)
            dqkv_ref[rows, cols[2]] = dv.astype(BF16)

    for seq in range(0, tokens, SEQ):
        one(seq)
    split_dot(ht_ref, dqkv_ref, keep_ref, *send_refs)


def k_last(plan, me, resid_ref, dmid_ref, gains_ref, dq0_ref, w0_ref, dq1_ref, w1_ref, gg_ref, gb_ref, spread_ref, pick_ref, out_ref, keep_ref, send_ref, dh_ref, tail_ref):
    tokens = resid_ref.shape[0]
    block = tokens // 2
    gain = gains_ref[0:1, :]

    def project(part):
        rows = slice(part * block, (part + 1) * block)
        dh_ref[rows, :] = dot_nt(dq0_ref[rows, :], w0_ref[...]) + dot_nt(dq1_ref[rows, :], w1_ref[...])

    def back(part, total):
        for at in range(part * block, (part + 1) * block, STEP):
            rows = slice(at, at + STEP)
            x1 = decomp(resid_ref[rows, :].astype(F32))
            dx, summand = norm_back(x1, inv_rms(x1), gain, dh_ref[rows, :])
            out_ref[rows, :] = (dmid_ref[rows, :] + decomp_back(dx))[:, : D - 1]
            total = total + fold8(summand)
        return total

    project(0)
    project(1)
    total = back(1, back(0, jnp.zeros((8, D), F32)))
    ga = jnp.sum(total, axis=0, keepdims=True)
    g = jnp.concatenate([gb_ref[:, : FF // 2] * pick_ref[...], gb_ref[:, FF // 2 :] * pick_ref[...]], axis=0)
    high = g.astype(BF16)
    lower = (g - high.astype(F32)).astype(BF16)
    both = dot_nt(jnp.concatenate([high, lower], axis=0), spread_ref[...])
    biases = jnp.concatenate([both[:8] + both[16:24], both[8:16] + both[24:]], axis=1)
    row = lax.broadcasted_iota(jnp.int32, (8, D), 0)
    rows8 = jnp.where(row == 0, ga, jnp.where(row == 1, gg_ref[...], biases))
    high = rows8.astype(BF16).astype(F32)
    both = jnp.concatenate([high, rows8 - high, jnp.zeros((112, D), F32)], axis=0)
    tail_ref[...] = both.T
    starts = plan.starts(me[0], plan.SUM, D)
    if len(starts) == 1:
        keep_ref[0] = tail_ref[: D // 2, :].astype(BF16)
        send_ref[0] = tail_ref[D // 2 :, :].astype(BF16)
    else:
        half = len(starts) // 2
        rows = D // len(starts)
        for s, start in enumerate(starts):
            ref, at = (keep_ref, s) if s < half else (send_ref, s - half)
            ref[at] = tail_ref[pl.ds(pl.multiple_of(start, rows), rows), :].astype(BF16)


def renew(value):
    lane = lax.broadcasted_iota(jnp.int32, value.shape, 1)
    total = value + pltpu.roll(value, 120, 1)
    high = total.astype(BF16).astype(F32)
    lower = pltpu.roll(total - high, 8, 1)
    return jnp.where(lane < 8, high, jnp.where(lane < 16, lower, 0.0))


def add_blocks(tail, a, b):
    value = a.astype(F32) + b.astype(F32)
    if not tail:
        return value
    return jnp.concatenate([value[:, :-128], renew(value[:, -128:])], axis=1)


def k_sum_half(tail, keep_ref, *refs):
    *got, mine_ref, yours_ref = refs
    half = mine_ref.shape[0]
    for s in range(half):
        for ref, at in ((yours_ref, half + s), (mine_ref, s)):
            other, place = place_of(got, at)
            ref[s] = add_blocks(tail, keep_ref[at], other[place]).astype(BF16)


def k_sum_down(plan, me, *refs):
    keeps, gots, (mine_ref, yours_ref) = refs[:4], refs[4:8], refs[8:]
    first = ((me[0] >> plan.core) & 1) == 0
    for z2 in range(2):
        for z1 in range(2):
            for m1, out_ref in ((1, yours_ref), (0, mine_ref)):
                for m2 in range(2):
                    sums = []
                    for which in sorted({2 * z2 + z1, 2 * z1 + z2}):
                        sums.append(add_blocks(False, keeps[which][2 * m1 + m2], gots[which][2 * m1 + m2]))
                    if z1 != z2:
                        own, swapped = (sums[0], sums[1]) if z2 == 0 else (sums[1], sums[0])
                        sums = [jnp.where(first, own, swapped)]
                    out_ref[4 * z2 + 2 * z1 + m2] = sums[0].astype(BF16)


def k_sum_small(keep_ref, keep_t, got_t, *refs):
    *got, mine_ref, yours_ref = refs
    half = mine_ref.shape[0]
    width = keep_ref.shape[2]
    for s in range(2 * half):
        ref, at = (mine_ref, s) if s < half else (yours_ref, s - half)
        other, place = place_of(got, s)
        ref[at, :, :width] = add_blocks(False, keep_ref[s], other[place]).astype(BF16)
        ref[at, :, width:] = renew(add_blocks(False, keep_t[s], got_t[s])).astype(BF16)


def k_sum_four(keep_b, got_b, keep_a, got_a, own, one, two, three):
    width = keep_b.shape[2]
    for m, ref in enumerate((own, one, two, three)):
        ref[:, :width] = add_blocks(False, keep_b[m], got_b[m]).astype(ref.dtype)
        ref[:, width:] = add_blocks(True, keep_a[m], got_a[m]).astype(ref.dtype)


def k_final(n, *refs):
    parts, (qkv_ref, out_ref, b_ref, ga_ref, gm_ref) = refs[:n], refs[n:]
    rows = qkv_ref.shape[0]

    def total(start, width):
        value = parts[0][:, start : start + width]
        for part in parts[1:]:
            value = value + part[:, start : start + width].astype(F32)
        return value

    for part in range(3):
        for at, start in ((0, 3 * HALF + D), (HALF, 0)):
            qkv_ref[:, part * D + at : part * D + at + HALF] = total(start + part * HALF, HALF)
    out_ref[...] = total(3 * HALF, D)
    small = total(6 * HALF + D, 128)
    small = small + pltpu.roll(small, 120, 1)
    lane = lax.broadcasted_iota(jnp.int32, (rows, 128), 1)
    row = lax.broadcasted_iota(jnp.int32, (rows, 128), 0)

    def as_row(column, first):
        return jnp.sum(jnp.where(lane == row + first, small[:, column : column + 1], 0.0), axis=0, keepdims=True)

    ga_ref[...] = as_row(0, 0)[:, :rows]
    gm_ref[...] = as_row(1, 0)[:, :rows]
    b_ref[...] = sum(as_row(2 + k, k * rows) for k in range(4))[:, : 4 * rows]


def bits_of(count):
    return count.bit_length() - 1


SWAP = {"m1": "m2", "m2": "m1", "z1": "z2", "z2": "z1", "zl": "zl", "zh": "zh"}


class Plan:
    LATE = ("zl", "zh", "m1", "m2")
    EARLY = ("m1", "z1", "z2", "m2")
    SUM = ("z1", "z2", "m2", "m1")
    SUM_DOWN = ("m2", "z1", "z2", "m1")

    def __init__(self, mesh):
        self.wide, self.narrow = mesh.shape["wide"], mesh.shape["narrow"]
        self.count = self.wide * self.narrow
        self.low = bits_of(self.narrow)
        self.bits = bits_of(self.count)
        self.core = self.low
        outer = list(range(self.low + 1, self.bits))
        self.ys = list(range(self.low))
        self.x_bit, self.z_bits = outer[0], outer[1:]
        self.cm, self.xm, self.ym = 1 << self.core, 1 << self.x_bit, 1
        self.zl, self.zh = (1 << b for b in self.z_bits[:2])
        self.fine = (D // self.count) % 8 == 0 and self.low == 1 and len(self.z_bits) == 2
        self.pieces = 4 if self.fine else 1

    def index(self):
        return lax.axis_index("wide") * self.narrow + lax.axis_index("narrow")

    def send(self, value, mask, other=None):
        masks = [mask, mask if other is None else other]
        return lax.ppermute(value, AXES, [(i, i ^ masks[(i >> self.core) & 1]) for i in range(self.count)])

    def both(self, name):
        low = {"m1": self.xm, "m2": self.ym, "z1": self.zl, "z2": self.zh, "zl": self.zl, "zh": self.zh}
        return low[name], low[SWAP[name]]

    def exchange(self, name):
        return lambda value: self.send(value, *self.both(name))

    def mask(self, me, name):
        first, second = self.both(name)
        return first if first == second else jnp.where(((me >> self.core) & 1) == 0, first, second)

    def starts(self, me, bits, total):
        if not self.fine:
            return [0]
        masks = []
        for names, extra in ((bits, 0), ([SWAP[b] for b in bits], self.cm)):
            ways = [self.mask(me, name) for name in names]
            for block in range(1 << len(bits)):
                whole = extra
                for k, way in enumerate(ways):
                    if (block >> k) & 1:
                        whole = whole | way
                masks.append(whole)
        return [(me ^ m) * (total // self.count) for m in masks]

    def half(self, me, part):
        return ((me >> self.z_bits[1]) & 1) ^ part if self.fine else part

    def down_place(self, me, device):
        diff = (me ^ device) & (self.count // 2 - 1)
        other = (diff & self.cm) != 0
        at = jnp.where(other, 0, 8)
        at = at + jnp.where((diff & self.zl) != 0, 4, 0)
        for name, step in (("m1", 2), ("m2", 1)):
            way = jnp.where(other, self.mask(me, SWAP[name]), self.mask(me, name))
            at = at + jnp.where((diff & way) != 0, step, 0)
        return at

    def pair_up(self, own, other, bit, axis):
        mine = (self.index() >> bit) & 1
        return jnp.where(mine == 1, jnp.stack([other, own], axis), jnp.stack([own, other], axis))

    def gather_plain(self, shard):
        value, held = shard, []
        for b in self.z_bits + [self.x_bit] + self.ys + [self.core]:
            axis = sum(1 for h in held if h > b)
            value = self.pair_up(value, self.send(value, 1 << b), b, axis)
            held.append(b)
        return value.reshape(1, -1, shard.shape[1])

    def scatter_plain(self, keep, send, add):
        me = self.index()
        blocks = jnp.concatenate([keep[0], send[0]], 0)
        value = blocks.reshape((2,) * self.bits + (-1, blocks.shape[1]))
        held = list(range(self.bits - 1, -1, -1))
        for b in [self.core] + self.ys + [self.x_bit] + self.z_bits:
            axis, bit = held.index(b), (me >> b) & 1
            mine = lax.dynamic_index_in_dim(value, bit, axis, keepdims=False)
            yours = lax.dynamic_index_in_dim(value, 1 - bit, axis, keepdims=False)
            held.remove(b)
            value = add([mine, self.send(yours, 1 << b)], not held)
        return value


class Gather:
    def __init__(self, plan):
        self.plan, self.fine = plan, plan.fine

    def begin(self, blocks, name):
        if self.fine:
            self.a = blocks if blocks.ndim == 3 else blocks.reshape((1,) + blocks.shape)
            self.got = self.plan.exchange(name)(self.a)
        else:
            self.got = self.plan.gather_plain(blocks) if blocks.ndim == 2 else blocks

    def grow(self, name, waits=()):
        if self.fine:
            count, rows, columns = self.a.shape
            (self.a,) = call(k_join, [((2 * count, rows, columns), BF16)], self.a, self.got, waits=waits)
            self.got = self.plan.exchange(name)(self.a)

    def to_core(self, *after):
        self.near = [self.plan.send(fence(self.a, *after)[0] if after else self.a, self.plan.cm)] if self.fine else []

    def finish(self, *after):
        if self.fine:
            far = fence(self.got, *after)[0] if after else self.got
            return [self.a, self.got, *self.near, self.plan.send(far, self.plan.cm)]
        return [self.got]


def stack(plan, shard, got, widths, waits):
    if not plan.fine:
        cuts = [sum(widths[:i]) for i in range(len(widths) + 1)]
        return [got[:, :, i:j] for i, j in zip(cuts, cuts[1:])]
    return call(functools.partial(k_stack, 4), [((4, shard.shape[0], w), BF16) for w in widths], shard, *got, waits=waits)


class Scatter:
    def __init__(self, plan, keep, *sends):
        self.plan, self.fine, self.keep = plan, plan.fine, keep
        self.small = False
        if plan.fine:
            self.got = [plan.send(part, plan.cm) for part in sends]
        else:
            self.got = [plan.scatter_plain(keep, sends[0], add_plain)]

    def add_small(self, keep, send):
        if self.fine:
            self.small_parts = [keep, self.plan.send(send, self.plan.cm)]
        else:
            self.got.append(self.plan.scatter_plain(keep, send, add_two))

    def halve(self, name, waits=(), me=None):
        if not self.fine:
            return
        count, rows, columns = (self.keep[0] if isinstance(self.keep, list) else self.keep).shape
        if isinstance(self.keep, list):
            self.keep, yours = call(
                functools.partial(k_sum_down, self.plan), [((8, rows, columns), BF16)] * 2,
                me, *self.keep, *self.got, smem=1, waits=waits,
            )
            self.got = [self.plan.exchange(name)(yours)]
            return
        if not self.small and hasattr(self, "small_parts"):
            self.small = True
            body, columns = k_sum_small, columns + 128
            args = [self.keep, *self.small_parts, *self.got]
        else:
            body = functools.partial(k_sum_half, self.small)
            args = [self.keep, *self.got]
        self.keep, yours = call(body, [((count // 2, rows, columns), BF16)] * 2, *args, waits=waits)
        self.got = [self.plan.exchange(name)(yours)]

    def total(self):
        if not self.fine:
            return self.got[0]
        return self.keep[0].astype(F32) + self.got[0][0].astype(F32)


def finish_late(plan, sb, sa):
    if not plan.fine:
        small = sa.got[1]
        rest = jnp.zeros((small.shape[0], 120), F32)
        return [jnp.concatenate([sb.got[0], sa.got[0], small, rest], axis=1)]
    rows, width = sb.keep.shape[1:]
    whole = width + sa.keep.shape[2]
    own, *others = call(
        k_sum_four, [((rows, whole), F32)] + [((rows, whole), BF16)] * 3, sb.keep, sb.got[0], sa.keep, sa.got[0]
    )
    return [own, plan.exchange("z1")(others[0]), plan.exchange("z2")(others[1]), plan.send(others[2], plan.zl | plan.zh)]


def add_plain(arrived, last):
    total = arrived[0].astype(F32)
    for part in arrived[1:]:
        total = total + part.astype(F32)
    return total if last else total.astype(BF16)


def add_two(arrived, last):
    total = 0.0
    for part in arrived:
        whole = part.astype(F32)
        total = total + (whole[..., :8] + whole[..., 8:16])
    if last:
        return total
    high = lax.reduce_precision(total, 8, 7)
    rest = jnp.zeros(total.shape[:-1] + (112,), F32)
    return jnp.concatenate([high, total - high, rest], axis=-1).astype(BF16)


def fence(*values):
    return lax.optimization_barrier(values)


def device_step(plan, resid_in, w_qkv, w_out, w_up, b_up, w_down, gain_attn, gain_mlp, cotangent):
    rows = w_qkv.shape[0]
    t, d, half = resid_in.shape[0], D, D // 2
    wide3 = 3 * HALF
    CHAIN.clear()
    KEEP.clear()
    first = wide3 + 128
    fine = plan.fine
    me = plan.index().reshape(1)
    bind = lambda body: functools.partial(body, plan)
    turned = [pltpu.VMEM((d, t), F32)] * 2

    def blocks(r, columns, *pieces):
        if not fine:
            return [((1, half * r // rows, columns), BF16)] * 2
        return [((count, r, columns), BF16) for count in (16, *(pieces or (16,)))]

    a, b, u, v = (Gather(plan) for _ in range(4))
    u.begin(w_up, "m1")
    v.begin(w_down, "m1")
    (shard,) = call(
        k_pack, [((rows, first + wide3 + d), BF16)],
        w_qkv, w_out, jnp.concatenate([gain_attn, gain_mlp, b_up]).reshape(1, 6 * rows), free=True,
        scratch=[pltpu.VMEM(shape, BF16) for shape in ((rows, 3 * d), (rows, d), (1, 6 * rows))]
        + [pltpu.SemaphoreType.DMA((3,))],
    )
    got = [plan.send(shard, m) for m in (plan.zl, plan.zh, plan.zl | plan.zh)] if fine else plan.gather_plain(shard)
    resid, cot, dz = call(k_prep, [((t, d), BF16)] * 3, resid_in, cotangent, waits=[me])
    four_a, four_b = stack(plan, shard, got, (first, wide3 + d), [u.got, v.got])
    KEEP.append(resid)
    a.begin(four_a, "m1")
    b.begin(four_b, "m1")
    u.grow("z1")
    v.grow("z1")
    a.grow("m2", [b.got, u.got, v.got])
    KEEP.extend([a.a] if fine else [])
    b.grow("m2")
    KEEP.extend([b.a] if fine else [])
    u.grow("z2")
    a.to_core()
    b.to_core()
    u.grow("m2", [a.got, b.got, *a.near, *b.near])
    u.to_core()
    KEEP.extend([*a.near, *b.near])
    v.grow("z2")
    a_pieces, b_pieces = a.finish(), b.finish()
    qkv0, w0, h1, gains = call(
        bind(k_qkv),
        [((t, wide3), BF16), ((d, wide3), BF16), ((t, d), BF16), ((8, d), F32)],
        me, resid, *a_pieces,
        scratch=[pltpu.VMEM((d, 128), BF16), pltpu.VMEM((d, half), F32)], smem=1, waits=b_pieces[-1:],
    )
    KEEP[:] = [resid, b.a, *b.near] if fine else [resid]
    (attn0,) = call(k_attn, [((t, HALF), BF16)], qkv0)
    qkv1, w1, wo, attn, x2, h2 = call(
        bind(k_second),
        [((t, wide3), BF16), ((d, wide3), BF16), ((d, d), BF16), ((t, d), BF16), ((t, d), F32), ((t, d), BF16)],
        me, resid, h1, attn0, gains, *b_pieces,
        scratch=[pltpu.VMEM((d, half), F32)], smem=1,
    )
    KEEP.clear()
    bias, spread, pick = call(
        functools.partial(k_bias, rows), [((1, FF), F32), ((half, 4 * half), BF16), ((8, 4 * half), F32)], gains
    )
    v.grow("m2", [u.got, *u.near])
    v.to_core(CHAIN[-1])
    u_pieces = u.finish(h2)
    ups = []
    for part in range(2):
        grads = [((4, 4 * rows, d), BF16)] * 4 if fine else [((1, FF // 2, d), BF16)]
        ups.append(call(
            functools.partial(k_up, plan, part),
            [((d, FF // 2), BF16), ((t, FF // 2), BF16), ((t, FF // 2), F32)] + grads,
            me, h2, bias, dz, *u_pieces,
            scratch=[pltpu.VMEM((2, t // 2, d), F32), pltpu.VMEM((d, half), F32), pltpu.VMEM((FF // 2, t), BF16)],
            smem=1, waits=v.near if part else (),
        ))
    wu, act, slope = ([up[i] for up in ups] for i in range(3))
    if fine:
        sv = Scatter(plan, [part for up in ups for part in up[5:7]], *[part for up in ups for part in up[3:5]])
    else:
        sv = Scatter(plan, ups[0][3], ups[1][3])
    h1t, attnt, h2t = call(bind(k_turn), [((d, t), BF16)] * 3, me, h1, attn, h2, scratch=turned, smem=1)
    sv.halve("m1", me=me)
    du, gb, w_down_all = call(
        bind(k_du),
        [((t, FF), BF16), ((1, FF), F32), ((FF, d), BF16)],
        me, dz, *slope, *v.finish(*([sv.keep] if fine else [])), scratch=[pltpu.VMEM((2, t, d), F32)], smem=1,
    )
    su = Scatter(plan, *call(split_dot, blocks(rows, FF, 4, 4, 4, 4), h2t, du))
    dmid, dy, gg, keep_o, send_o = call(
        bind(k_mid),
        [((t, d), F32), ((t, d), BF16), ((1, d), F32)] + blocks(rows, d),
        me, cot, x2, gains, du, *wu, attnt,
        scratch=[pltpu.VMEM((t, d), F32)], smem=1,
    )
    su.halve("m1")
    sv.halve("z2")
    back_scratch = [pltpu.VMEM((t, HALF), BF16)]
    dqkv1, *parts = call(
        functools.partial(k_attn_back, 1), [((t, wide3), BF16)] + blocks(rows, wide3 + d, 6, 5, 5),
        dy, wo, qkv1, h1t, keep_o, send_o, scratch=back_scratch,
    )
    sb = Scatter(plan, *parts)
    dqkv0, *parts = call(
        functools.partial(k_attn_back, 0), [((t, wide3), BF16)] + blocks(rows, wide3, 8, 8),
        dy, wo, qkv0, h1t, scratch=back_scratch,
    )
    sa = Scatter(plan, *parts)
    sb.halve("m1")
    su.halve("m2")
    dres, *parts = call(
        bind(k_last),
        [((t, d - 1), F32)] + blocks(rows, 128),
        me, resid, dmid, gains, dqkv0, w0, dqkv1, w1, gg, gb, spread, pick,
        scratch=[pltpu.VMEM((t, d), F32), pltpu.VMEM((d, 128), F32)], smem=1,
    )
    sa.add_small(*parts)
    sv.halve("z1")
    sa.halve("m1")
    (out,) = call(
        bind(k_result), [((t, d - 1), BF16)], me, x2, *act, w_down_all,
        scratch=[pltpu.VMEM((t, d), F32), pltpu.VMEM((t, d - 1), BF16), pltpu.SemaphoreType.DMA], smem=1, far=True,
    )
    su.halve("z2")
    sb.halve("m2")
    sa.halve("m2")
    sv.halve("m2")
    su.halve("z1")
    late = finish_late(plan, sb, sa)
    s_down, s_up = sv.total(), su.total()
    s_qkv, s_out, s_b, s_a, s_m = call(
        functools.partial(k_final, len(late)),
        [((rows, 3 * d), F32), ((rows, d), F32), ((1, 4 * rows), F32), ((1, rows), F32), ((1, rows), F32)],
        *late,
    )
    return (out, dres, s_qkv, s_out, s_up, s_b.reshape(4 * rows), s_down, s_a.reshape(rows), s_m.reshape(rows))


def solution(mesh):
    rows2, rows1 = P(AXES, None), P(AXES)
    in_specs = (rows2, rows2, rows2, rows2, rows1, rows2, rows1, rows1, rows2)
    out_specs = (rows2, rows2, rows2, rows2, rows2, rows1, rows2, rows1, rows1)
    plan = Plan(mesh)

    def on_device(*arrays):
        return device_step(plan, *arrays)

    return jax.shard_map(on_device, mesh=mesh, in_specs=in_specs, out_specs=out_specs, check_vma=False)
```
